128 devices in a mesh: pipe: 8 (over x, y_hi), dp: 16 (over y_lo, z, core).
Axes of the slice: x: 4, y: 4 (y_hi: 2, y_lo: 2; y = y_hi * 2 + y_lo), z: 4, core: 2. Of those that a mesh axis runs over, the one named last changes fastest.
Arguments:
- stored_section_input: bfloat16 [8, 2048, 1792], P('pipe', 'dp'), may hold values from -6 to 6
- common_block_weight: bfloat16 [1792, 2, 1792], P('dp'), may hold values from -0.125 to 0.125
- adapter_down_weight: bfloat16 [8, 2, 1792, 128], P('pipe'), may hold values from -0.125 to 0.125
- adapter_up_weight: bfloat16 [8, 2, 1792, 128], P('pipe'), may hold values from -0.5 to 0.5
- block_selection: int32 [8, 2], P('pipe'), may hold values from 0 to 1
- final_output_cotangent: bfloat16 [2048, 1792], P('dp'), may hold values from -6 to 6
Outputs:
- section_cotangent: bfloat16 [8, 2048, 1792], P('pipe', 'dp')
- shared_grad: float32 [1792, 2, 1792], P(('pipe', 'dp'))
- down_grad: float32 [8, 2, 1792, 128], P('pipe', None, 'dp')
- up_grad: float32 [8, 2, 1792, 128], P('pipe', None, 'dp')
The draws below stay inside these ranges and needn't reach their ends.
All inputs are finite; a program needn't handle non-finite values.
Results may differ from the reference program's by a relative error of at most 0.035.
Values may be sent and summed in bfloat16 or wider, within the bound.
No kernel may reach another device: no remote copies, remote signals or barrier semaphores. Data moves between devices by JAX's collectives and lax.ppermute only.
A program may use at most 128 MiB of HBM per device.

```python
import jax
import jax.numpy as jnp
from jax import lax

MODEL_FEATURES = 1792
ADAPTER_RANK = 128
TOK_DEV = 128
TOKENS = 2048
N_PIPE = 8
N_DP = 16


def set_ends(array, rng, least, top_value):
    dims = array.shape
    spot = [jax.random.randint(jax.random.fold_in(rng, axis), (), 0, dims[axis]) for axis in range(len(dims))]
    array = array.at[tuple(spot)].set(least)
    longest = dims.index(max(dims))
    spot[longest] = (spot[longest] + 1) % dims[longest]
    return array.at[tuple(spot)].set(top_value)


def raised(drawn, rng, source, target, blocks, factor):
    def block_of(position):
        return (jnp.arange(drawn.shape[position]) // (drawn.shape[position] // blocks)).reshape((-1,) + (1,) * (drawn.ndim - 1 - position))

    one_side = jax.random.permutation(rng, blocks)[block_of(target)]
    other_side = (block_of(target) + blocks // 2) % blocks
    return jnp.where((block_of(source) == one_side) | (block_of(source) == other_side), factor * drawn, drawn)


def levels(rng, dims, cuts, smallest, high):
    loudness, own = 1.0, jax.random.fold_in(rng, 6)
    for axis_at, blocks in cuts:
        steps = jnp.exp(jax.random.uniform(jax.random.fold_in(own, axis_at), (blocks,), jnp.float32, smallest / len(cuts), high / len(cuts)))
        loudness = loudness * jnp.repeat(steps, dims[axis_at] // blocks).reshape([-1 if axis == axis_at else 1 for axis in range(len(dims))])
    return loudness


def centred(stream_key, shape, scale, reach, split=(), kind=jnp.bfloat16):
    entries = scale * jax.random.normal(stream_key, shape, jnp.float32)
    if split:
        entries = entries * levels(stream_key, shape, split, -0.22, 0.18)
    return jnp.clip(entries, -reach, reach).astype(kind)


def gaussian_with(rng, extent, width, bound, split, heavy, kind=jnp.bfloat16):
    drawn = width * jax.random.normal(rng, extent, jnp.float32)
    if split:
        drawn = drawn * levels(rng, extent, split, -0.22, 0.18)
    return jnp.clip(raised(drawn, jax.random.fold_in(rng, 3), *heavy), -bound, bound).astype(kind)


def setup_inputs(seed: int = 0) -> dict:
    key_list = jax.random.split(jax.random.key(seed), 7)
    stored_section_input = gaussian_with(key_list[0], (N_PIPE, TOKENS, MODEL_FEATURES), 1.0, 6.0, ((0, 8), (1, 16)), (0, 2, 8, 2.0))
    common_block_weight = centred(key_list[1], (MODEL_FEATURES, 2, MODEL_FEATURES), MODEL_FEATURES ** -0.5, 0.125, ((0, 16),))
    adapter_down_weight = centred(key_list[2], (N_PIPE, 2, MODEL_FEATURES, ADAPTER_RANK), MODEL_FEATURES ** -0.5, 0.125, ((0, 8),))
    adapter_up_weight = centred(key_list[3], (N_PIPE, 2, MODEL_FEATURES, ADAPTER_RANK), ADAPTER_RANK ** -0.5, 0.5, ((0, 8),))
    block_selection = set_ends(jax.random.randint(key_list[4], (N_PIPE, 2), 0, 2), jax.random.fold_in(key_list[4], 1), 0, 1).astype(jnp.int32)
    final_output_cotangent = centred(key_list[5], (TOKENS, MODEL_FEATURES), 1.0, 6.0, ((0, 16),))
    return {"stored_section_input": stored_section_input, "common_block_weight": common_block_weight, "adapter_down_weight": adapter_down_weight, "adapter_up_weight": adapter_up_weight, "block_selection": block_selection, "final_output_cotangent": final_output_cotangent}


EPS = 1e-06

def prepare_section(rows_in, weight, down, up):
    as_float = rows_in.astype(jnp.float32)
    scale = lax.rsqrt(lax.optimization_barrier(jnp.mean(as_float * as_float, axis=-1, keepdims=True)) + EPS)
    normed = (as_float * scale).astype(jnp.bfloat16)
    lowrank = jnp.dot(normed, down, preferred_element_type=jnp.float32).astype(jnp.bfloat16)
    before = jnp.dot(normed, weight, preferred_element_type=jnp.float32) + lax.dot_general(lowrank, up, (((1,), (1,)), ((), ())), preferred_element_type=jnp.float32)
    return (as_float, scale, normed, lowrank, before)

def forward_move(pieces):
    as_float, scale, normed, lowrank, before = pieces
    return (as_float + jax.nn.silu(before)).astype(jnp.bfloat16)

def backward_move(pieces, incoming, weight, down, up):
    as_float, scale, normed, lowrank, before = pieces
    sigma = jax.nn.sigmoid(before)
    slope = sigma * (1.0 + before * (1.0 - sigma))
    carried_gradient = incoming.astype(jnp.float32)
    grad_pre = (carried_gradient * slope).astype(jnp.bfloat16)
    grad_low = jnp.dot(grad_pre, up, preferred_element_type=jnp.float32).astype(jnp.bfloat16)
    grad_norm = lax.dot_general(grad_pre, weight, (((1,), (1,)), ((), ())), preferred_element_type=jnp.float32)
    grad_norm = grad_norm + lax.dot_general(grad_low, down, (((1,), (1,)), ((), ())), preferred_element_type=jnp.float32)
    unit = as_float * scale
    grad_in = scale * (grad_norm - unit * lax.optimization_barrier(jnp.mean(grad_norm * unit, axis=-1, keepdims=True)))
    return ((carried_gradient + grad_in).astype(jnp.bfloat16), grad_pre, grad_low)

def reference(stored_section_input, common_block_weight, adapter_down_weight, adapter_up_weight, block_selection, final_output_cotangent):
    carried_gradient = final_output_cotangent
    section_rows = []
    down_rows = []
    up_rows = []
    piped = jnp.zeros((N_DP, MODEL_FEATURES, 2, MODEL_FEATURES), jnp.float32)
    contract = (((0,), (0,)), ((), ()))
    for section_index in range(N_PIPE - 1, -1, -1):
        first_invocation = lax.dynamic_index_in_dim(common_block_weight, block_selection[section_index, 0], 1, keepdims=False)
        second_invocation = lax.dynamic_index_in_dim(common_block_weight, block_selection[section_index, 1], 1, keepdims=False)
        first_weight_shards = prepare_section(stored_section_input[section_index], first_invocation, adapter_down_weight[section_index, 0], adapter_up_weight[section_index, 0])
        second_weight_shards = prepare_section(forward_move(first_weight_shards), second_invocation, adapter_down_weight[section_index, 1], adapter_up_weight[section_index, 1])
        middle_activation, second_preact_gradient, second_lowrank_gradient = backward_move(second_weight_shards, carried_gradient, second_invocation, adapter_down_weight[section_index, 1], adapter_up_weight[section_index, 1])
        carried_gradient, first_preact_gradient, first_lowrank_gradient = backward_move(first_weight_shards, middle_activation, first_invocation, adapter_down_weight[section_index, 0], adapter_up_weight[section_index, 0])
        section_rows.append(carried_gradient)
        hot = (block_selection[section_index][:, None] == jnp.arange(2, dtype=jnp.int32)[None, :]).astype(jnp.float32)
        term = jnp.zeros((N_DP, MODEL_FEATURES, 2, MODEL_FEATURES), jnp.float32)
        for slot, normed, grad_pre in ((0, first_weight_shards[2], first_preact_gradient), (1, second_weight_shards[2], second_preact_gradient)):
            local = jnp.einsum('nrd,nre->nde', normed.astype(jnp.float32).reshape(N_DP, TOK_DEV, MODEL_FEATURES), grad_pre.astype(jnp.float32).reshape(N_DP, TOK_DEV, MODEL_FEATURES))
            term = term + local[:, :, None, :] * hot[slot][None, None, :, None]
        piped = piped + lax.optimization_barrier(term.astype(jnp.bfloat16)).astype(jnp.float32)
        down_rows.append(jnp.stack([lax.dot_general(first_weight_shards[2], first_lowrank_gradient, contract, preferred_element_type=jnp.float32), lax.dot_general(second_weight_shards[2], second_lowrank_gradient, contract, preferred_element_type=jnp.float32)]))
        up_rows.append(jnp.stack([lax.dot_general(first_preact_gradient, first_weight_shards[3], contract, preferred_element_type=jnp.float32), lax.dot_general(second_preact_gradient, second_weight_shards[3], contract, preferred_element_type=jnp.float32)]))
    rounded = lax.optimization_barrier(piped.astype(jnp.bfloat16)).astype(jnp.float32)
    shared_grad = lax.optimization_barrier(jnp.sum(rounded, axis=0))
    section_cotangent = jnp.stack(section_rows[::-1])
    down_grad = jnp.stack(down_rows[::-1])
    up_grad = jnp.stack(up_rows[::-1])
    return (section_cotangent, shared_grad, down_grad, up_grad)
```

```python
import functools

import jax
import jax.numpy as jnp
from jax import lax
from jax.experimental import pallas as pl
from jax.experimental.pallas import tpu as pltpu
from jax.sharding import PartitionSpec as P

EPS = 1e-06
TILE = 256
F32 = jnp.float32
BF16 = jnp.bfloat16
NT = (((1,), (1,)), ((), ()))
TN = (((0,), (0,)), ((), ()))
ANY = pl.BlockSpec(memory_space=pl.ANY)
VM = pl.BlockSpec(memory_space=pltpu.VMEM)
SM = pl.BlockSpec(memory_space=pltpu.SMEM)


def dot(a, b, dims=(((1,), (0,)), ((), ()))):
    return lax.dot_general(a, b, dims, preferred_element_type=F32)


def weight_copies(w0, w1, a0, a1, u0, u1, wv, av, uv, sems):
    pairs = ((w0, wv.at[0]), (w1, wv.at[1]), (a0, av.at[0]), (a1, av.at[1]), (u0, uv.at[0]), (u1, uv.at[1]))
    return [pltpu.make_async_copy(src, dst, sems.at[i]) for i, (src, dst) in enumerate(pairs)]


def forward_kernel(sel, x, w0, w1, a0, a1, u0, u1, normed, lowrank, slope, scale, wv, av, uv, xs, sems):
    width = x.shape[-1]
    copies = weight_copies(w0, w1, a0, a1, u0, u1, wv, av, uv, sems)
    for copy in copies[2:] + copies[:2]:
        copy.start()
    for o in range(2):
        xs[o] = x[o]
    waited = False
    for k in range(2):
        for o in range(2):
            rows = xs[o].astype(F32)
            sc = lax.rsqrt(jnp.mean(rows * rows, axis=-1, keepdims=True) + EPS)
            scale[o, k] = jnp.broadcast_to(sc, scale.shape[2:])
            nm = (rows * sc).astype(BF16)
            normed[o, k] = nm
            if not waited:
                for copy in copies[2:]:
                    copy.wait()
            low = dot(nm, av[o, k]).astype(BF16)
            lowrank[o, k] = low
            if not waited:
                for copy in copies[:2]:
                    copy.wait()
                waited = True
            block = sel[o, k]
            for t in range(width // TILE):
                cols = pl.ds(t * TILE, TILE)
                pre = dot(nm, wv[block, :, cols]) + dot(low, uv[o, k, cols, :], NT)
                sigma = 1.0 / (1.0 + jnp.exp(-pre))
                slope[o, k, :, cols] = sigma * (1.0 + pre * (1.0 - sigma))
                if k == 0:
                    xs[o, :, cols] = (xs[o, :, cols].astype(F32) + pre * sigma).astype(BF16)


def backward_kernel(sel, c, w0, w1, a0, a1, u0, u1, normed, slope, scale, gp, gl, ct, wv, av, uv, gn, sems):
    width = c.shape[-1]
    copies = weight_copies(w0, w1, a0, a1, u0, u1, wv, av, uv, sems)
    for copy in copies[4:] + copies[:4]:
        copy.start()
    h = sel[2, 0]
    waited = False
    cur = c[...]
    for j in (1, 0):
        o = jnp.bitwise_xor(h, j)
        for k in (1, 0):
            c32 = cur.astype(F32)
            g = (c32 * slope[o, k]).astype(BF16)
            gp[o, k] = g
            if not waited:
                for copy in copies[4:]:
                    copy.wait()
            low = dot(g, uv[o, k]).astype(BF16)
            gl[o, k] = low
            if not waited:
                for copy in copies[:4]:
                    copy.wait()
                waited = True
            block = sel[o, k]
            total = jnp.zeros((g.shape[0], 1), F32)
            for t in range(width // TILE):
                cols = pl.ds(t * TILE, TILE)
                part = dot(g, wv[block, cols, :], NT) + dot(low, av[o, k, cols, :], NT)
                gn[:, cols] = part
                total = total + jnp.sum(part * normed[o, k, :, cols].astype(F32), axis=-1, keepdims=True)
            mean = total / width
            z = normed[o, k].astype(F32)
            sc = scale[o, k, :, 0:1]
            cur = (c32 + sc * (gn[...] - z * mean)).astype(BF16)
        ct[o] = cur


def weight_scratch(width, rank):
    return [
        pltpu.VMEM((2, width, width), BF16),
        pltpu.VMEM((2, 2, width, rank), BF16),
        pltpu.VMEM((2, 2, width, rank), BF16),
    ]


def forward(sel, x, weights):
    rows, width = x.shape[1:]
    rank = weights[2].shape[-1]
    sd = jax.ShapeDtypeStruct
    return pl.pallas_call(
        forward_kernel,
        out_shape=(
            sd((2, 2, rows, width), BF16),
            sd((2, 2, rows, rank), BF16),
            sd((2, 2, rows, width), F32),
            sd((2, 2, rows, 128), F32),
        ),
        in_specs=[SM, VM] + [ANY] * 6,
        out_specs=(VM,) * 4,
        scratch_shapes=weight_scratch(width, rank)
        + [pltpu.VMEM((2, rows, width), BF16), pltpu.SemaphoreType.DMA((6,))],
        compiler_params=pltpu.CompilerParams(vmem_limit_bytes=40 << 20),
        name="forward",
    )(sel, x, *weights)


def backward(sel, c, weights, normed, slope, scale):
    rows, width = c.shape
    rank = weights[2].shape[-1]
    sd = jax.ShapeDtypeStruct
    return pl.pallas_call(
        backward_kernel,
        out_shape=(
            sd((2, 2, rows, width), BF16),
            sd((2, 2, rows, rank), BF16),
            sd((2, rows, width), BF16),
        ),
        in_specs=[SM, VM] + [ANY] * 6 + [VM] * 3,
        out_specs=(VM,) * 3,
        scratch_shapes=weight_scratch(width, rank)
        + [pltpu.VMEM((rows, width), F32), pltpu.SemaphoreType.DMA((6,))],
        compiler_params=pltpu.CompilerParams(vmem_limit_bytes=40 << 20),
        name="backward",
    )(sel, c, *weights, normed, slope, scale)


def shards(stored, common, down, up, selection, final_c):
    n_pipe, n_dp = lax.axis_size("pipe"), lax.axis_size("dp")
    p = lax.axis_index("pipe")
    x_at, h = p // 2, p % 2
    swap = [(i, i ^ 1) for i in range(n_pipe)]
    own = stored[0]
    rows, width = own.shape
    half = rows // 2
    a_own, u_own = down[0], up[0]

    block0, block1 = common[:, 0], common[:, 1]
    w0 = lax.all_gather(block0, "dp", axis=0, tiled=True)
    w1 = lax.all_gather(block1, "dp", axis=0, tiled=True)
    x_mine = lax.dynamic_slice_in_dim(own, h * half, half, 0)
    x_other = lax.dynamic_slice_in_dim(own, (1 - h) * half, half, 0)
    x_peer = lax.ppermute(x_other, "pipe", swap)
    sel_peer = lax.ppermute(selection, "pipe", swap)
    a_peer = lax.ppermute(a_own, "pipe", swap)
    u_peer = lax.ppermute(u_own, "pipe", swap)
    sel = jnp.concatenate([selection, sel_peer, jnp.full((1, 2), h, jnp.int32)])
    weights = (w0, w1, a_own, a_peer, u_own, u_peer)
    normed, lowrank, slope, scale = forward(sel, jnp.stack([x_mine, x_peer]), weights)
    normed_peer = lax.ppermute(normed[1], "pipe", swap)
    lowrank_peer = lax.ppermute(lowrank[1], "pipe", swap)

    c = lax.dynamic_slice_in_dim(final_c, h * half, half, 0)
    rank = a_own.shape[-1]
    bufs = (
        jnp.zeros((2, 2, half, width), BF16),
        jnp.zeros((2, 2, half, rank), BF16),
        jnp.zeros((2, half, width), BF16),
    )
    steps = n_pipe // 2
    for t in range(steps):
        place = steps - 1 - t
        bufs = lax.cond(
            x_at == place,
            lambda state: tuple(backward(sel, state[1], weights, normed, slope, scale)),
            lambda state: state[0],
            (bufs, c),
        )
        if place > 0:
            c = lax.ppermute(
                bufs[2][h], "pipe", [(2 * place + i, 2 * place - 2 + i) for i in range(2)]
            )
    gp, gl, ct = bufs
    gp_peer = lax.ppermute(gp[1], "pipe", swap)
    gl_peer = lax.ppermute(gl[1], "pipe", swap)
    ct_peer = lax.ppermute(ct[1], "pipe", swap)
    result = jnp.where(
        h == 0, jnp.concatenate([ct[0], ct_peer]), jnp.concatenate([ct_peer, ct[0]])
    )
    n_all = jnp.concatenate([normed[0], normed_peer], axis=1)
    l_all = jnp.concatenate([lowrank[0], lowrank_peer], axis=1)
    gp_all = jnp.concatenate([gp[0], gp_peer], axis=1)
    gl_all = jnp.concatenate([gl[0], gl_peer], axis=1)
    hot = (selection[0][:, None] == jnp.arange(2, dtype=jnp.int32)[None, :]).astype(F32)
    prods = [dot(n_all[k], gp_all[k], TN) for k in range(2)]
    term = jnp.stack(
        [(prods[0] * hot[0, b] + prods[1] * hot[1, b]).astype(BF16) for b in range(2)], axis=1
    )
    each = width // (n_pipe * n_dp)
    term = term.reshape(n_pipe, n_dp, each, 2, width).transpose(1, 0, 2, 3, 4)
    term = term.reshape(n_dp * n_pipe * each * 2, width)
    part = lax.psum_scatter(term, "dp", scatter_dimension=0, tiled=True)
    shared = lax.psum_scatter(part, "pipe", scatter_dimension=0, tiled=True)
    shared = shared.astype(F32).reshape(each, 2, width)
    d_terms = jnp.stack([dot(n_all[k], gl_all[k], TN) for k in range(2)])
    u_terms = jnp.stack([dot(gp_all[k], l_all[k], TN) for k in range(2)])
    both = jnp.stack([d_terms, u_terms]).astype(BF16)
    both = lax.psum_scatter(both, "dp", scatter_dimension=2, tiled=True).astype(F32)
    return result[None], shared, both[0][None], both[1][None]


def solution(mesh):
    return jax.shard_map(
        shards,
        mesh=mesh,
        in_specs=(
            P("pipe", "dp", None),
            P("dp", None, None),
            P("pipe", None, None, None),
            P("pipe", None, None, None),
            P("pipe", None),
            P("dp", None),
        ),
        out_specs=(
            P("pipe", "dp", None),
            P(("pipe", "dp"), None, None),
            P("pipe", None, "dp", None),
            P("pipe", None, "dp", None),
        ),
        check_vma=False,
    )
```

```python
import functools

import jax
import jax.numpy as jnp
from jax import lax
from jax.experimental import pallas as pl
from jax.experimental.pallas import tpu as pltpu
from jax.sharding import PartitionSpec as P

EPS = 1e-06
TILE = 256
F32 = jnp.float32
BF16 = jnp.bfloat16
NT = (((1,), (1,)), ((), ()))
TN = (((0,), (0,)), ((), ()))
ANY = pl.BlockSpec(memory_space=pl.ANY)
VM = pl.BlockSpec(memory_space=pltpu.VMEM)
SM = pl.BlockSpec(memory_space=pltpu.SMEM)


def dot(a, b, dims=(((1,), (0,)), ((), ()))):
    return lax.dot_general(a, b, dims, preferred_element_type=F32)


def weight_copies(gathered, a0, a1, u0, u1, wv, av, uv, sems):
    per = gathered.shape[2]
    big = []
    for block in range(2):
        for r in range(gathered.shape[0]):
            dst = wv.at[block, pl.ds(r * per, per), :]
            big.append(pltpu.make_async_copy(gathered.at[r, block], dst, sems.at[block]))
    pairs = ((a0, av.at[0]), (a1, av.at[1]), (u0, uv.at[0]), (u1, uv.at[1]))
    return big, [pltpu.make_async_copy(src, dst, sems.at[2 + i]) for i, (src, dst) in enumerate(pairs)]


def wait_blocks(wv, sems):
    for block in range(2):
        pltpu.make_async_copy(wv.at[block], wv.at[block], sems.at[block]).wait()


def forward_kernel(sel, x, gathered, a0, a1, u0, u1, normed, lowrank, slope, scale, wv, av, uv, xs, sems):
    width = x.shape[-1]
    big, small = weight_copies(gathered, a0, a1, u0, u1, wv, av, uv, sems)
    for copy in small + big:
        copy.start()
    for o in range(2):
        xs[o] = x[o]
    waited = False
    for k in range(2):
        for o in range(2):
            rows = xs[o].astype(F32)
            sc = lax.rsqrt(jnp.mean(rows * rows, axis=-1, keepdims=True) + EPS)
            scale[o, k] = jnp.broadcast_to(sc, scale.shape[2:])
            nm = (rows * sc).astype(BF16)
            normed[o, k] = nm
            if not waited:
                for copy in small:
                    copy.wait()
            low = dot(nm, av[o, k]).astype(BF16)
            lowrank[o, k] = low
            if not waited:
                wait_blocks(wv, sems)
                waited = True
            block = sel[o, k]
            for t in range(width // TILE):
                cols = pl.ds(t * TILE, TILE)
                pre = dot(nm, wv[block, :, cols]) + dot(low, uv[o, k, cols, :], NT)
                sigma = 1.0 / (1.0 + jnp.exp(-pre))
                slope[o, k, :, cols] = sigma * (1.0 + pre * (1.0 - sigma))
                if k == 0:
                    xs[o, :, cols] = (xs[o, :, cols].astype(F32) + pre * sigma).astype(BF16)


def backward_kernel(sel, c, gathered, a0, a1, u0, u1, normed, slope, scale, gp, gl, ct, wv, av, uv, gn, sems):
    width = c.shape[-1]
    big, small = weight_copies(gathered, a0, a1, u0, u1, wv, av, uv, sems)
    for copy in small[2:] + big + small[:2]:
        copy.start()
    h = sel[2, 0]
    waited = False
    cur = c[...]
    for j in (1, 0):
        o = jnp.bitwise_xor(h, j)
        for k in (1, 0):
            c32 = cur.astype(F32)
            g = (c32 * slope[o, k]).astype(BF16)
            gp[o, k] = g
            if not waited:
                for copy in small:
                    copy.wait()
            low = dot(g, uv[o, k]).astype(BF16)
            gl[o, k] = low
            if not waited:
                wait_blocks(wv, sems)
                waited = True
            block = sel[o, k]
            total = jnp.zeros((g.shape[0], 1), F32)
            for t in range(width // TILE):
                cols = pl.ds(t * TILE, TILE)
                part = dot(g, wv[block, cols, :], NT) + dot(low, av[o, k, cols, :], NT)
                gn[:, cols] = part
                total = total + jnp.sum(part * normed[o, k, :, cols].astype(F32), axis=-1, keepdims=True)
            mean = total / width
            z = normed[o, k].astype(F32)
            sc = scale[o, k, :, 0:1]
            cur = (c32 + sc * (gn[...] - z * mean)).astype(BF16)
        ct[o] = cur


def weight_scratch(width, rank):
    return [
        pltpu.VMEM((2, width, width), BF16),
        pltpu.VMEM((2, 2, width, rank), BF16),
        pltpu.VMEM((2, 2, width, rank), BF16),
    ]


def forward(sel, x, weights):
    rows, width = x.shape[1:]
    rank = weights[1].shape[-1]
    sd = jax.ShapeDtypeStruct
    return pl.pallas_call(
        forward_kernel,
        out_shape=(
            sd((2, 2, rows, width), BF16),
            sd((2, 2, rows, rank), BF16),
            sd((2, 2, rows, width), F32),
            sd((2, 2, rows, 128), F32),
        ),
        in_specs=[SM, VM] + [ANY] * 5,
        out_specs=(VM,) * 4,
        scratch_shapes=weight_scratch(width, rank)
        + [pltpu.VMEM((2, rows, width), BF16), pltpu.SemaphoreType.DMA((6,))],
        compiler_params=pltpu.CompilerParams(vmem_limit_bytes=40 << 20),
        name="forward",
    )(sel, x, *weights)


def backward(sel, c, weights, normed, slope, scale):
    rows, width = c.shape
    rank = weights[1].shape[-1]
    sd = jax.ShapeDtypeStruct
    return pl.pallas_call(
        backward_kernel,
        out_shape=(
            sd((2, 2, rows, width), BF16),
            sd((2, 2, rows, rank), BF16),
            sd((2, rows, width), BF16),
        ),
        in_specs=[SM, VM] + [ANY] * 5 + [VM] * 3,
        out_specs=(VM,) * 3,
        scratch_shapes=weight_scratch(width, rank)
        + [pltpu.VMEM((rows, width), F32), pltpu.SemaphoreType.DMA((6,))],
        compiler_params=pltpu.CompilerParams(vmem_limit_bytes=40 << 20),
        name="backward",
    )(sel, c, *weights, normed, slope, scale)


def transpose_kernel(sel, gp, out):
    quarter = gp.shape[-1] // 4
    for k in range(2):
        lanes = pl.ds(k * 128, 128)
        both = jnp.concatenate([gp[0, k], gp[1, k]], axis=0)
        for q in range(4):
            for t in range(0, quarter, 64):
                out[q, pl.ds(t, 64), lanes] = both[:, q * quarter + t : q * quarter + t + 64].T
        side = lax.broadcasted_iota(jnp.int32, (16, 128), 1) // 64
        mark = jnp.where(side == 0, sel[0, k], sel[1, k])
        for q in range(4):
            out[q, pl.ds(quarter, 16), lanes] = mark.astype(F32).astype(BF16)


def transposed(sel, gp):
    quarter = gp.shape[-1] // 4
    return pl.pallas_call(
        transpose_kernel,
        out_shape=jax.ShapeDtypeStruct((4, quarter + 16, 256), BF16),
        in_specs=[SM, VM],
        out_specs=VM,
        compiler_params=pltpu.CompilerParams(vmem_limit_bytes=16 << 20),
        name="transposed",
    )(sel, gp)


def gradient_kernel(*refs):
    pieces, firsts, seconds = refs[:8], refs[8:12], refs[12:16]
    out, left, right, sems = refs[16:]
    copies = []
    for s in range(4):
        for side in range(2):
            for k, src in enumerate((firsts[s], seconds[s])):
                lanes = pl.ds(((s * 2 + side) * 2 + k) * 128, 128)
                copies.append(pltpu.make_async_copy(src.at[side], left.at[:, lanes], sems.at[len(copies)]))
    for copy in copies:
        copy.start()
    quarter = pieces[0].shape[0] - 16
    for i, piece in enumerate(pieces):
        lanes = pl.ds(i * 256, 256)
        whole = piece[pl.ds(0, quarter), :].astype(F32)
        second = whole * piece[pl.ds(quarter, 16), :][0:1].astype(F32)
        right[pl.ds(0, quarter), lanes] = (whole - second).astype(BF16)
        right[pl.ds(quarter, quarter), lanes] = second.astype(BF16)
    for copy in copies:
        copy.wait()
    for m in range(out.shape[0] // TILE):
        rows = pl.ds(m * TILE, TILE)
        out[rows, :] = dot(left[rows, :], right[...], NT).astype(BF16)


def gradient(pieces, firsts, seconds):
    rows = firsts[0].shape[1]
    cols = 2 * (pieces[0].shape[0] - 16)
    return pl.pallas_call(
        gradient_kernel,
        out_shape=jax.ShapeDtypeStruct((rows, cols), BF16),
        in_specs=[VM] * 8 + [ANY] * 8,
        out_specs=VM,
        scratch_shapes=[
            pltpu.VMEM((rows, 2048), BF16),
            pltpu.VMEM((cols, 2048), BF16),
            pltpu.SemaphoreType.DMA((16,)),
        ],
        compiler_params=pltpu.CompilerParams(vmem_limit_bytes=40 << 20),
        name="gradient",
    )(*pieces, *firsts, *seconds)


def at(array, index):
    return lax.dynamic_index_in_dim(array, index, 0, keepdims=False)


def feature_rows(normed):
    tokens = normed.shape[0]
    v = normed.reshape(tokens, 4, 2, 2, 4, 2, 14).transpose(2, 5, 4, 3, 1, 6, 0)
    v = jnp.pad(v, [(0, 0)] * 5 + [(0, 2), (0, 0)])
    return v.reshape(2, -1, tokens)


def sum_dp(buf):
    r = lax.axis_index("dp")
    core, z, y = r % 2, (r // 2) % 4, r // 8
    got = lax.ppermute(at(buf, 1 - core), "dp", [(i, i ^ 1) for i in range(16)])
    buf = (at(buf, core).astype(F32) + got.astype(F32)).astype(BF16)
    total = at(buf, z).astype(F32)
    for d in range(1, 4):
        pairs = [(i, i // 8 * 8 + (i + 2 * d) % 8) for i in range(16)]
        total = total + lax.ppermute(at(buf, (z + d) % 4), "dp", pairs).astype(F32)
    buf = total.astype(BF16)
    got = lax.ppermute(at(buf, 1 - y), "dp", [(i, i ^ 8) for i in range(16)])
    return at(buf, y).astype(F32) + got.astype(F32)


def shards(stored, common, down, up, selection, final_c):
    n_pipe, n_dp = lax.axis_size("pipe"), lax.axis_size("dp")
    p = lax.axis_index("pipe")
    x_at, h = p // 2, p % 2
    swap = [(i, i ^ 1) for i in range(n_pipe)]
    turns = [[(i, (i + 2 * d) % n_pipe) for i in range(n_pipe)] for d in range(4)]
    own = stored[0]
    rows, width = own.shape
    half = rows // 2
    a_own, u_own = down[0], up[0]

    def spread(normed):
        parts = feature_rows(normed)
        pair = jnp.stack([at(parts, h), lax.ppermute(at(parts, 1 - h), "pipe", swap)])
        return [pair] + [lax.ppermute(pair, "pipe", turns[d]) for d in range(1, 4)]

    mixed = common.transpose(1, 0, 2).reshape(-1, width)
    gathered = lax.all_gather(mixed, "dp", axis=0, tiled=True).reshape(n_dp, 2, -1, width)
    x_mine = lax.dynamic_slice_in_dim(own, h * half, half, 0)
    x_other = lax.dynamic_slice_in_dim(own, (1 - h) * half, half, 0)
    x_peer = lax.ppermute(x_other, "pipe", swap)
    sel_peer = lax.ppermute(selection, "pipe", swap)
    a_peer = lax.ppermute(a_own, "pipe", swap)
    u_peer = lax.ppermute(u_own, "pipe", swap)
    sel = jnp.concatenate([selection, sel_peer, jnp.full((1, 2), h, jnp.int32)])
    weights = (gathered, a_own, a_peer, u_own, u_peer)
    entered = jnp.stack([x_mine, x_peer])
    as_float = entered.reshape(rows, width).astype(F32)
    first = as_float * lax.rsqrt(jnp.mean(as_float * as_float, axis=-1, keepdims=True) + EPS)
    firsts = spread(first.astype(BF16))
    normed, lowrank, slope, scale = forward(sel, entered, weights)

    c = lax.dynamic_slice_in_dim(final_c, h * half, half, 0)
    rank = a_own.shape[-1]
    bufs = (
        jnp.zeros((2, 2, half, width), BF16),
        jnp.zeros((2, 2, half, rank), BF16),
        jnp.zeros((2, half, width), BF16),
    )
    steps = n_pipe // 2
    for t in range(steps):
        place = steps - 1 - t
        bufs = lax.cond(
            x_at == place,
            lambda state: tuple(backward(sel, state[1], weights, normed, slope, scale)),
            lambda state: state[0],
            (bufs, c),
        )
        if place > 0:
            c = lax.ppermute(
                bufs[2][h], "pipe", [(2 * place + i, 2 * place - 2 + i) for i in range(2)]
            )
    gp, gl, ct = bufs
    seconds = spread(normed[:, 1].reshape(rows, width))
    normed_peer = lax.ppermute(normed[1], "pipe", swap)
    lowrank_peer = lax.ppermute(lowrank[1], "pipe", swap)

    quarters = transposed(sel, gp)
    pieces = [at(quarters, x_at)]
    pieces += [lax.ppermute(at(quarters, (x_at + d) % 4), "pipe", turns[d]) for d in range(1, 4)]
    pieces = [q for piece in pieces for q in (piece, lax.ppermute(piece, "pipe", swap))]
    tile = gradient(pieces, firsts, seconds)
    tile = sum_dp(tile.reshape(2, 4, 2, 4, 16, tile.shape[-1])).astype(BF16)
    placed = jnp.stack(
        [at(tile, x_at)]
        + [lax.ppermute(at(tile, (x_at + d) % 4), "pipe", turns[d]) for d in range(1, 4)]
    )
    placed = jnp.stack([at(placed, (x_at - s) % 4) for s in range(4)], axis=1)
    each = width // (n_pipe * n_dp)
    shared = placed[:each].reshape(each, 4, 2, width // 4).transpose(0, 2, 1, 3)
    shared = shared.reshape(each, 2, width).astype(F32)

    gp_peer = lax.ppermute(gp[1], "pipe", swap)
    gl_peer = lax.ppermute(gl[1], "pipe", swap)
    ct_peer = lax.ppermute(ct[1], "pipe", swap)
    result = jnp.where(
        h == 0, jnp.concatenate([ct[0], ct_peer]), jnp.concatenate([ct_peer, ct[0]])
    )
    n_all = jnp.concatenate([normed[0], normed_peer], axis=1)
    l_all = jnp.concatenate([lowrank[0], lowrank_peer], axis=1)
    gp_all = jnp.concatenate([gp[0], gp_peer], axis=1)
    gl_all = jnp.concatenate([gl[0], gl_peer], axis=1)
    both = [dot(n_all[k], gl_all[k], TN) for k in range(2)]
    both += [dot(gp_all[k], l_all[k], TN) for k in range(2)]
    both = jnp.stack(both).astype(BF16).reshape(4, 2, 4, 2, -1, rank).transpose(3, 2, 1, 0, 4, 5)
    both = sum_dp(both)
    return result[None], shared, both[None, :2], both[None, 2:]


def solution(mesh):
    return jax.shard_map(
        shards,
        mesh=mesh,
        in_specs=(
            P("pipe", "dp", None),
            P("dp", None, None),
            P("pipe", None, None, None),
            P("pipe", None, None, None),
            P("pipe", None),
            P("dp", None),
        ),
        out_specs=(
            P("pipe", "dp", None),
            P(("pipe", "dp"), None, None),
            P("pipe", None, "dp", None),
            P("pipe", None, "dp", None),
        ),
        check_vma=False,
    )
```

```python
import functools

import jax
import jax.numpy as jnp
from jax import lax
from jax.experimental import pallas as pl
from jax.experimental.pallas import tpu as pltpu
from jax.sharding import PartitionSpec as P

EPS = 1e-06
TILE = 256
F32 = jnp.float32
BF16 = jnp.bfloat16
NT = (((1,), (1,)), ((), ()))
TN = (((0,), (0,)), ((), ()))
ANY = pl.BlockSpec(memory_space=pl.ANY)
VM = pl.BlockSpec(memory_space=pltpu.VMEM)
SM = pl.BlockSpec(memory_space=pltpu.SMEM)


def dot(a, b, dims=(((1,), (0,)), ((), ()))):
    return lax.dot_general(a, b, dims, preferred_element_type=F32)


def row_blocks(src, tile, dst, h, lanes):
    width = src.shape[1]
    for t in range(width // TILE):
        tile[pl.ds(t * TILE, TILE), :] = src[:, t * TILE : (t + 1) * TILE].astype(F32).T
    tile[pl.ds(width, 8), :] = jnp.zeros((8, tile.shape[1]), F32)
    for p in range(8):
        x, half = p // 2, p % 2
        slot = jnp.bitwise_xor(h, half)
        for r in range(16):
            core, z, y = r % 2, (r // 2) % 4, r // 8
            at_row = (((core * 4 + z) * 2 + y) * 4 + x) * 16
            dst[slot, pl.ds(at_row, 16), lanes] = tile[pl.ds((p * 16 + r) * 14, 16), :].astype(BF16)


def first_kernel(sel, x, out, tile):
    rows = jnp.concatenate([x[0], x[1]], axis=0).astype(F32)
    sc = lax.rsqrt(jnp.mean(rows * rows, axis=-1, keepdims=True) + EPS)
    row_blocks((rows * sc).astype(BF16), tile, out, sel[2, 0], pl.ds(0, 128))


def first_rows(sel, x):
    width = x.shape[-1]
    return pl.pallas_call(
        first_kernel,
        out_shape=jax.ShapeDtypeStruct((2, 1024, 128), BF16),
        in_specs=[SM, VM],
        out_specs=VM,
        scratch_shapes=[pltpu.VMEM((width + 8, 128), F32)],
        compiler_params=pltpu.CompilerParams(vmem_limit_bytes=16 << 20),
        name="first_rows",
    )(sel, x)


def forward_kernel(sel, x, gathered, a0, a1, u0, u1, nl, slope, scale, wt, av, uv, out, wv, xs, tile, sems):
    width = x.shape[-1]
    per = gathered.shape[2]
    h = sel[2, 0]
    small = []
    for i, (src, dst) in enumerate(((a0, av.at[0]), (a1, av.at[1]), (u0, uv.at[0]), (u1, uv.at[1]))):
        small.append(pltpu.make_async_copy(src, dst, sems.at[32 + i]))
    big = []
    for block in range(2):
        for r in range(16):
            dst = wv.at[block, pl.ds(r * per, per), :]
            big.append(pltpu.make_async_copy(gathered.at[r, block], dst, sems.at[block * 16 + r]))
    for copy in small + big:
        copy.start()
    for o in range(2):
        xs[o] = x[o]
    here = 0
    for block in range(2):
        for t in range(width // TILE):
            while here < 16 * block + min(16, -(-(t + 1) * TILE // per)):
                big[here].wait()
                here += 1
            wt[block, :, pl.ds(t * TILE, TILE)] = wv[block, pl.ds(t * TILE, TILE), :].T
    for copy in small:
        copy.wait()
    for k in range(2):
        rows = jnp.concatenate([xs[0], xs[1]], axis=0).astype(F32)
        sc = lax.rsqrt(jnp.mean(rows * rows, axis=-1, keepdims=True) + EPS)
        nm = (rows * sc).astype(BF16)
        if k == 1:
            row_blocks(nm, tile, out, h, pl.ds(0, 128))
        for o in range(2):
            part = slice(o * 64, (o + 1) * 64)
            scale[o, k] = jnp.broadcast_to(sc[part], scale.shape[2:])
            mine = nm[part]
            nl[o, k, :, pl.ds(0, width)] = mine
            low = dot(mine, av[o, k]).astype(BF16)
            nl[o, k, :, pl.ds(width, 128)] = low
            block = sel[o, k]
            for t in range(width // TILE):
                cols = pl.ds(t * TILE, TILE)
                pre = dot(mine, wv[block, :, cols]) + dot(low, uv[o, k, cols, :], NT)
                sigma = 1.0 / (1.0 + jnp.exp(-pre))
                slope[o, k, :, cols] = sigma * (1.0 + pre * (1.0 - sigma))
                if k == 0:
                    xs[o, :, cols] = (xs[o, :, cols].astype(F32) + pre * sigma).astype(BF16)


def forward(sel, x, weights):
    rows, width = x.shape[1:]
    rank = weights[1].shape[-1]
    return pl.pallas_call(
        forward_kernel,
        out_shape=(
            pltpu.VMEM((2, 2, rows, width + rank), BF16),
            pltpu.VMEM((2, 2, rows, width), F32),
            pltpu.VMEM((2, 2, rows, 128), F32),
            pltpu.VMEM((2, width, width), BF16),
            pltpu.VMEM((2, 2, width, rank), BF16),
            pltpu.VMEM((2, 2, width, rank), BF16),
            jax.ShapeDtypeStruct((2, 1024, 128), BF16),
        ),
        in_specs=[SM, VM] + [ANY] * 5,
        out_specs=(VM,) * 7,
        scratch_shapes=[
            pltpu.VMEM((2, width, width), BF16),
            pltpu.VMEM((2, rows, width), BF16),
            pltpu.VMEM((width + 8, 128), F32),
            pltpu.SemaphoreType.DMA((36,)),
        ],
        compiler_params=pltpu.CompilerParams(vmem_limit_bytes=28 << 20),
        name="forward",
    )(sel, x, *weights)


def backward_kernel(sel, live, c, nl, slope, scale, wt, av, uv, old_gg, gg, send, gn):
    width = c.shape[-1]

    @pl.when(live[0] == 1)
    def _():
        h = sel[2, 0]
        cur = c[...]
        for j in (1, 0):
            o = jnp.bitwise_xor(h, j)
            for k in (1, 0):
                c32 = cur.astype(F32)
                g = (c32 * slope[o, k]).astype(BF16)
                gg[o, k, :, pl.ds(0, width)] = g
                low = dot(g, uv[o, k]).astype(BF16)
                gg[o, k, :, pl.ds(width, 128)] = low
                block = sel[o, k]
                total = jnp.zeros((g.shape[0], 1), F32)
                for t in range(width // TILE):
                    cols = pl.ds(t * TILE, TILE)
                    part = dot(g, wt[block, :, cols]) + dot(low, av[o, k, cols, :], NT)
                    gn[:, cols] = part
                    total = total + jnp.sum(part * nl[o, k, :, cols].astype(F32), axis=-1, keepdims=True)
                mean = total / width
                z = nl[o, k, :, pl.ds(0, width)].astype(F32)
                sc = scale[o, k, :, 0:1]
                cur = (c32 + sc * (gn[...] - z * mean)).astype(BF16)
            gg[o, 2, :, pl.ds(0, width)] = cur
        send[...] = cur


def pinned(array):
    return pltpu.with_memory_space_constraint(array, pltpu.VMEM)


def backward(sel, live, c, kept, gg):
    rows, width = c.shape
    kept = [pinned(a) for a in kept]
    return pl.pallas_call(
        backward_kernel,
        out_shape=(jax.ShapeDtypeStruct(gg.shape, BF16), jax.ShapeDtypeStruct((rows, width), BF16)),
        in_specs=[SM, SM, VM] + [VM] * 7,
        out_specs=(VM, VM),
        scratch_shapes=[pltpu.VMEM((rows, width), F32)],
        input_output_aliases={9: 0},
        compiler_params=pltpu.CompilerParams(vmem_limit_bytes=12 << 20),
        name="backward",
    )(sel, live, c, *kept, pinned(gg))


def adapter_kernel(nl, gg, nl_peer, gg_peer, out):
    width = nl.shape[-1] - 128
    for k in range(2):
        n = jnp.concatenate([nl[0, k], nl_peer[k]], axis=0)
        g = jnp.concatenate([gg[0, k], gg_peer[k]], axis=0)
        for i, (left, right) in enumerate(((n, g[:, width:]), (g, n[:, width:]))):
            term = dot(left[:, :width], right, TN).astype(BF16)
            for r in range(16):
                out[r % 2, (r // 2) % 4, r // 8, 2 * i + k] = term[r * 112 : (r + 1) * 112]


def adapter_terms(nl, gg, nl_peer, gg_peer):
    return pl.pallas_call(
        adapter_kernel,
        out_shape=jax.ShapeDtypeStruct((2, 4, 2, 4, 112, 128), BF16),
        in_specs=[VM] * 4,
        out_specs=VM,
        compiler_params=pltpu.CompilerParams(vmem_limit_bytes=16 << 20),
        name="adapter_terms",
    )(pinned(nl), pinned(gg), nl_peer, gg_peer)


def transpose_kernel(sel, gp, out):
    quarter = (gp.shape[-1] - 128) // 4
    for k in range(2):
        lanes = pl.ds(k * 128, 128)
        both = jnp.concatenate([gp[0, k], gp[1, k]], axis=0)[:, : 4 * quarter]
        for q in range(4):
            for t in range(0, quarter, 64):
                out[q, pl.ds(t, 64), lanes] = both[:, q * quarter + t : q * quarter + t + 64].T
        side = lax.broadcasted_iota(jnp.int32, (16, 128), 1) // 64
        mark = jnp.where(side == 0, sel[0, k], sel[1, k])
        for q in range(4):
            out[q, pl.ds(quarter, 16), lanes] = mark.astype(F32).astype(BF16)


def transposed(sel, gp):
    quarter = (gp.shape[-1] - 128) // 4
    return pl.pallas_call(
        transpose_kernel,
        out_shape=jax.ShapeDtypeStruct((4, quarter + 16, 256), BF16),
        in_specs=[SM, VM],
        out_specs=VM,
        compiler_params=pltpu.CompilerParams(vmem_limit_bytes=16 << 20),
        name="transposed",
    )(sel, pinned(gp))


def gradient_kernel(*refs):
    pieces, firsts, seconds = refs[:8], refs[8:12], refs[12:16]
    out, left, right, sems = refs[16:]
    copies = []
    for s in range(4):
        for side in range(2):
            for k, src in enumerate((firsts[s], seconds[s])):
                lanes = pl.ds(((s * 2 + side) * 2 + k) * 128, 128)
                copies.append(pltpu.make_async_copy(src.at[side], left.at[:, lanes], sems.at[len(copies)]))
    for copy in copies:
        copy.start()
    quarter = pieces[0].shape[0] - 16
    for i, piece in enumerate(pieces):
        lanes = pl.ds(i * 256, 256)
        whole = piece[pl.ds(0, quarter), :].astype(F32)
        second = whole * piece[pl.ds(quarter, 16), :][0:1].astype(F32)
        right[pl.ds(0, quarter), lanes] = (whole - second).astype(BF16)
        right[pl.ds(quarter, quarter), lanes] = second.astype(BF16)
    for copy in copies:
        copy.wait()
    for m in range(out.shape[0] // TILE):
        rows = pl.ds(m * TILE, TILE)
        out[rows, :] = dot(left[rows, :], right[...], NT).astype(BF16)


def gradient(pieces, firsts, seconds):
    rows = firsts[0].shape[1]
    cols = 2 * (pieces[0].shape[0] - 16)
    return pl.pallas_call(
        gradient_kernel,
        out_shape=jax.ShapeDtypeStruct((rows, cols), BF16),
        in_specs=[VM] * 8 + [ANY] * 8,
        out_specs=VM,
        scratch_shapes=[
            pltpu.VMEM((rows, 2048), BF16),
            pltpu.VMEM((cols, 2048), BF16),
            pltpu.SemaphoreType.DMA((16,)),
        ],
        compiler_params=pltpu.CompilerParams(vmem_limit_bytes=40 << 20),
        name="gradient",
    )(*pieces, *firsts, *seconds)


def at(array, index):
    return lax.dynamic_index_in_dim(array, index, 0, keepdims=False)


def sum_dp(buf):
    r = lax.axis_index("dp")
    core, z, y = r % 2, (r // 2) % 4, r // 8
    got = lax.ppermute(at(buf, 1 - core), "dp", [(i, i ^ 1) for i in range(16)])
    buf = (at(buf, core).astype(F32) + got.astype(F32)).astype(BF16)
    total = at(buf, z).astype(F32)
    for d in range(1, 4):
        pairs = [(i, i // 8 * 8 + (i + 2 * d) % 8) for i in range(16)]
        total = total + lax.ppermute(at(buf, (z + d) % 4), "dp", pairs).astype(F32)
    buf = total.astype(BF16)
    got = lax.ppermute(at(buf, 1 - y), "dp", [(i, i ^ 8) for i in range(16)])
    return at(buf, y).astype(F32) + got.astype(F32)


def shards(stored, common, down, up, selection, final_c):
    n_pipe, n_dp = lax.axis_size("pipe"), lax.axis_size("dp")
    p = lax.axis_index("pipe")
    x_at, h = p // 2, p % 2
    swap = [(i, i ^ 1) for i in range(n_pipe)]
    turns = [[(i, (i + 2 * d) % n_pipe) for i in range(n_pipe)] for d in range(4)]
    own = stored[0]
    rows, width = own.shape
    half = rows // 2
    a_own, u_own = down[0], up[0]

    def joined(parts):
        return jnp.stack([parts[0], lax.ppermute(parts[1], "pipe", swap)])

    mixed = common.transpose(1, 0, 2).reshape(-1, width)
    gathered = lax.all_gather(mixed, "dp", axis=0, tiled=True).reshape(n_dp, 2, -1, width)
    x_mine = lax.dynamic_slice_in_dim(own, h * half, half, 0)
    x_other = lax.dynamic_slice_in_dim(own, (1 - h) * half, half, 0)
    x_peer = lax.ppermute(x_other, "pipe", swap)
    sel_peer = lax.ppermute(selection, "pipe", swap)
    a_peer = lax.ppermute(a_own, "pipe", swap)
    u_peer = lax.ppermute(u_own, "pipe", swap)
    sel = jnp.concatenate([selection, sel_peer, jnp.full((1, 2), h, jnp.int32)])
    weights = (gathered, a_own, a_peer, u_own, u_peer)
    entered = jnp.stack([x_mine, x_peer])
    firsts = [joined(first_rows(sel, entered))]
    firsts += [lax.ppermute(firsts[0], "pipe", turns[d]) for d in range(1, 4)]
    *kept, second = forward(sel, entered, weights)
    nl = kept[0]

    c = lax.dynamic_slice_in_dim(final_c, h * half, half, 0)
    rank = a_own.shape[-1]
    gg = jnp.zeros((2, 3, half, width + rank), BF16)
    seconds = [joined(second)]
    steps = n_pipe // 2
    for t in range(steps):
        place = steps - 1 - t
        live = (x_at == place).astype(jnp.int32)[None]
        gg, send = backward(sel, live, c, kept, gg)
        if place > 0:
            c = lax.ppermute(send, "pipe", [(2 * place + i, 2 * place - 2 + i) for i in range(2)])
            seconds.append(lax.ppermute(seconds[-1], "pipe", turns[1]))
    nl_peer = lax.ppermute(nl[1], "pipe", swap)

    quarters = transposed(sel, gg)
    pieces = [at(quarters, x_at)]
    pieces += [lax.ppermute(at(quarters, (x_at + d) % 4), "pipe", turns[d]) for d in range(1, 4)]
    pieces = [q for piece in pieces for q in (piece, lax.ppermute(piece, "pipe", swap))]
    tile = gradient(pieces, firsts, seconds)
    tile = sum_dp(tile.reshape(2, 4, 2, 4, 16, tile.shape[-1])).astype(BF16)
    placed = jnp.stack(
        [at(tile, x_at)]
        + [lax.ppermute(at(tile, (x_at + d) % 4), "pipe", turns[d]) for d in range(1, 4)]
    )
    placed = jnp.stack([at(placed, (x_at - s) % 4) for s in range(4)], axis=1)
    each = width // (n_pipe * n_dp)
    shared = placed[:each].reshape(each, 4, 2, width // 4).transpose(0, 2, 1, 3)
    shared = shared.reshape(each, 2, width).astype(F32)

    gg_peer = lax.ppermute(gg[1], "pipe", swap)
    ours, theirs = gg[0, 2, :, :width], gg_peer[2, :, :width]
    result = jnp.where(
        h == 0, jnp.concatenate([ours, theirs]), jnp.concatenate([theirs, ours])
    )
    both = sum_dp(adapter_terms(nl, gg, nl_peer, gg_peer))
    return result[None], shared, both[None, :2], both[None, 2:]


def solution(mesh):
    return jax.shard_map(
        shards,
        mesh=mesh,
        in_specs=(
            P("pipe", "dp", None),
            P("dp", None, None),
            P("pipe", None, None, None),
            P("pipe", None, None, None),
            P("pipe", None),
            P("dp", None),
        ),
        out_specs=(
            P("pipe", "dp", None),
            P(("pipe", "dp"), None, None),
            P("pipe", None, "dp", None),
            P("pipe", None, "dp", None),
        ),
        check_vma=False,
    )
```

```python
import functools

import jax
import jax.numpy as jnp
from jax import lax
from jax.experimental import pallas as pl
from jax.experimental.pallas import tpu as pltpu
from jax.sharding import PartitionSpec as P

EPS = 1e-06
TILE = 256
F32 = jnp.float32
BF16 = jnp.bfloat16
NT = (((1,), (1,)), ((), ()))
TN = (((0,), (0,)), ((), ()))
ANY = pl.BlockSpec(memory_space=pl.ANY)
VM = pl.BlockSpec(memory_space=pltpu.VMEM)
SM = pl.BlockSpec(memory_space=pltpu.SMEM)


def dot(a, b, dims=(((1,), (0,)), ((), ()))):
    return lax.dot_general(a, b, dims, preferred_element_type=F32)


PIECES = ((0, 0, None), (0, 3, None), (0, 1, None), (0, 2, 0), (0, 2, 1)) + (
    (1, 0, 0), (1, 0, 1), (1, 3, None), (1, 1, None), (1, 2, 0), (1, 2, 1)
)


def row_blocks(src, tile, dst, h, lanes):
    width = src.shape[1]
    for t in range(width // TILE):
        tile[pl.ds(t * TILE, TILE), :] = src[:, t * TILE : (t + 1) * TILE].astype(F32).T
    tile[pl.ds(width, 8), :] = jnp.zeros((8, tile.shape[1]), F32)
    for p in range(8):
        x, half = p // 2, p % 2
        slot = jnp.bitwise_xor(h, half)
        for r in range(16):
            core, z, y = r % 2, (r // 2) % 4, r // 8
            at_row = (((core * 4 + z) * 2 + y) * 4 + x) * 16
            dst[slot, pl.ds(at_row, 16), lanes] = tile[pl.ds((p * 16 + r) * 14, 16), :].astype(BF16)


def first_kernel(sel, x, out, tile):
    rows = jnp.concatenate([x[0], x[1]], axis=0).astype(F32)
    sc = lax.rsqrt(jnp.mean(rows * rows, axis=-1, keepdims=True) + EPS)
    row_blocks((rows * sc).astype(BF16), tile, out, sel[2, 0], pl.ds(0, 128))


def first_rows(sel, x):
    width = x.shape[-1]
    return pl.pallas_call(
        first_kernel,
        out_shape=jax.ShapeDtypeStruct((2, 1024, 128), BF16),
        in_specs=[SM, VM],
        out_specs=VM,
        scratch_shapes=[pltpu.VMEM((width + 8, 128), F32)],
        compiler_params=pltpu.CompilerParams(vmem_limit_bytes=16 << 20),
        name="first_rows",
    )(sel, x)


def forward_kernel(sel, x, *refs):
    a_own, u_own, near, far = refs[:4]
    pieces = refs[4 : 4 + 2 * len(PIECES)]
    nl, slope, scale, wt, auv, out, wv, xs, tile, sems = refs[4 + 2 * len(PIECES) :]
    av, uv = auv.at[0], auv.at[1]
    width = x.shape[-1]
    per = pieces[0].shape[-2]
    h, r = sel[2, 0], sel[2, 1]
    core, z, y = r % 2, (r // 2) % 4, r // 8
    small = []
    for i, (src, dst) in enumerate(
        ((a_own, av.at[0]), (u_own, uv.at[0]), (near, auv.at[core, 1]), (far, auv.at[1 - core, 1]))
    ):
        small.append(pltpu.make_async_copy(src, dst, sems.at[32 + i]))
    for copy in small:
        copy.start()
    for block in range(2):
        for i, ref in enumerate(pieces):
            dy, dz, held = PIECES[i // 2]
            if held is not None and held != block:
                continue
            place = jnp.bitwise_xor(y, dy) * 8 + (z + dz) % 4 * 2 + jnp.bitwise_xor(core, i % 2)
            dst = wv.at[block, pl.ds(pl.multiple_of(place * per, 16), per), :]
            src = ref.at[block] if held is None else ref
            pltpu.make_async_copy(src, dst, sems.at[block * 16 + place]).start()
    big = []
    for block in range(2):
        for place in range(16):
            dst = wv.at[block, pl.ds(place * per, per), :]
            big.append(pltpu.make_async_copy(dst, dst, sems.at[block * 16 + place]))
    for o in range(2):
        xs[o] = x[o]
    here = 0
    for block in range(2):
        for t in range(width // TILE):
            while here < 16 * block + min(16, -(-(t + 1) * TILE // per)):
                big[here].wait()
                here += 1
            wt[block, :, pl.ds(t * TILE, TILE)] = wv[block, pl.ds(t * TILE, TILE), :].T
    for copy in small:
        copy.wait()
    for k in range(2):
        rows = jnp.concatenate([xs[0], xs[1]], axis=0).astype(F32)
        sc = lax.rsqrt(jnp.mean(rows * rows, axis=-1, keepdims=True) + EPS)
        nm = (rows * sc).astype(BF16)
        if k == 1:
            row_blocks(nm, tile, out, h, pl.ds(0, 128))
        for o in range(2):
            part = slice(o * 64, (o + 1) * 64)
            scale[o, k] = jnp.broadcast_to(sc[part], scale.shape[2:])
            mine = nm[part]
            nl[o, k, :, pl.ds(0, width)] = mine
            low = dot(mine, av[o, k]).astype(BF16)
            nl[o, k, :, pl.ds(width, 128)] = low
            block = sel[o, k]
            for t in range(width // TILE):
                cols = pl.ds(t * TILE, TILE)
                pre = dot(mine, wv[block, :, cols]) + dot(low, uv[o, k, cols, :], NT)
                sigma = 1.0 / (1.0 + jnp.exp(-pre))
                slope[o, k, :, cols] = sigma * (1.0 + pre * (1.0 - sigma))
                if k == 0:
                    xs[o, :, cols] = (xs[o, :, cols].astype(F32) + pre * sigma).astype(BF16)


def forward(sel, x, weights):
    rows, width = x.shape[1:]
    rank = weights[0].shape[-1]
    return pl.pallas_call(
        forward_kernel,
        out_shape=(
            pltpu.VMEM((2, 2, rows, width + rank), BF16),
            pltpu.VMEM((2, 2, rows, width), F32),
            pltpu.VMEM((2, 2, rows, 128), F32),
            pltpu.VMEM((2, width, width), BF16),
            pltpu.VMEM((2, 2, 2, width, rank), BF16),
            jax.ShapeDtypeStruct((2, 1024, 128), BF16),
        ),
        in_specs=[SM, VM] + [ANY] * len(weights),
        out_specs=(VM,) * 6,
        scratch_shapes=[
            pltpu.VMEM((2, width, width), BF16),
            pltpu.VMEM((2, rows, width), BF16),
            pltpu.VMEM((width + 8, 128), F32),
            pltpu.SemaphoreType.DMA((36,)),
        ],
        compiler_params=pltpu.CompilerParams(vmem_limit_bytes=28 << 20),
        name="forward",
    )(sel, x, *weights)


def backward_kernel(sel, live, c, nl, slope, scale, wt, auv, old_gg, gg, send, gn):
    width = c.shape[-1]
    av, uv = auv.at[0], auv.at[1]

    @pl.when(live[0] == 1)
    def _():
        h = sel[2, 0]
        cur = c[...]
        for j in (1, 0):
            o = jnp.bitwise_xor(h, j)
            for k in (1, 0):
                c32 = cur.astype(F32)
                g = (c32 * slope[o, k]).astype(BF16)
                gg[o, k, :, pl.ds(0, width)] = g
                low = dot(g, uv[o, k]).astype(BF16)
                gg[o, k, :, pl.ds(width, 128)] = low
                block = sel[o, k]
                total = jnp.zeros((g.shape[0], 1), F32)
                for t in range(width // TILE):
                    cols = pl.ds(t * TILE, TILE)
                    part = dot(g, wt[block, :, cols]) + dot(low, av[o, k, cols, :], NT)
                    gn[:, cols] = part
                    total = total + jnp.sum(part * nl[o, k, :, cols].astype(F32), axis=-1, keepdims=True)
                mean = total / width
                z = nl[o, k, :, pl.ds(0, width)].astype(F32)
                sc = scale[o, k, :, 0:1]
                cur = (c32 + sc * (gn[...] - z * mean)).astype(BF16)
            gg[o, 2, :, pl.ds(0, width)] = cur
        send[...] = cur


def pinned(array):
    return pltpu.with_memory_space_constraint(array, pltpu.VMEM)


def backward(sel, live, c, kept, gg):
    rows, width = c.shape
    kept = [pinned(a) for a in kept]
    return pl.pallas_call(
        backward_kernel,
        out_shape=(jax.ShapeDtypeStruct(gg.shape, BF16), jax.ShapeDtypeStruct((rows, width), BF16)),
        in_specs=[SM, SM, VM] + [VM] * 6,
        out_specs=(VM, VM),
        scratch_shapes=[pltpu.VMEM((rows, width), F32)],
        input_output_aliases={8: 0},
        compiler_params=pltpu.CompilerParams(vmem_limit_bytes=12 << 20),
        name="backward",
    )(sel, live, c, *kept, pinned(gg))


def transpose_kernel(sel, gp, out):
    quarter = (gp.shape[-1] - 128) // 4
    for k in range(2):
        lanes = pl.ds(k * 128, 128)
        both = jnp.concatenate([gp[0, k], gp[1, k]], axis=0)[:, : 4 * quarter]
        for q in range(4):
            for t in range(0, quarter, 64):
                out[q, pl.ds(t, 64), lanes] = both[:, q * quarter + t : q * quarter + t + 64].T
        side = lax.broadcasted_iota(jnp.int32, (16, 128), 1) // 64
        mark = jnp.where(side == 0, sel[0, k], sel[1, k])
        for q in range(4):
            out[q, pl.ds(quarter, 16), lanes] = mark.astype(F32).astype(BF16)


def transposed(sel, gp):
    quarter = (gp.shape[-1] - 128) // 4
    return pl.pallas_call(
        transpose_kernel,
        out_shape=jax.ShapeDtypeStruct((4, quarter + 16, 256), BF16),
        in_specs=[SM, VM],
        out_specs=VM,
        compiler_params=pltpu.CompilerParams(vmem_limit_bytes=16 << 20),
        name="transposed",
    )(sel, pinned(gp))


def gradient_kernel(*refs):
    sel, firsts, seconds, nl, gg, nl_peer, gg_peer = refs[:7]
    pieces = refs[7:15]
    out, left, right, sems = refs[15:]
    x_at = sel[3, 0]
    copies = []
    for s in range(4):
        source = (x_at + 4 - s) % 4
        for side in range(2):
            for k, rows in enumerate((firsts, seconds)):
                lanes = pl.ds(((s * 2 + side) * 2 + k) * 128, 128)
                copies.append(
                    pltpu.make_async_copy(rows.at[source, side], left.at[:, lanes], sems.at[len(copies)])
                )
    for copy in copies:
        copy.start()
    width = nl.shape[-1] - 128
    for k in range(2):
        n = jnp.concatenate([nl[0, k], nl_peer[k]], axis=0)
        g = jnp.concatenate([gg[0, k], gg_peer[k]], axis=0)
        for i, (lhs, rhs) in enumerate(((n, g[:, width:]), (g, n[:, width:]))):
            term = dot(lhs[:, :width], rhs, TN).astype(BF16)
            for r in range(16):
                for t in range(7):
                    out[r % 2, (r // 2) % 4, r // 8, pl.ds(64 + (2 * i + k) * 16, 16), pl.ds(t * 128, 128)] = (
                        term[r * 112 + t * 16 : r * 112 + t * 16 + 16]
                    )
    quarter = pieces[0].shape[0] - 16
    for i, piece in enumerate(pieces):
        lanes = pl.ds(i * 256, 256)
        whole = piece[pl.ds(0, quarter), :].astype(F32)
        second = whole * piece[pl.ds(quarter, 16), :][0:1].astype(F32)
        right[pl.ds(0, quarter), lanes] = (whole - second).astype(BF16)
        right[pl.ds(quarter, quarter), lanes] = second.astype(BF16)
    for copy in copies:
        copy.wait()
    for m in range(left.shape[0] // TILE):
        part = dot(left[pl.ds(m * TILE, TILE), :], right[...], NT).astype(BF16)
        for i in range(4):
            at_chunk = m * 4 + i
            out[at_chunk // 8, at_chunk // 2 % 4, at_chunk % 2, pl.ds(0, 64), :] = part[i * 64 : i * 64 + 64]


def gradient(sel, firsts, seconds, nl, gg, nl_peer, gg_peer, pieces):
    rows = firsts.shape[2]
    cols = 2 * (pieces[0].shape[0] - 16)
    return pl.pallas_call(
        gradient_kernel,
        out_shape=jax.ShapeDtypeStruct((2, 4, 2, 128, cols), BF16),
        in_specs=[SM, ANY, ANY] + [VM] * 12,
        out_specs=VM,
        scratch_shapes=[
            pltpu.VMEM((rows, 2048), BF16),
            pltpu.VMEM((cols, 2048), BF16),
            pltpu.SemaphoreType.DMA((16,)),
        ],
        compiler_params=pltpu.CompilerParams(vmem_limit_bytes=32 << 20),
        name="gradient",
    )(sel, firsts, seconds, pinned(nl), pinned(gg), nl_peer, gg_peer, *pieces)


def at(array, index):
    return lax.dynamic_index_in_dim(array, index, 0, keepdims=False)


def move(array, dy=0, dz=0, flip=0):
    pairs = []
    for x in range(4):
        for y in range(4):
            for z in range(4):
                for core in range(2):
                    to_y, to_z = (y + dy) % 4, (z + dz) % 4
                    src = (x * 2 + y // 2) * 16 + y % 2 * 8 + z * 2 + core
                    dst = (x * 2 + to_y // 2) * 16 + to_y % 2 * 8 + to_z * 2 + (core ^ flip)
                    pairs.append((src, dst))
    return lax.ppermute(array, ("pipe", "dp"), pairs)


def sum_dp(buf):
    r = lax.axis_index("dp")
    core, z, y = r % 2, (r // 2) % 4, r // 8
    got = lax.ppermute(at(buf, 1 - core), "dp", [(i, i ^ 1) for i in range(16)])
    buf = (at(buf, core).astype(F32) + got.astype(F32)).astype(BF16)
    total = at(buf, z).astype(F32)
    for d in range(1, 4):
        pairs = [(i, i // 8 * 8 + (i + 2 * d) % 8) for i in range(16)]
        total = total + lax.ppermute(at(buf, (z + d) % 4), "dp", pairs).astype(F32)
    buf = total.astype(BF16)
    got = lax.ppermute(at(buf, 1 - y), "dp", [(i, i ^ 8) for i in range(16)])
    return at(buf, y).astype(F32) + got.astype(F32)


def shards(stored, common, down, up, selection, final_c):
    n_pipe, n_dp = lax.axis_size("pipe"), lax.axis_size("dp")
    p = lax.axis_index("pipe")
    x_at, h = p // 2, p % 2
    swap = [(i, i ^ 1) for i in range(n_pipe)]
    turns = [[(i, (i + 2 * d) % n_pipe) for i in range(n_pipe)] for d in range(4)]
    own = stored[0]
    rows, width = own.shape
    half = rows // 2
    a_own, u_own = down[0], up[0]

    def joined(parts):
        return jnp.stack([parts[0], lax.ppermute(parts[1], "pipe", swap)])

    r = lax.axis_index("dp")
    core = r % 2
    spread = [[0, 2, 4, 6], [1, 3, 5, 7]]

    def over_x(array):
        return lax.all_gather(array, "pipe", axis_index_groups=spread)

    mixed = common.transpose(1, 0, 2)
    up_z, down_z = move(mixed, dz=1), move(mixed, dz=-1)
    other_y = [move(mixed[0], dy=1), move(mixed[1], dy=-1)]
    far_z = [move(up_z[0], dz=1), move(down_z[1], dz=-1)]
    tail = [move(up_z, dy=1), move(down_z, dy=-1), move(far_z[0], dy=1), move(far_z[1], dy=-1)]
    pieces = [mixed, up_z, down_z] + far_z + other_y + tail
    pieces = [q for piece in pieces for q in (piece, move(piece, flip=1))]
    near = move(jnp.where(core == 0, a_own, u_own), dy=2)
    far = move(near, flip=1)
    x_mine = lax.dynamic_slice_in_dim(own, h * half, half, 0)
    x_other = lax.dynamic_slice_in_dim(own, (1 - h) * half, half, 0)
    x_peer = lax.ppermute(x_other, "pipe", swap)
    sel_peer = lax.ppermute(selection, "pipe", swap)
    sel = jnp.concatenate([selection, sel_peer, jnp.stack([h, r, x_at, x_at]).astype(jnp.int32).reshape(2, 2)])
    weights = (a_own, u_own, near, far, *pieces)
    entered = jnp.stack([x_mine, x_peer])
    firsts = over_x(joined(first_rows(sel, entered)))
    entered, firsts = lax.optimization_barrier((entered, firsts))
    *kept, second = forward(sel, entered, weights)
    nl = kept[0]

    c = lax.dynamic_slice_in_dim(final_c, h * half, half, 0)
    rank = a_own.shape[-1]
    gg = jnp.zeros((2, 3, half, width + rank), BF16)
    seconds = over_x(joined(second))
    steps = n_pipe // 2
    for t in range(steps):
        place = steps - 1 - t
        live = (x_at == place).astype(jnp.int32)[None]
        gg, send = backward(sel, live, c, kept, gg)
        if place > 0:
            c = lax.ppermute(send, "pipe", [(2 * place + i, 2 * place - 2 + i) for i in range(2)])
    nl_peer = lax.ppermute(nl[1], "pipe", swap)

    quarters = transposed(sel, gg)
    quarters, gg = lax.optimization_barrier((quarters, gg))
    gg_peer = lax.ppermute(gg[1], "pipe", swap)
    pieces = [at(quarters, x_at)]
    pieces += [lax.ppermute(at(quarters, (x_at + d) % 4), "pipe", turns[d]) for d in range(1, 4)]
    pieces = [q for piece in pieces for q in (piece, lax.ppermute(piece, "pipe", swap))]
    summed = sum_dp(gradient(sel, firsts, seconds, nl, gg, nl_peer, gg_peer, pieces))
    tile = summed[:64].astype(BF16).reshape(4, 16, -1)
    placed = jnp.stack(
        [at(tile, x_at)]
        + [lax.ppermute(at(tile, (x_at + d) % 4), "pipe", turns[d]) for d in range(1, 4)]
    )
    placed = jnp.stack([at(placed, (x_at - s) % 4) for s in range(4)], axis=1)
    each = width // (n_pipe * n_dp)
    shared = placed[:each].reshape(each, 4, 2, width // 4).transpose(0, 2, 1, 3)
    shared = shared.reshape(each, 2, width).astype(F32)

    ours, theirs = gg[0, 2, :, :width], gg_peer[2, :, :width]
    result = jnp.where(
        h == 0, jnp.concatenate([ours, theirs]), jnp.concatenate([theirs, ours])
    )
    both = summed[64:].reshape(4, 16, 7, rank).transpose(0, 2, 1, 3).reshape(4, 112, rank)
    return result[None], shared, both[None, :2], both[None, 2:]


def solution(mesh):
    return jax.shard_map(
        shards,
        mesh=mesh,
        in_specs=(
            P("pipe", "dp", None),
            P("dp", None, None),
            P("pipe", None, None, None),
            P("pipe", None, None, None),
            P("pipe", None),
            P("dp", None),
        ),
        out_specs=(
            P("pipe", "dp", None),
            P(("pipe", "dp"), None, None),
            P("pipe", None, "dp", None),
            P("pipe", None, "dp", None),
        ),
        check_vma=False,
    )
```

```python
import functools

import jax
import jax.numpy as jnp
from jax import lax
from jax.experimental import pallas as pl
from jax.experimental.pallas import tpu as pltpu
from jax.sharding import PartitionSpec as P

EPS = 1e-06
TILE = 256
F32 = jnp.float32
BF16 = jnp.bfloat16
NT = (((1,), (1,)), ((), ()))
TN = (((0,), (0,)), ((), ()))
HB = pl.BlockSpec(memory_space=pltpu.HBM)
VM = pl.BlockSpec(memory_space=pltpu.VMEM)
SM = pl.BlockSpec(memory_space=pltpu.SMEM)


def dot(a, b, dims=(((1,), (0,)), ((), ()))):
    return lax.dot_general(a, b, dims, preferred_element_type=F32)


def pinned(array):
    return pltpu.with_memory_space_constraint(array, pltpu.VMEM)


def in_hbm(array):
    return pltpu.with_memory_space_constraint(array, pltpu.HBM)


PIECES = ((0, 0, None), (0, 3, None), (0, 1, None), (0, 2, 0), (0, 2, 1)) + (
    (1, 0, 0), (1, 0, 1), (1, 3, None), (1, 1, None), (1, 2, 0), (1, 2, 1)
)


def row_blocks(src, tile, dst, h, lanes):
    width = src.shape[1]
    for t in range(width // TILE):
        tile[pl.ds(t * TILE, TILE), :] = src[:, t * TILE : (t + 1) * TILE].astype(F32).T
    tile[pl.ds(width, 8), :] = jnp.zeros((8, tile.shape[1]), F32)
    for p in range(8):
        x, half = p // 2, p % 2
        slot = jnp.bitwise_xor(h, half)
        for r in range(16):
            core, z, y = r % 2, (r // 2) % 4, r // 8
            at_row = (((core * 4 + z) * 2 + y) * 4 + x) * 16
            dst[slot, pl.ds(at_row, 16), lanes] = tile[pl.ds((p * 16 + r) * 14, 16), :].astype(BF16)


def first_kernel(sel, x, out, tile):
    rows = jnp.concatenate([x[0], x[1]], axis=0).astype(F32)
    sc = lax.rsqrt(jnp.mean(rows * rows, axis=-1, keepdims=True) + EPS)
    row_blocks((rows * sc).astype(BF16), tile, out, sel[2, 0], pl.ds(0, 128))


def first_rows(sel, x):
    width = x.shape[-1]
    return pl.pallas_call(
        first_kernel,
        out_shape=jax.ShapeDtypeStruct((2, 1024, 128), BF16),
        in_specs=[SM, VM],
        out_specs=VM,
        scratch_shapes=[pltpu.VMEM((width + 8, 128), F32)],
        compiler_params=pltpu.CompilerParams(vmem_limit_bytes=16 << 20),
        name="first_rows",
    )(sel, x)


def forward_kernel(sel, x, *refs):
    a_own, u_own, near, far = refs[:4]
    pieces = refs[4 : 4 + 2 * len(PIECES)]
    nl, slope, scale, wt, auv, gg, out, wv, xs, tile, sems = refs[4 + 2 * len(PIECES) :]
    av, uv = auv.at[0], auv.at[1]
    width = x.shape[-1]
    per = pieces[0].shape[-2]
    h, r = sel[2, 0], sel[2, 1]
    core, z, y = r % 2, (r // 2) % 4, r // 8
    small = []
    for i, (src, dst) in enumerate(
        ((a_own, av.at[0]), (u_own, uv.at[0]), (near, auv.at[core, 1]), (far, auv.at[1 - core, 1]))
    ):
        small.append(pltpu.make_async_copy(src, dst, sems.at[32 + i]))
    for copy in small:
        copy.start()
    for block in range(2):
        for i, ref in enumerate(pieces):
            dy, dz, held = PIECES[i // 2]
            if held is not None and held != block:
                continue
            place = jnp.bitwise_xor(y, dy) * 8 + (z + dz) % 4 * 2 + jnp.bitwise_xor(core, i % 2)
            dst = wv.at[block, pl.ds(pl.multiple_of(place * per, 16), per), :]
            src = ref.at[block] if held is None else ref
            pltpu.make_async_copy(src, dst, sems.at[block * 16 + place]).start()
    big = []
    for block in range(2):
        for place in range(16):
            dst = wv.at[block, pl.ds(place * per, per), :]
            big.append(pltpu.make_async_copy(dst, dst, sems.at[block * 16 + place]))
    gg[...] = jnp.zeros_like(gg)
    for o in range(2):
        xs[o] = x[o]
    here = 0
    for block in range(2):
        for t in range(width // TILE):
            while here < 16 * block + min(16, -(-(t + 1) * TILE // per)):
                big[here].wait()
                here += 1
            wt[block, :, pl.ds(t * TILE, TILE)] = wv[block, pl.ds(t * TILE, TILE), :].T
    for copy in small:
        copy.wait()
    for k in range(2):
        rows = jnp.concatenate([xs[0], xs[1]], axis=0).astype(F32)
        sc = lax.rsqrt(jnp.mean(rows * rows, axis=-1, keepdims=True) + EPS)
        nm = (rows * sc).astype(BF16)
        if k == 1:
            row_blocks(nm, tile, out, h, pl.ds(0, 128))
        for o in range(2):
            part = slice(o * 64, (o + 1) * 64)
            scale[o, k] = jnp.broadcast_to(sc[part], scale.shape[2:])
            mine = nm[part]
            nl[o, k, :, pl.ds(0, width)] = mine
            low = dot(mine, av[o, k]).astype(BF16)
            nl[o, k, :, pl.ds(width, 128)] = low
            block = sel[o, k]
            for t in range(width // TILE):
                cols = pl.ds(t * TILE, TILE)
                pre = dot(mine, wv[block, :, cols]) + dot(low, uv[o, k, cols, :], NT)
                sigma = 1.0 / (1.0 + jnp.exp(-pre))
                slope[o, k, :, cols] = sigma * (1.0 + pre * (1.0 - sigma))
                if k == 0:
                    xs[o, :, cols] = (xs[o, :, cols].astype(F32) + pre * sigma).astype(BF16)


def forward(sel, x, weights):
    rows, width = x.shape[1:]
    rank = weights[0].shape[-1]
    return pl.pallas_call(
        forward_kernel,
        out_shape=(
            pltpu.VMEM((2, 2, rows, width + rank), BF16),
            pltpu.VMEM((2, 2, rows, width), F32),
            pltpu.VMEM((2, 2, rows, 128), F32),
            pltpu.VMEM((2, width, width), BF16),
            pltpu.VMEM((2, 2, 2, width, rank), BF16),
            pltpu.VMEM((2, 3, rows, width + rank), BF16),
            jax.ShapeDtypeStruct((2, 1024, 128), BF16),
        ),
        in_specs=[SM, VM] + [HB] * len(weights),
        out_specs=(VM,) * 7,
        scratch_shapes=[
            pltpu.VMEM((2, width, width), BF16),
            pltpu.VMEM((2, rows, width), BF16),
            pltpu.VMEM((width + 8, 128), F32),
            pltpu.SemaphoreType.DMA((36,)),
        ],
        compiler_params=pltpu.CompilerParams(vmem_limit_bytes=28 << 20),
        name="forward",
    )(sel, x, *[in_hbm(w) for w in weights])


def backward_kernel(at_place, sel, c, nl, slope, scale, wt, auv, old_gg, gg, send, gn):
    width = c.shape[-1]
    av, uv = auv.at[0], auv.at[1]

    @pl.when(sel[3, 0] == at_place)
    def _():
        h = sel[2, 0]
        cur = c[...]
        for j in (1, 0):
            o = jnp.bitwise_xor(h, j)
            for k in (1, 0):
                c32 = cur.astype(F32)
                g = (c32 * slope[o, k]).astype(BF16)
                gg[o, k, :, pl.ds(0, width)] = g
                low = dot(g, uv[o, k]).astype(BF16)
                gg[o, k, :, pl.ds(width, 128)] = low
                block = sel[o, k]
                total = jnp.zeros((g.shape[0], 1), F32)
                for t in range(width // TILE):
                    cols = pl.ds(t * TILE, TILE)
                    part = dot(g, wt[block, :, cols]) + dot(low, av[o, k, cols, :], NT)
                    gn[:, cols] = part
                    total = total + jnp.sum(part * nl[o, k, :, cols].astype(F32), axis=-1, keepdims=True)
                mean = total / width
                z = nl[o, k, :, pl.ds(0, width)].astype(F32)
                sc = scale[o, k, :, 0:1]
                cur = (c32 + sc * (gn[...] - z * mean)).astype(BF16)
            gg[o, 2, :, pl.ds(0, width)] = cur
        send[...] = cur


def backward(at_place, sel, c, kept, gg):
    rows, width = c.shape
    kept = [pinned(a) for a in kept]
    return pl.pallas_call(
        functools.partial(backward_kernel, at_place),
        out_shape=(jax.ShapeDtypeStruct(gg.shape, BF16), jax.ShapeDtypeStruct((rows, width), BF16)),
        in_specs=[SM, VM] + [VM] * 6,
        out_specs=(VM, VM),
        scratch_shapes=[pltpu.VMEM((rows, width), F32)],
        input_output_aliases={7: 0},
        compiler_params=pltpu.CompilerParams(vmem_limit_bytes=12 << 20),
        name="backward",
    )(sel, c, *kept, pinned(gg))


def transpose_kernel(at_place, sel, gp, out):
    quarter = (gp.shape[-1] - 128) // 4

    @pl.when(sel[3, 0] == at_place)
    def _():
        for k in range(2):
            lanes = pl.ds(k * 128, 128)
            both = jnp.concatenate([gp[0, k], gp[1, k]], axis=0)[:, : 4 * quarter]
            for q in range(4):
                for t in range(0, quarter, 64):
                    out[q, pl.ds(t, 64), lanes] = both[:, q * quarter + t : q * quarter + t + 64].T
            side = lax.broadcasted_iota(jnp.int32, (16, 128), 1) // 64
            mark = jnp.where(side == 0, sel[0, k], sel[1, k])
            for q in range(4):
                out[q, pl.ds(quarter, 16), lanes] = mark.astype(F32).astype(BF16)


def transposed(at_place, sel, gp):
    quarter = (gp.shape[-1] - 128) // 4
    return pl.pallas_call(
        functools.partial(transpose_kernel, at_place),
        out_shape=jax.ShapeDtypeStruct((4, quarter + 16, 256), BF16),
        in_specs=[SM, VM],
        out_specs=VM,
        compiler_params=pltpu.CompilerParams(vmem_limit_bytes=12 << 20),
        name="transposed",
    )(sel, pinned(gp))


def choose_kernel(at_place, sel, quarters, one, two, three, out):
    away = (sel[3, 0] + 4 - at_place) % 4

    @pl.when(away == 0)
    def _():
        out[...] = quarters[at_place]

    for d, got in ((1, one), (2, two), (3, three)):

        @pl.when(away == d)
        def _(got=got):
            out[...] = got[...]


def choose(at_place, sel, quarters, got):
    return pl.pallas_call(
        functools.partial(choose_kernel, at_place),
        out_shape=jax.ShapeDtypeStruct(quarters.shape[1:], BF16),
        in_specs=[SM] + [VM] * 4,
        out_specs=VM,
        compiler_params=pltpu.CompilerParams(vmem_limit_bytes=8 << 20),
        name="choose",
    )(sel, quarters, *got)


def gradient_kernel(*refs):
    sel, nl, gg, nl_peer, gg_peer = refs[:5]
    pieces, firsts, seconds = refs[5:13], refs[13:17], refs[17:21]
    out, left, right, sems = refs[21:]
    copies = []
    for d in range(4):
        source = (sel[3, 0] + 4 - d) % 4
        for side in range(2):
            for k, rows in enumerate((firsts[d], seconds[d])):
                lanes = pl.ds(pl.multiple_of(source * 512, 128) + (side * 2 + k) * 128, 128)
                copies.append(pltpu.make_async_copy(rows.at[side], left.at[:, lanes], sems.at[len(copies)]))
    for copy in copies:
        copy.start()
    width = nl.shape[-1] - 128
    for k in range(2):
        n = jnp.concatenate([nl[0, k], nl_peer[k]], axis=0)
        g = jnp.concatenate([gg[0, k], gg_peer[k]], axis=0)
        for i, (lhs, rhs) in enumerate(((n, g[:, width:]), (g, n[:, width:]))):
            term = dot(lhs[:, :width], rhs, TN).astype(BF16)
            for r in range(16):
                for t in range(7):
                    out[r % 2, (r // 2) % 4, r // 8, pl.ds(64 + (2 * i + k) * 16, 16), pl.ds(t * 128, 128)] = (
                        term[r * 112 + t * 16 : r * 112 + t * 16 + 16]
                    )
    quarter = pieces[0].shape[0] - 16
    for i, piece in enumerate(pieces):
        lanes = pl.ds(i * 256, 256)
        whole = piece[pl.ds(0, quarter), :].astype(F32)
        second = whole * piece[pl.ds(quarter, 16), :][0:1].astype(F32)
        right[pl.ds(0, quarter), lanes] = (whole - second).astype(BF16)
        right[pl.ds(quarter, quarter), lanes] = second.astype(BF16)
    for copy in copies:
        copy.wait()
    for m in range(left.shape[0] // TILE):
        part = dot(left[pl.ds(m * TILE, TILE), :], right[...], NT).astype(BF16)
        for i in range(4):
            at_chunk = m * 4 + i
            out[at_chunk // 8, at_chunk // 2 % 4, at_chunk % 2, pl.ds(0, 64), :] = part[i * 64 : i * 64 + 64]


def gradient(sel, firsts, seconds, nl, gg, nl_peer, gg_peer, pieces):
    rows = firsts[0].shape[1]
    cols = 2 * (pieces[0].shape[0] - 16)
    return pl.pallas_call(
        gradient_kernel,
        out_shape=jax.ShapeDtypeStruct((2, 4, 2, 128, cols), BF16),
        in_specs=[SM] + [VM] * 12 + [HB] * 8,
        out_specs=VM,
        scratch_shapes=[
            pltpu.VMEM((rows, 2048), BF16),
            pltpu.VMEM((cols, 2048), BF16),
            pltpu.SemaphoreType.DMA((16,)),
        ],
        compiler_params=pltpu.CompilerParams(vmem_limit_bytes=32 << 20),
        name="gradient",
    )(sel, pinned(nl), pinned(gg), nl_peer, gg_peer, *pieces, *[in_hbm(a) for a in (*firsts, *seconds)])


def at(array, index):
    return lax.dynamic_index_in_dim(array, index, 0, keepdims=False)


def move(array, dy=0, dz=0, flip=0):
    pairs = []
    for x in range(4):
        for y in range(4):
            for z in range(4):
                for core in range(2):
                    to_y, to_z = (y + dy) % 4, (z + dz) % 4
                    src = (x * 2 + y // 2) * 16 + y % 2 * 8 + z * 2 + core
                    dst = (x * 2 + to_y // 2) * 16 + to_y % 2 * 8 + to_z * 2 + (core ^ flip)
                    pairs.append((src, dst))
    return lax.ppermute(array, ("pipe", "dp"), pairs)


def sum_dp(buf, r):
    core, z, y = r % 2, (r // 2) % 4, r // 8
    got = lax.ppermute(at(buf, 1 - core), "dp", [(i, i ^ 1) for i in range(16)])
    buf = (at(buf, core).astype(F32) + got.astype(F32)).astype(BF16)
    total = at(buf, z).astype(F32)
    for d in range(1, 4):
        pairs = [(i, i // 8 * 8 + (i + 2 * d) % 8) for i in range(16)]
        total = total + lax.ppermute(at(buf, (z + d) % 4), "dp", pairs).astype(F32)
    buf = total.astype(BF16)
    got = lax.ppermute(at(buf, 1 - y), "dp", [(i, i ^ 8) for i in range(16)])
    return at(buf, y).astype(F32) + got.astype(F32)


def shards(stored, common, down, up, selection, final_c):
    n_pipe, n_dp = lax.axis_size("pipe"), lax.axis_size("dp")
    together = lax.optimization_barrier
    p = lax.axis_index("pipe")
    r = lax.axis_index("dp")
    x_at, h, core = p // 2, p % 2, r % 2
    swap = [(i, i ^ 1) for i in range(n_pipe)]
    turns = [[(i, (i + 2 * d) % n_pipe) for i in range(n_pipe)] for d in range(4)]
    own = stored[0]
    rows, width = own.shape
    half = rows // 2
    a_own, u_own = down[0], up[0]
    rank = a_own.shape[-1]

    def swapped(array):
        return lax.ppermute(array, "pipe", swap)

    def onward(array):
        return lax.ppermute(array, "pipe", turns[1])

    def flip(array):
        return move(array, flip=1)

    mixed = common.transpose(1, 0, 2)
    x_mine = lax.dynamic_slice_in_dim(own, h * half, half, 0)
    x_other = lax.dynamic_slice_in_dim(own, (1 - h) * half, half, 0)
    c = lax.dynamic_slice_in_dim(final_c, h * half, half, 0)
    x_peer = swapped(x_other)
    sel_peer = swapped(selection)
    up_z, down_z = move(mixed, dz=1), move(mixed, dz=-1)
    y_a, y_b = move(mixed[0], dy=1), move(mixed[1], dy=-1)
    near = move(jnp.where(core == 0, a_own, u_own), dy=2)
    sel = jnp.concatenate([selection, sel_peer, jnp.stack([h, r, x_at, x_at]).astype(jnp.int32).reshape(2, 2)])
    up_z, down_z, y_a, y_b, near, x_peer, sel, c, x_mine = together(
        (up_z, down_z, y_a, y_b, near, x_peer, sel, c, x_mine)
    )
    entered = jnp.stack([x_mine, x_peer])
    yz_a, yz_b = move(up_z, dy=1), move(down_z, dy=-1)
    z_a, z_b = move(up_z[0], dz=1), move(down_z[1], dz=-1)
    flips = [flip(a) for a in (mixed, up_z, down_z, y_a, y_b, near)]
    first = first_rows(sel, entered)
    first_peer = swapped(first[1])
    yz_a, yz_b, z_a, z_b, flips, first_peer = together((yz_a, yz_b, z_a, z_b, flips, first_peer))
    yf_a, yf_b = move(z_a, dy=1), move(z_b, dy=-1)
    flips += [flip(a) for a in (z_a, z_b, yz_a, yz_b)]
    firsts = [jnp.stack([first[0], first_peer])]
    firsts.append(onward(firsts[0]))
    yf_a, yf_b, flips, firsts = together((yf_a, yf_b, flips, firsts))
    flips += [flip(a) for a in (yf_a, yf_b)]
    flip_of = dict(zip(("mixed", "up", "down", "ya", "yb", "near", "za", "zb", "yza", "yzb", "yfa", "yfb"), flips))
    pieces = []
    for piece, name in (
        (mixed, "mixed"), (up_z, "up"), (down_z, "down"), (z_a, "za"), (z_b, "zb"), (y_a, "ya"), (y_b, "yb"),
        (yz_a, "yza"), (yz_b, "yzb"), (yf_a, "yfa"), (yf_b, "yfb"),
    ):
        pieces += [piece, flip_of[name]]
    *kept, gg, second = forward(sel, entered, (a_own, u_own, near, flip_of["near"], *pieces))
    nl = kept[0]

    steps = n_pipe // 2
    second_peer = swapped(second[1])
    nl_peer = swapped(nl[1])
    seconds, quarters = [], []

    def pass_quarters(at_place, gg):
        parts = transposed(at_place, sel, gg)
        got = []
        for d in range(1, steps):
            to = (at_place + d) % steps
            pairs = [(2 * at_place + i, 2 * to + i) for i in range(2)]
            got.append(lax.ppermute(parts[to], "pipe", pairs))
        piece = choose(at_place, sel, parts, got)
        return [piece, swapped(piece)]

    for t in range(steps):
        place = steps - 1 - t
        gg, send = backward(place, sel, c, kept, gg)
        if place > 0:
            c = lax.ppermute(send, "pipe", [(2 * place + i, 2 * place - 2 + i) for i in range(2)])
        if t == 0:
            c, second_peer = together((c, second_peer))
            seconds.append(jnp.stack([second[0], second_peer]))
            waiting = (onward(seconds[0]), onward(firsts[1]), nl_peer)
        elif t == 1:
            c, waiting, quarters = together((c, waiting, quarters))
            seconds.append(waiting[0])
            firsts.append(waiting[1])
            nl_peer = waiting[2]
            waiting = (onward(seconds[1]), onward(firsts[2]))
        elif t == 2:
            c, waiting, quarters = together((c, waiting, quarters))
            seconds.append(waiting[0])
            firsts.append(waiting[1])
            seconds.append(onward(seconds[2]))
        quarters = quarters + pass_quarters(place, gg)
    gg, quarters[-2], x_at, r = together((gg, quarters[-2], x_at, r))
    gg_peer = swapped(gg[1, :2])
    quarters = [q for t in range(steps) for q in quarters[2 * (steps - 1 - t) : 2 * (steps - t)]]
    tile = gradient(sel, firsts, seconds, nl, gg, nl_peer, gg_peer, quarters)
    tile, ct = together((tile, gg[:, 2, :, :width]))
    summed = sum_dp(tile, r)
    tile = summed[:64].astype(BF16).reshape(4, 16, -1)
    placed = jnp.stack(
        [at(tile, x_at)]
        + [lax.ppermute(at(tile, (x_at + d) % 4), "pipe", turns[d]) for d in range(1, 4)]
    )
    placed = jnp.stack([at(placed, (x_at - s) % 4) for s in range(4)], axis=1)
    each = width // (n_pipe * n_dp)
    shared = placed[:each].reshape(each, 4, 2, width // 4).transpose(0, 2, 1, 3)
    shared = shared.reshape(each, 2, width).astype(F32)

    ours, theirs = ct[0], swapped(ct[1])
    result = jnp.where(
        h == 0, jnp.concatenate([ours, theirs]), jnp.concatenate([theirs, ours])
    )
    both = summed[64:].reshape(4, 16, 7, rank).transpose(0, 2, 1, 3).reshape(4, 112, rank)
    return result[None], shared, both[None, :2], both[None, 2:]


def solution(mesh):
    return jax.shard_map(
        shards,
        mesh=mesh,
        in_specs=(
            P("pipe", "dp", None),
            P("dp", None, None),
            P("pipe", None, None, None),
            P("pipe", None, None, None),
            P("pipe", None),
            P("dp", None),
        ),
        out_specs=(
            P("pipe", "dp", None),
            P(("pipe", "dp"), None, None),
            P("pipe", None, "dp", None),
            P("pipe", None, "dp", None),
        ),
        check_vma=False,
    )
```

```python
import functools

import jax
import jax.numpy as jnp
from jax import lax
from jax.experimental import pallas as pl
from jax.experimental.pallas import tpu as pltpu
from jax.sharding import PartitionSpec as P

EPS = 1e-06
TILE = 256
F32 = jnp.float32
BF16 = jnp.bfloat16
NT = (((1,), (1,)), ((), ()))
TN = (((0,), (0,)), ((), ()))
HB = pl.BlockSpec(memory_space=pltpu.HBM)
VM = pl.BlockSpec(memory_space=pltpu.VMEM)
SM = pl.BlockSpec(memory_space=pltpu.SMEM)


def dot(a, b, dims=(((1,), (0,)), ((), ()))):
    return lax.dot_general(a, b, dims, preferred_element_type=F32)


def pinned(array):
    return pltpu.with_memory_space_constraint(array, pltpu.VMEM)


def in_hbm(array):
    return pltpu.with_memory_space_constraint(array, pltpu.HBM)


PIECES = ((0, 0, None), (0, 3, None), (0, 1, None), (1, 0, 0), (1, 0, 1), (0, 2, 0), (0, 2, 1)) + (
    (1, 3, None), (1, 1, None), (1, 2, 0), (1, 2, 1)
)


def row_blocks(src, tile, dst, h, lanes):
    width = src.shape[1]
    for t in range(width // TILE):
        tile[pl.ds(t * TILE, TILE), :] = src[:, t * TILE : (t + 1) * TILE].astype(F32).T
    tile[pl.ds(width, 8), :] = jnp.zeros((8, tile.shape[1]), F32)
    for p in range(8):
        x, half = p // 2, p % 2
        slot = jnp.bitwise_xor(h, half)
        for r in range(16):
            core, z, y = r % 2, (r // 2) % 4, r // 8
            at_row = (((core * 4 + z) * 2 + y) * 4 + x) * 16
            dst[slot, pl.ds(at_row, 16), lanes] = tile[pl.ds((p * 16 + r) * 14, 16), :].astype(BF16)


def first_kernel(sel, x, out, tile):
    rows = jnp.concatenate([x[0], x[1]], axis=0).astype(F32)
    sc = lax.rsqrt(jnp.mean(rows * rows, axis=-1, keepdims=True) + EPS)
    row_blocks((rows * sc).astype(BF16), tile, out, sel[2, 0], pl.ds(0, 128))


def first_rows(sel, x):
    width = x.shape[-1]
    return pl.pallas_call(
        first_kernel,
        out_shape=jax.ShapeDtypeStruct((2, 1024, 128), BF16),
        in_specs=[SM, VM],
        out_specs=VM,
        scratch_shapes=[pltpu.VMEM((width + 8, 128), F32)],
        compiler_params=pltpu.CompilerParams(vmem_limit_bytes=16 << 20),
        name="first_rows",
    )(sel, x)


def forward_kernel(sel, x, *refs):
    a_own, u_own, near, far = refs[:4]
    pieces = refs[4 : 4 + 2 * len(PIECES)]
    nl, slope, scale, wt, auv, gg, out, wv, xs, tile, sems = refs[4 + 2 * len(PIECES) :]
    av, uv = auv.at[0], auv.at[1]
    width = x.shape[-1]
    per = pieces[0].shape[-2]
    h, r = sel[2, 0], sel[2, 1]
    core, z, y = r % 2, (r // 2) % 4, r // 8
    small = []
    for i, (src, dst) in enumerate(
        ((a_own, av.at[0]), (u_own, uv.at[0]), (near, auv.at[core, 1]), (far, auv.at[1 - core, 1]))
    ):
        small.append(pltpu.make_async_copy(src, dst, sems.at[32 + i]))
    for copy in small:
        copy.start()
    for block in range(2):
        for i, ref in enumerate(pieces):
            dy, dz, held = PIECES[i // 2]
            if held is not None and held != block:
                continue
            place = jnp.bitwise_xor(y, dy) * 8 + (z + dz) % 4 * 2 + jnp.bitwise_xor(core, i % 2)
            dst = wv.at[block, pl.ds(pl.multiple_of(place * per, 16), per), :]
            src = ref.at[block] if held is None else ref
            pltpu.make_async_copy(src, dst, sems.at[block * 16 + place]).start()
    big = []
    for block in range(2):
        for place in range(16):
            dst = wv.at[block, pl.ds(place * per, per), :]
            big.append(pltpu.make_async_copy(dst, dst, sems.at[block * 16 + place]))
    gg[...] = jnp.zeros_like(gg)
    for o in range(2):
        xs[o] = x[o]
    here = 0
    for block in range(2):
        for t in range(width // TILE):
            while here < 16 * block + min(16, -(-(t + 1) * TILE // per)):
                big[here].wait()
                here += 1
            wt[block, :, pl.ds(t * TILE, TILE)] = wv[block, pl.ds(t * TILE, TILE), :].T
    for copy in small:
        copy.wait()
    for k in range(2):
        rows = jnp.concatenate([xs[0], xs[1]], axis=0).astype(F32)
        sc = lax.rsqrt(jnp.mean(rows * rows, axis=-1, keepdims=True) + EPS)
        nm = (rows * sc).astype(BF16)
        if k == 1:
            row_blocks(nm, tile, out, h, pl.ds(0, 128))
        for o in range(2):
            part = slice(o * 64, (o + 1) * 64)
            scale[o, k] = jnp.broadcast_to(sc[part], scale.shape[2:])
            mine = nm[part]
            nl[o, k, :, pl.ds(0, width)] = mine
            low = dot(mine, av[o, k]).astype(BF16)
            nl[o, k, :, pl.ds(width, 128)] = low
            block = sel[o, k]
            for t in range(width // TILE):
                cols = pl.ds(t * TILE, TILE)
                pre = dot(mine, wv[block, :, cols]) + dot(low, uv[o, k, cols, :], NT)
                sigma = 1.0 / (1.0 + jnp.exp(-pre))
                slope[o, k, :, cols] = sigma * (1.0 + pre * (1.0 - sigma))
                if k == 0:
                    xs[o, :, cols] = (xs[o, :, cols].astype(F32) + pre * sigma).astype(BF16)


def forward(sel, x, weights):
    rows, width = x.shape[1:]
    rank = weights[0].shape[-1]
    return pl.pallas_call(
        forward_kernel,
        out_shape=(
            pltpu.VMEM((2, 2, rows, width + rank), BF16),
            pltpu.VMEM((2, 2, rows, width), F32),
            pltpu.VMEM((2, 2, rows, 128), F32),
            pltpu.VMEM((2, width, width), BF16),
            pltpu.VMEM((2, 2, 2, width, rank), BF16),
            pltpu.VMEM((2, 3, rows, width + rank), BF16),
            jax.ShapeDtypeStruct((2, 1024, 128), BF16),
        ),
        in_specs=[SM, VM] + [HB] * len(weights),
        out_specs=(VM,) * 7,
        scratch_shapes=[
            pltpu.VMEM((2, width, width), BF16),
            pltpu.VMEM((2, rows, width), BF16),
            pltpu.VMEM((width + 8, 128), F32),
            pltpu.SemaphoreType.DMA((36,)),
        ],
        compiler_params=pltpu.CompilerParams(vmem_limit_bytes=28 << 20),
        name="forward",
    )(sel, x, *[in_hbm(w) for w in weights])


def backward_kernel(at_place, sel, c, nl, slope, scale, wt, auv, old_gg, gg, send, gn):
    width = c.shape[-1]
    av, uv = auv.at[0], auv.at[1]

    @pl.when(sel[3, 0] == at_place)
    def _():
        h = sel[2, 0]
        cur = c[...]
        for j in (1, 0):
            o = jnp.bitwise_xor(h, j)
            for k in (1, 0):
                c32 = cur.astype(F32)
                g = (c32 * slope[o, k]).astype(BF16)
                gg[o, k, :, pl.ds(0, width)] = g
                low = dot(g, uv[o, k]).astype(BF16)
                gg[o, k, :, pl.ds(width, 128)] = low
                block = sel[o, k]
                total = jnp.zeros((g.shape[0], 1), F32)
                for t in range(width // TILE):
                    cols = pl.ds(t * TILE, TILE)
                    part = dot(g, wt[block, :, cols]) + dot(low, av[o, k, cols, :], NT)
                    gn[:, cols] = part
                    total = total + jnp.sum(part * nl[o, k, :, cols].astype(F32), axis=-1, keepdims=True)
                mean = total / width
                z = nl[o, k, :, pl.ds(0, width)].astype(F32)
                sc = scale[o, k, :, 0:1]
                cur = (c32 + sc * (gn[...] - z * mean)).astype(BF16)
            gg[o, 2, :, pl.ds(0, width)] = cur
        send[...] = cur


def backward(at_place, sel, c, kept, gg):
    rows, width = c.shape
    kept = [pinned(a) for a in kept]
    return pl.pallas_call(
        functools.partial(backward_kernel, at_place),
        out_shape=(jax.ShapeDtypeStruct(gg.shape, BF16), jax.ShapeDtypeStruct((rows, width), BF16)),
        in_specs=[SM, VM] + [VM] * 6,
        out_specs=(VM, VM),
        scratch_shapes=[pltpu.VMEM((rows, width), F32)],
        input_output_aliases={7: 0},
        compiler_params=pltpu.CompilerParams(vmem_limit_bytes=12 << 20),
        name="backward",
    )(sel, c, *kept, pinned(gg))


def transpose_kernel(places, sel, gp, out):
    quarter = (gp.shape[-1] - 128) // 4

    @pl.when((sel[3, 0] >= places[0]) & (sel[3, 0] <= places[-1]))
    def _():
        for k in range(2):
            lanes = pl.ds(k * 128, 128)
            both = jnp.concatenate([gp[0, k], gp[1, k]], axis=0)[:, : 4 * quarter]
            for q in range(4):
                d = (q + 4 - sel[3, 0]) % 4
                for t in range(0, quarter, 64):
                    out[d, pl.ds(t, 64), lanes] = both[:, q * quarter + t : q * quarter + t + 64].T
            side = lax.broadcasted_iota(jnp.int32, (16, 128), 1) // 64
            mark = jnp.where(side == 0, sel[0, k], sel[1, k])
            for q in range(4):
                out[q, pl.ds(quarter, 16), lanes] = mark.astype(F32).astype(BF16)


def transposed(places, sel, gp):
    quarter = (gp.shape[-1] - 128) // 4
    return pl.pallas_call(
        functools.partial(transpose_kernel, places),
        out_shape=jax.ShapeDtypeStruct((4, quarter + 16, 256), BF16),
        in_specs=[SM, VM],
        out_specs=VM,
        compiler_params=pltpu.CompilerParams(vmem_limit_bytes=12 << 20),
        name="transposed",
    )(sel, pinned(gp))


def choose_kernel(places, sel, quarters, one, two, three, out):
    for i, place in enumerate(places):
        away = (sel[3, 0] + 4 - place) % 4

        @pl.when(away == 0)
        def _(i=i):
            out[i] = quarters[0]

        for d, got in ((1, one), (2, two), (3, three)):

            @pl.when(away == d)
            def _(i=i, got=got):
                out[i] = got[...]


def choose(places, sel, quarters, got):
    return pl.pallas_call(
        functools.partial(choose_kernel, places),
        out_shape=jax.ShapeDtypeStruct((len(places),) + quarters.shape[1:], BF16),
        in_specs=[SM] + [VM] * 4,
        out_specs=VM,
        compiler_params=pltpu.CompilerParams(vmem_limit_bytes=8 << 20),
        name="choose",
    )(sel, quarters, *got)


def gradient_kernel(*refs):
    sel, nl, gg, nl_peer, gg_peer = refs[:5]
    low, low_peer, high, high_peer, firsts = refs[5:10]
    seconds = refs[10:14]
    out, left, right, sems = refs[14:]
    pieces = [ref.at[i] for mine, peer in ((low, low_peer), (high, high_peer)) for i in range(2) for ref in (mine, peer)]
    copies = []
    for d in range(4):
        source = (sel[3, 0] + 4 - d) % 4
        for side in range(2):
            for k, rows in enumerate((firsts.at[source], seconds[d])):
                lanes = pl.ds(pl.multiple_of(source * 512, 128) + (side * 2 + k) * 128, 128)
                copies.append(pltpu.make_async_copy(rows.at[side], left.at[:, lanes], sems.at[len(copies)]))
    for copy in copies:
        copy.start()
    width = nl.shape[-1] - 128
    for k in range(2):
        n = jnp.concatenate([nl[0, k], nl_peer[k]], axis=0)
        g = jnp.concatenate([gg[0, k], gg_peer[k]], axis=0)
        for i, (lhs, rhs) in enumerate(((n, g[:, width:]), (g, n[:, width:]))):
            term = dot(lhs[:, :width], rhs, TN).astype(BF16)
            for r in range(16):
                for t in range(7):
                    out[r % 2, (r // 2) % 4, r // 8, pl.ds(64 + (2 * i + k) * 16, 16), pl.ds(t * 128, 128)] = (
                        term[r * 112 + t * 16 : r * 112 + t * 16 + 16]
                    )
    quarter = low.shape[1] - 16
    for i, piece in enumerate(pieces):
        lanes = pl.ds(i * 256, 256)
        whole = piece[pl.ds(0, quarter), :].astype(F32)
        second = whole * piece[pl.ds(quarter, 16), :][0:1].astype(F32)
        right[pl.ds(0, quarter), lanes] = (whole - second).astype(BF16)
        right[pl.ds(quarter, quarter), lanes] = second.astype(BF16)
    for copy in copies:
        copy.wait()
    for m in range(left.shape[0] // TILE):
        part = dot(left[pl.ds(m * TILE, TILE), :], right[...], NT).astype(BF16)
        for i in range(4):
            at_chunk = m * 4 + i
            out[at_chunk // 8, at_chunk // 2 % 4, at_chunk % 2, pl.ds(0, 64), :] = part[i * 64 : i * 64 + 64]


def gradient(sel, firsts, seconds, nl, gg, nl_peer, gg_peer, pieces):
    rows = firsts.shape[2]
    cols = 2 * (pieces[0].shape[1] - 16)
    return pl.pallas_call(
        gradient_kernel,
        out_shape=jax.ShapeDtypeStruct((2, 4, 2, 128, cols), BF16),
        in_specs=[SM] + [VM] * 8 + [HB] * 5,
        out_specs=VM,
        scratch_shapes=[
            pltpu.VMEM((rows, 2048), BF16),
            pltpu.VMEM((cols, 2048), BF16),
            pltpu.SemaphoreType.DMA((16,)),
        ],
        compiler_params=pltpu.CompilerParams(vmem_limit_bytes=32 << 20),
        name="gradient",
    )(sel, pinned(nl), pinned(gg), nl_peer, gg_peer, *pieces, *[in_hbm(a) for a in (firsts, *seconds)])


def at(array, index):
    return lax.dynamic_index_in_dim(array, index, 0, keepdims=False)


def move(array, dy=0, dz=0, flip=0):
    pairs = []
    for x in range(4):
        for y in range(4):
            for z in range(4):
                for core in range(2):
                    to_y, to_z = (y + dy) % 4, (z + dz) % 4
                    src = (x * 2 + y // 2) * 16 + y % 2 * 8 + z * 2 + core
                    dst = (x * 2 + to_y // 2) * 16 + to_y % 2 * 8 + to_z * 2 + (core ^ flip)
                    pairs.append((src, dst))
    return lax.ppermute(array, ("pipe", "dp"), pairs)


def sum_dp(buf, r):
    core, z, y = r % 2, (r // 2) % 4, r // 8
    got = lax.ppermute(at(buf, 1 - core), "dp", [(i, i ^ 1) for i in range(16)])
    buf = (at(buf, core).astype(F32) + got.astype(F32)).astype(BF16)
    total = at(buf, z).astype(F32)
    for d in range(1, 4):
        pairs = [(i, i // 8 * 8 + (i + 2 * d) % 8) for i in range(16)]
        total = total + lax.ppermute(at(buf, (z + d) % 4), "dp", pairs).astype(F32)
    buf = total.astype(BF16)
    got = lax.ppermute(at(buf, 1 - y), "dp", [(i, i ^ 8) for i in range(16)])
    return at(buf, y).astype(F32) + got.astype(F32)


def shards(stored, common, down, up, selection, final_c):
    n_pipe, n_dp = lax.axis_size("pipe"), lax.axis_size("dp")
    together = lax.optimization_barrier
    p = lax.axis_index("pipe")
    r = lax.axis_index("dp")
    x_at, h, core = p // 2, p % 2, r % 2
    swap = [(i, i ^ 1) for i in range(n_pipe)]
    turns = [[(i, (i + 2 * d) % n_pipe) for i in range(n_pipe)] for d in range(4)]
    own = stored[0]
    rows, width = own.shape
    half = rows // 2
    a_own, u_own = down[0], up[0]
    rank = a_own.shape[-1]

    def swapped(array):
        return lax.ppermute(array, "pipe", swap)

    def onward(array):
        return lax.ppermute(array, "pipe", turns[1])

    def flip(array):
        return move(array, flip=1)

    def after(value, other):
        return together((value, other))[0]

    mixed = common.transpose(1, 0, 2)
    up_z, down_z = move(mixed, dz=1), move(mixed, dz=-1)
    y_a, y_b = move(mixed[0], dy=1), move(mixed[1], dy=-1)
    x_mine = lax.dynamic_slice_in_dim(own, h * half, half, 0)
    x_other = lax.dynamic_slice_in_dim(own, (1 - h) * half, half, 0)
    c = lax.dynamic_slice_in_dim(final_c, h * half, half, 0)
    marks = jnp.broadcast_to(jnp.pad(selection[0], (0, width - 2)).astype(BF16), (16, width))
    x_peer = swapped(jnp.concatenate([x_other, marks]))
    sel_peer = x_peer[half:, :2][:1].astype(F32).astype(jnp.int32)
    sel = jnp.concatenate([selection, sel_peer, jnp.stack([h, r, x_at, x_at]).astype(jnp.int32).reshape(2, 2)])
    entered = jnp.stack([x_mine, x_peer[:half]])
    near = jnp.where(core == 0, a_own, u_own)
    first = first_rows(sel, entered)
    first_peer = swapped(first[1])
    up_z, down_z, y_a, y_b, near, sel, c, entered = together((up_z, down_z, y_a, y_b, near, sel, c, entered))
    yz_a, yz_b = move(up_z, dy=1), move(down_z, dy=-1)
    z_a, z_b = move(up_z[0], dz=1), move(down_z[1], dz=-1)
    flips = [flip(a) for a in (mixed, up_z, down_z, y_a, y_b)]
    yz_a, yz_b, z_a, z_b, flips, first_peer, near = together((yz_a, yz_b, z_a, z_b, flips, first_peer, near))
    firsts = lax.all_gather(
        jnp.stack([first[0], first_peer]), "pipe", axis_index_groups=[[0, 2, 4, 6], [1, 3, 5, 7]]
    )
    near = move(near, dy=2)
    yf_a, yf_b = move(yz_a[0], dz=1), move(yz_b[1], dz=-1)
    flips += [flip(a) for a in (z_a, z_b, yz_a, yz_b)]
    yf_a, yf_b, near, flips = together((yf_a, yf_b, near, flips))
    flips += [flip(a) for a in (yf_a, yf_b, near)]
    direct = (mixed, up_z, down_z, y_a, y_b, z_a, z_b, yz_a, yz_b, yf_a, yf_b)
    pieces = [q for pair in zip(direct, flips) for q in pair]
    entered, firsts = together((entered, firsts))
    *kept, gg, second = forward(sel, entered, (a_own, u_own, near, flips[-1], *pieces))
    nl = kept[0]

    def hop(send, place):
        return lax.ppermute(send, "pipe", [(2 * place + i, 2 * place - 2 + i) for i in range(2)])

    def quarters_of(places, gg):
        parts = transposed(places, sel, gg)
        got = []
        for d in range(1, 4):
            pairs = [(2 * place + i, 2 * ((place + d) % 4) + i) for place in places for i in range(2)]
            got.append(lax.ppermute(parts[d], "pipe", pairs))
        return parts, got

    second_peer = swapped(second[1])
    nl_peer = swapped(nl[1])
    gg, send = backward(3, sel, c, kept, gg)
    c = hop(send, 3)
    second_peer = after(second_peer, gg)
    ring = [jnp.stack([second[0], second_peer])]
    ring.append(onward(ring[0]))
    gg, send = backward(2, sel, c, kept, gg)
    c = hop(send, 2)
    ring[1], nl_peer = after((ring[1], nl_peer), gg)
    ring.append(onward(ring[1]))
    parts, got = quarters_of((2, 3), gg)
    gg, send = backward(1, sel, c, kept, gg)
    c = hop(send, 1)
    got = after(got, gg)
    high = choose((2, 3), sel, parts, got)
    high_peer = swapped(high)
    ring[2] = after(ring[2], gg)
    ring.append(onward(ring[2]))
    gg, _ = backward(0, sel, c, kept, gg)
    high_peer, ring[3] = after((high_peer, ring[3]), gg)
    parts, got = quarters_of((0, 1), gg)
    gg_peer = swapped(after(gg, parts)[1, :2])
    low = choose((0, 1), sel, parts, got)
    low_peer = swapped(low)
    low, x_at, r = together((low, x_at, r))
    pieces = (low, low_peer, high, high_peer)
    tile = gradient(sel, firsts, ring, nl, gg, nl_peer, gg_peer, pieces)
    tile, ct = together((tile, gg[:, 2, :, :width]))
    summed = sum_dp(tile, r)
    tile = summed[:64].astype(BF16).reshape(4, 16, -1)
    placed = jnp.stack(
        [at(tile, x_at)]
        + [lax.ppermute(at(tile, (x_at + d) % 4), "pipe", turns[d]) for d in range(1, 4)]
    )
    placed = jnp.stack([at(placed, (x_at - s) % 4) for s in range(4)], axis=1)
    each = width // (n_pipe * n_dp)
    shared = placed[:each].reshape(each, 4, 2, width // 4).transpose(0, 2, 1, 3)
    shared = shared.reshape(each, 2, width).astype(F32)

    ours, theirs = ct[0], swapped(ct[1])
    result = jnp.where(
        h == 0, jnp.concatenate([ours, theirs]), jnp.concatenate([theirs, ours])
    )
    both = summed[64:].reshape(4, 16, 7, rank).transpose(0, 2, 1, 3).reshape(4, 112, rank)
    return result[None], shared, both[None, :2], both[None, 2:]


def solution(mesh):
    return jax.shard_map(
        shards,
        mesh=mesh,
        in_specs=(
            P("pipe", "dp", None),
            P("dp", None, None),
            P("pipe", None, None, None),
            P("pipe", None, None, None),
            P("pipe", None),
            P("dp", None),
        ),
        out_specs=(
            P("pipe", "dp", None),
            P(("pipe", "dp"), None, None),
            P("pipe", None, "dp", None),
            P("pipe", None, "dp", None),
        ),
        check_vma=False,
    )
```

```python
import functools

import jax
import jax.numpy as jnp
from jax import lax
from jax.experimental import pallas as pl
from jax.experimental.pallas import tpu as pltpu
from jax.sharding import PartitionSpec as P

EPS = 1e-06
TILE = 256
F32 = jnp.float32
BF16 = jnp.bfloat16
NT = (((1,), (1,)), ((), ()))
TN = (((0,), (0,)), ((), ()))
HB = pl.BlockSpec(memory_space=pltpu.HBM)
VM = pl.BlockSpec(memory_space=pltpu.VMEM)
SM = pl.BlockSpec(memory_space=pltpu.SMEM)


def dot(a, b, dims=(((1,), (0,)), ((), ()))):
    return lax.dot_general(a, b, dims, preferred_element_type=F32)


def pinned(array):
    return pltpu.with_memory_space_constraint(array, pltpu.VMEM)


def in_hbm(array):
    return pltpu.with_memory_space_constraint(array, pltpu.HBM)


PIECES = ((0, 0, None), (0, 3, None), (0, 1, None), (1, 0, 0), (1, 0, 1), (0, 2, 0), (0, 2, 1)) + (
    (1, 3, None), (1, 1, None), (1, 2, 0), (1, 2, 1)
)


def row_blocks(src, tile, dst, h, lanes):
    width = src.shape[1]
    for t in range(width // TILE):
        tile[pl.ds(t * TILE, TILE), :] = src[:, t * TILE : (t + 1) * TILE].astype(F32).T
    tile[pl.ds(width, 8), :] = jnp.zeros((8, tile.shape[1]), F32)
    for p in range(8):
        x, half = p // 2, p % 2
        slot = jnp.bitwise_xor(h, half)
        for r in range(16):
            core, z, y = r % 2, (r // 2) % 4, r // 8
            at_row = (((core * 4 + z) * 2 + y) * 4 + x) * 16
            dst[slot, pl.ds(at_row, 16), lanes] = tile[pl.ds((p * 16 + r) * 14, 16), :].astype(BF16)


def first_kernel(sel, x, out, tile):
    rows = jnp.concatenate([x[0], x[1]], axis=0).astype(F32)
    sc = lax.rsqrt(jnp.mean(rows * rows, axis=-1, keepdims=True) + EPS)
    row_blocks((rows * sc).astype(BF16), tile, out, sel[2, 0], pl.ds(0, 128))


def first_rows(sel, x):
    width = x.shape[-1]
    return pl.pallas_call(
        first_kernel,
        out_shape=jax.ShapeDtypeStruct((2, 1024, 128), BF16),
        in_specs=[SM, VM],
        out_specs=VM,
        scratch_shapes=[pltpu.VMEM((width + 8, 128), F32)],
        compiler_params=pltpu.CompilerParams(vmem_limit_bytes=16 << 20),
        name="first_rows",
    )(sel, x)


def forward_kernel(sel, x, *refs):
    a_own, u_own, near, far = refs[:4]
    pieces = refs[4 : 4 + 2 * len(PIECES)]
    nl, slope, scale, wt, auv, gg, out, wv, xs, tile, sems = refs[4 + 2 * len(PIECES) :]
    av, uv = auv.at[0], auv.at[1]
    width = x.shape[-1]
    per = pieces[0].shape[-2]
    h, r = sel[2, 0], sel[2, 1]
    core, z, y = r % 2, (r // 2) % 4, r // 8
    small = []
    for i, (src, dst) in enumerate(
        ((a_own, av.at[0]), (u_own, uv.at[0]), (near, auv.at[core, 1]), (far, auv.at[1 - core, 1]))
    ):
        small.append(pltpu.make_async_copy(src, dst, sems.at[32 + i]))
    for copy in small:
        copy.start()
    for block in range(2):
        for i, ref in enumerate(pieces):
            dy, dz, held = PIECES[i // 2]
            if held is not None and held != block:
                continue
            place = jnp.bitwise_xor(y, dy) * 8 + (z + dz) % 4 * 2 + jnp.bitwise_xor(core, i % 2)
            dst = wv.at[block, pl.ds(pl.multiple_of(place * per, 16), per), :]
            src = ref.at[block] if held is None else ref
            pltpu.make_async_copy(src, dst, sems.at[block * 16 + place]).start()
    big = []
    for block in range(2):
        for place in range(16):
            dst = wv.at[block, pl.ds(place * per, per), :]
            big.append(pltpu.make_async_copy(dst, dst, sems.at[block * 16 + place]))
    gg[...] = jnp.zeros_like(gg)
    for o in range(2):
        xs[o] = x[o]
    here = 0
    for block in range(2):
        for t in range(width // TILE):
            while here < 16 * block + min(16, -(-(t + 1) * TILE // per)):
                big[here].wait()
                here += 1
            wt[block, :, pl.ds(t * TILE, TILE)] = wv[block, pl.ds(t * TILE, TILE), :].T
    for copy in small:
        copy.wait()
    for k in range(2):
        rows = jnp.concatenate([xs[0], xs[1]], axis=0).astype(F32)
        sc = lax.rsqrt(jnp.mean(rows * rows, axis=-1, keepdims=True) + EPS)
        nm = (rows * sc).astype(BF16)
        if k == 1:
            row_blocks(nm, tile, out, h, pl.ds(0, 128))
        for o in range(2):
            part = slice(o * 64, (o + 1) * 64)
            scale[o, k] = jnp.broadcast_to(sc[part], scale.shape[2:])
            mine = nm[part]
            nl[o, k, :, pl.ds(0, width)] = mine
            low = dot(mine, av[o, k]).astype(BF16)
            nl[o, k, :, pl.ds(width, 128)] = low
            if o == 1:
                for t in range(width // 128):
                    out[1, pl.ds(1024 + t * 128 + k * 64, 64), :] = mine[:, t * 128 : t * 128 + 128]
                out[1, pl.ds(1024 + width + k * 64, 64), :] = low
            block = sel[o, k]
            for t in range(width // TILE):
                cols = pl.ds(t * TILE, TILE)
                pre = dot(mine, wv[block, :, cols]) + dot(low, uv[o, k, cols, :], NT)
                sigma = 1.0 / (1.0 + jnp.exp(-pre))
                slope[o, k, :, cols] = sigma * (1.0 + pre * (1.0 - sigma))
                if k == 0:
                    xs[o, :, cols] = (xs[o, :, cols].astype(F32) + pre * sigma).astype(BF16)


def forward(sel, x, weights):
    rows, width = x.shape[1:]
    rank = weights[0].shape[-1]
    return pl.pallas_call(
        forward_kernel,
        out_shape=(
            pltpu.VMEM((2, 2, rows, width + rank), BF16),
            pltpu.VMEM((2, 2, rows, width), F32),
            pltpu.VMEM((2, 2, rows, 128), F32),
            pltpu.VMEM((2, width, width), BF16),
            pltpu.VMEM((2, 2, 2, width, rank), BF16),
            pltpu.VMEM((2, 3, rows, width + rank), BF16),
            jax.ShapeDtypeStruct((2, 1024 + width + rank, 128), BF16),
        ),
        in_specs=[SM, VM] + [HB] * len(weights),
        out_specs=(VM,) * 7,
        scratch_shapes=[
            pltpu.VMEM((2, width, width), BF16),
            pltpu.VMEM((2, rows, width), BF16),
            pltpu.VMEM((width + 8, 128), F32),
            pltpu.SemaphoreType.DMA((36,)),
        ],
        compiler_params=pltpu.CompilerParams(vmem_limit_bytes=28 << 20),
        name="forward",
    )(sel, x, *[in_hbm(w) for w in weights])


def backward_kernel(at_place, sel, c, nl, slope, scale, wt, auv, old_gg, gg, send, gn):
    width = c.shape[-1]
    av, uv = auv.at[0], auv.at[1]

    @pl.when(sel[3, 0] == at_place)
    def _():
        h = sel[2, 0]
        cur = c[...]
        for j in (1, 0):
            o = jnp.bitwise_xor(h, j)
            for k in (1, 0):
                c32 = cur.astype(F32)
                g = (c32 * slope[o, k]).astype(BF16)
                gg[o, k, :, pl.ds(0, width)] = g
                low = dot(g, uv[o, k]).astype(BF16)
                gg[o, k, :, pl.ds(width, 128)] = low
                block = sel[o, k]
                total = jnp.zeros((g.shape[0], 1), F32)
                for t in range(width // TILE):
                    cols = pl.ds(t * TILE, TILE)
                    part = dot(g, wt[block, :, cols]) + dot(low, av[o, k, cols, :], NT)
                    gn[:, cols] = part
                    total = total + jnp.sum(part * nl[o, k, :, cols].astype(F32), axis=-1, keepdims=True)
                mean = total / width
                z = nl[o, k, :, pl.ds(0, width)].astype(F32)
                sc = scale[o, k, :, 0:1]
                cur = (c32 + sc * (gn[...] - z * mean)).astype(BF16)
            gg[o, 2, :, pl.ds(0, width)] = cur
        send[...] = cur


def backward(at_place, sel, c, kept, gg):
    rows, width = c.shape
    kept = [pinned(a) for a in kept]
    return pl.pallas_call(
        functools.partial(backward_kernel, at_place),
        out_shape=(jax.ShapeDtypeStruct(gg.shape, BF16), jax.ShapeDtypeStruct((rows, width), BF16)),
        in_specs=[SM, VM] + [VM] * 6,
        out_specs=(VM, VM),
        scratch_shapes=[pltpu.VMEM((rows, width), F32)],
        input_output_aliases={7: 0},
        compiler_params=pltpu.CompilerParams(vmem_limit_bytes=12 << 20),
        name="backward",
    )(sel, c, *kept, pinned(gg))


def transpose_kernel(places, sel, gp, out):
    quarter = (gp.shape[-1] - 128) // 4

    @pl.when((sel[3, 0] >= places[0]) & (sel[3, 0] <= places[-1]))
    def _():
        for k in range(2):
            lanes = pl.ds(k * 128, 128)
            both = jnp.concatenate([gp[0, k], gp[1, k]], axis=0)[:, : 4 * quarter]
            for q in range(4):
                d = (q + 4 - sel[3, 0]) % 4
                for t in range(0, quarter, 64):
                    out[d, pl.ds(t, 64), lanes] = both[:, q * quarter + t : q * quarter + t + 64].T
            side = lax.broadcasted_iota(jnp.int32, (16, 128), 1) // 64
            mark = jnp.where(side == 0, sel[0, k], sel[1, k])
            for q in range(4):
                out[q, pl.ds(quarter, 16), lanes] = mark.astype(F32).astype(BF16)


def transposed(places, sel, gp):
    quarter = (gp.shape[-1] - 128) // 4
    return pl.pallas_call(
        functools.partial(transpose_kernel, places),
        out_shape=jax.ShapeDtypeStruct((4, quarter + 16, 256), BF16),
        in_specs=[SM, VM],
        out_specs=VM,
        compiler_params=pltpu.CompilerParams(vmem_limit_bytes=12 << 20),
        name="transposed",
    )(sel, pinned(gp))


def choose_kernel(places, sel, quarters, one, two, three, out):
    for i, place in enumerate(places):
        away = (sel[3, 0] + 4 - place) % 4

        @pl.when(away == 0)
        def _(i=i):
            out[i] = quarters[0]

        for d, got in ((1, one), (2, two), (3, three)):

            @pl.when(away == d)
            def _(i=i, got=got):
                out[i] = got[...]


def choose(places, sel, quarters, got):
    return pl.pallas_call(
        functools.partial(choose_kernel, places),
        out_shape=jax.ShapeDtypeStruct((len(places),) + quarters.shape[1:], BF16),
        in_specs=[SM] + [VM] * 4,
        out_specs=VM,
        compiler_params=pltpu.CompilerParams(vmem_limit_bytes=8 << 20),
        name="choose",
    )(sel, quarters, *got)


def gradient_kernel(*refs):
    sel, nl, gg, nl_peer, gg_peer = refs[:5]
    low, low_peer, high, high_peer, firsts = refs[5:10]
    seconds = refs[10:14]
    out, left, right, sems = refs[14:]
    pieces = [ref.at[i] for mine, peer in ((low, low_peer), (high, high_peer)) for i in range(2) for ref in (mine, peer)]
    copies = []
    for d in range(4):
        source = (sel[3, 0] + 4 - d) % 4
        for side in range(2):
            for k, rows in enumerate((firsts.at[source], seconds[d])):
                lanes = pl.ds(pl.multiple_of(source * 512, 128) + (side * 2 + k) * 128, 128)
                copies.append(pltpu.make_async_copy(rows.at[side], left.at[:, lanes], sems.at[len(copies)]))
    for copy in copies:
        copy.start()
    width = nl.shape[-1] - 128
    for k in range(2):
        peer = [nl_peer[pl.ds(t * 128 + k * 64, 64), :] for t in range(nl.shape[-1] // 128)]
        n = jnp.concatenate([nl[0, k], jnp.concatenate(peer, axis=1)], axis=0)
        g = jnp.concatenate([gg[0, k], gg_peer[k]], axis=0)
        for i, (lhs, rhs) in enumerate(((n, g[:, width:]), (g, n[:, width:]))):
            term = dot(lhs[:, :width], rhs, TN).astype(BF16)
            for r in range(16):
                for t in range(7):
                    out[r % 2, (r // 2) % 4, r // 8, pl.ds(64 + (2 * i + k) * 16, 16), pl.ds(t * 128, 128)] = (
                        term[r * 112 + t * 16 : r * 112 + t * 16 + 16]
                    )
    quarter = low.shape[1] - 16
    for i, piece in enumerate(pieces):
        lanes = pl.ds(i * 256, 256)
        whole = piece[pl.ds(0, quarter), :].astype(F32)
        second = whole * piece[pl.ds(quarter, 16), :][0:1].astype(F32)
        right[pl.ds(0, quarter), lanes] = (whole - second).astype(BF16)
        right[pl.ds(quarter, quarter), lanes] = second.astype(BF16)
    for copy in copies:
        copy.wait()
    for m in range(left.shape[0] // TILE):
        part = dot(left[pl.ds(m * TILE, TILE), :], right[...], NT).astype(BF16)
        for i in range(4):
            at_chunk = m * 4 + i
            out[at_chunk // 8, at_chunk // 2 % 4, at_chunk % 2, pl.ds(0, 64), :] = part[i * 64 : i * 64 + 64]


def gradient(sel, firsts, seconds, nl, gg, nl_peer, gg_peer, pieces):
    rows = firsts.shape[2]
    cols = 2 * (pieces[0].shape[1] - 16)
    return pl.pallas_call(
        gradient_kernel,
        out_shape=jax.ShapeDtypeStruct((2, 4, 2, 128, cols), BF16),
        in_specs=[SM] + [VM] * 8 + [HB] * 5,
        out_specs=VM,
        scratch_shapes=[
            pltpu.VMEM((rows, 2048), BF16),
            pltpu.VMEM((cols, 2048), BF16),
            pltpu.SemaphoreType.DMA((16,)),
        ],
        compiler_params=pltpu.CompilerParams(vmem_limit_bytes=32 << 20),
        name="gradient",
    )(sel, pinned(nl), pinned(gg), nl_peer, gg_peer, *pieces, *[in_hbm(a) for a in (firsts, *seconds)])


def at(array, index):
    return lax.dynamic_index_in_dim(array, index, 0, keepdims=False)


def move(array, dy=0, dz=0, flip=0):
    pairs = []
    for x in range(4):
        for y in range(4):
            for z in range(4):
                for core in range(2):
                    to_y, to_z = (y + dy) % 4, (z + dz) % 4
                    src = (x * 2 + y // 2) * 16 + y % 2 * 8 + z * 2 + core
                    dst = (x * 2 + to_y // 2) * 16 + to_y % 2 * 8 + to_z * 2 + (core ^ flip)
                    pairs.append((src, dst))
    return lax.ppermute(array, ("pipe", "dp"), pairs)


def sum_dp(buf, r):
    core, z, y = r % 2, (r // 2) % 4, r // 8
    half = buf.shape[3] // 2

    def over_y(part):
        return lax.ppermute(part, "dp", [(i, i ^ 8) for i in range(16)]).astype(F32)

    def over_z(part):
        total = at(part, z).astype(F32)
        for d in range(1, 4):
            pairs = [(i, i // 8 * 8 + (i + 2 * d) % 8) for i in range(16)]
            total = total + lax.ppermute(at(part, (z + d) % 4), "dp", pairs).astype(F32)
        return total

    got = lax.ppermute(at(buf, 1 - core), "dp", [(i, i ^ 1) for i in range(16)])
    buf = (at(buf, core).astype(F32) + got.astype(F32)).astype(BF16)
    first, second = buf[:, :, :half], buf[:, :, half:].transpose(1, 0, 2, 3)
    first = over_z(first).astype(BF16)
    second = (at(second, y).astype(F32) + over_y(at(second, 1 - y))).astype(BF16)
    return at(first, y).astype(F32) + over_y(at(first, 1 - y)), over_z(second)


def shards(stored, common, down, up, selection, final_c):
    n_pipe, n_dp = lax.axis_size("pipe"), lax.axis_size("dp")
    together = lax.optimization_barrier
    p = lax.axis_index("pipe")
    r = lax.axis_index("dp")
    x_at, h, core = p // 2, p % 2, r % 2
    swap = [(i, i ^ 1) for i in range(n_pipe)]
    turns = [[(i, (i + 2 * d) % n_pipe) for i in range(n_pipe)] for d in range(4)]
    own = stored[0]
    rows, width = own.shape
    half = rows // 2
    a_own, u_own = down[0], up[0]
    rank = a_own.shape[-1]

    def swapped(array):
        return lax.ppermute(array, "pipe", swap)

    def onward(array):
        return lax.ppermute(array, "pipe", turns[1])

    def flip(array):
        return move(array, flip=1)

    def after(value, other):
        return together((value, other))[0]

    mixed = common.transpose(1, 0, 2)
    up_z, down_z = move(mixed, dz=1), move(mixed, dz=-1)
    y_a, y_b = move(mixed[0], dy=1), move(mixed[1], dy=-1)
    x_mine = lax.dynamic_slice_in_dim(own, h * half, half, 0)
    x_other = lax.dynamic_slice_in_dim(own, (1 - h) * half, half, 0)
    c = lax.dynamic_slice_in_dim(final_c, h * half, half, 0)
    marks = jnp.broadcast_to(jnp.pad(selection[0], (0, width - 2)).astype(BF16), (16, width))
    x_peer = swapped(jnp.concatenate([x_other, marks]))
    sel_peer = x_peer[half:, :2][:1].astype(F32).astype(jnp.int32)
    sel = jnp.concatenate([selection, sel_peer, jnp.stack([h, r, x_at, x_at]).astype(jnp.int32).reshape(2, 2)])
    entered = jnp.stack([x_mine, x_peer[:half]])
    near = jnp.where(core == 0, a_own, u_own)
    first = first_rows(sel, entered)
    first_peer = swapped(first[1])
    up_z, down_z, y_a, y_b, near, sel, c, entered, first_peer = together(
        (up_z, down_z, y_a, y_b, near, sel, c, entered, first_peer)
    )
    firsts = lax.all_gather(
        jnp.stack([first[0], first_peer]), "pipe", axis_index_groups=[[0, 2, 4, 6], [1, 3, 5, 7]]
    )
    yz_a, yz_b = move(up_z, dy=1), move(down_z, dy=-1)
    z_a, z_b = move(up_z[0], dz=1), move(down_z[1], dz=-1)
    flips = [flip(a) for a in (mixed, up_z, down_z, y_a, y_b)]
    yz_a, yz_b, z_a, z_b, flips, near = together((yz_a, yz_b, z_a, z_b, flips, near))
    near = move(near, dy=2)
    yf_a, yf_b = move(yz_a[0], dz=1), move(yz_b[1], dz=-1)
    flips += [flip(a) for a in (z_a, z_b, yz_a, yz_b)]
    yf_a, yf_b, near, flips = together((yf_a, yf_b, near, flips))
    flips += [flip(a) for a in (yf_a, yf_b, near)]
    direct = (mixed, up_z, down_z, y_a, y_b, z_a, z_b, yz_a, yz_b, yf_a, yf_b)
    pieces = [q for pair in zip(direct, flips) for q in pair]
    entered, firsts = together((entered, firsts))
    *kept, gg, second = forward(sel, entered, (a_own, u_own, near, flips[-1], *pieces))
    nl = kept[0]

    def hop(send, place):
        return lax.ppermute(send, "pipe", [(2 * place + i, 2 * place - 2 + i) for i in range(2)])

    def quarters_of(places, gg):
        parts = transposed(places, sel, gg)
        got = []
        for d in range(1, 4):
            pairs = [(2 * place + i, 2 * ((place + d) % 4) + i) for place in places for i in range(2)]
            got.append(lax.ppermute(parts[d], "pipe", pairs))
        return parts, got

    sent = swapped(second[1])
    gg, send = backward(3, sel, c, kept, gg)
    c = hop(send, 3)
    gg, send = backward(2, sel, c, kept, gg)
    c = hop(send, 2)
    sent, gg, c = together((sent, gg, c))
    second_peer, nl_peer = sent[:1024], sent[1024:]
    ring = [jnp.stack([second[0, :1024], second_peer])]
    ring.append(onward(ring[0]))
    parts, got = quarters_of((2, 3), gg)
    gg, send = backward(1, sel, c, kept, gg)
    c = hop(send, 1)
    got, ring[1] = after((got, ring[1]), gg)
    ring.append(onward(ring[1]))
    high = choose((2, 3), sel, parts, got)
    high_peer = swapped(high)
    c, high = together((c, high))
    gg, _ = backward(0, sel, c, kept, gg)
    high_peer, ring[2] = after((high_peer, ring[2]), gg)
    ring.append(onward(ring[2]))
    parts, got = quarters_of((0, 1), gg)
    gg_peer = swapped(after(gg, parts)[1, :2])
    low = choose((0, 1), sel, parts, got)
    low_peer = swapped(low)
    low, x_at, r = together((low, x_at, r))
    pieces = (low, low_peer, high, high_peer)
    tile = gradient(sel, firsts, ring, nl, gg, nl_peer, gg_peer, pieces)
    tile, ct = together((tile, gg[:, 2, :, :width]))
    tile, terms = sum_dp(tile, r)
    tile = tile.astype(BF16).reshape(4, 16, -1)
    placed = jnp.stack(
        [at(tile, x_at)]
        + [lax.ppermute(at(tile, (x_at + d) % 4), "pipe", turns[d]) for d in range(1, 4)]
    )
    placed = jnp.stack([at(placed, (x_at - s) % 4) for s in range(4)], axis=1)
    each = width // (n_pipe * n_dp)
    shared = placed[:each].reshape(each, 4, 2, width // 4).transpose(0, 2, 1, 3)
    shared = shared.reshape(each, 2, width).astype(F32)

    ours, theirs = ct[0], swapped(ct[1])
    result = jnp.where(
        h == 0, jnp.concatenate([ours, theirs]), jnp.concatenate([theirs, ours])
    )
    both = terms.reshape(4, 16, 7, rank).transpose(0, 2, 1, 3).reshape(4, 112, rank)
    return result[None], shared, both[None, :2], both[None, 2:]


def solution(mesh):
    return jax.shard_map(
        shards,
        mesh=mesh,
        in_specs=(
            P("pipe", "dp", None),
            P("dp", None, None),
            P("pipe", None, None, None),
            P("pipe", None, None, None),
            P("pipe", None),
            P("dp", None),
        ),
        out_specs=(
            P("pipe", "dp", None),
            P(("pipe", "dp"), None, None),
            P("pipe", None, "dp", None),
            P("pipe", None, "dp", None),
        ),
        check_vma=False,
    )
```

```python
import functools

import jax
import jax.numpy as jnp
from jax import lax
from jax.experimental import pallas as pl
from jax.experimental.pallas import tpu as pltpu
from jax.sharding import PartitionSpec as P

EPS = 1e-06
TILE = 256
F32 = jnp.float32
BF16 = jnp.bfloat16
NT = (((1,), (1,)), ((), ()))
TN = (((0,), (0,)), ((), ()))
HB = pl.BlockSpec(memory_space=pltpu.HBM)
VM = pl.BlockSpec(memory_space=pltpu.VMEM)
SM = pl.BlockSpec(memory_space=pltpu.SMEM)


def dot(a, b, dims=(((1,), (0,)), ((), ()))):
    return lax.dot_general(a, b, dims, preferred_element_type=F32)


def cost(flops, bytes_accessed):
    return pl.CostEstimate(flops=int(flops), bytes_accessed=int(bytes_accessed), transcendentals=0)


def pinned(array):
    return pltpu.with_memory_space_constraint(array, pltpu.VMEM)


def in_hbm(array):
    return pltpu.with_memory_space_constraint(array, pltpu.HBM)


PIECES = ((0, 0, None), (0, 3, None), (0, 1, None), (1, 0, 0), (1, 0, 1), (0, 2, 0), (0, 2, 1)) + (
    (1, 3, None), (1, 1, None), (1, 2, 0), (1, 2, 1)
)


def row_blocks(src, tile, dst, h, lanes):
    width = src.shape[1]
    for t in range(width // TILE):
        tile[pl.ds(t * TILE, TILE), :] = src[:, t * TILE : (t + 1) * TILE].astype(F32).T
    tile[pl.ds(width, 8), :] = jnp.zeros((8, tile.shape[1]), F32)
    for p in range(8):
        x, half = p // 2, p % 2
        slot = jnp.bitwise_xor(h, half)
        for r in range(16):
            core, z, y = r % 2, (r // 2) % 4, r // 8
            at_row = (((core * 4 + z) * 2 + y) * 4 + x) * 16
            dst[slot, pl.ds(at_row, 16), lanes] = tile[pl.ds((p * 16 + r) * 14, 16), :].astype(BF16)


def first_kernel(sel, x, out, tile):
    rows = jnp.concatenate([x[0], x[1]], axis=0).astype(F32)
    sc = lax.rsqrt(jnp.mean(rows * rows, axis=-1, keepdims=True) + EPS)
    row_blocks((rows * sc).astype(BF16), tile, out, sel[2, 0], pl.ds(0, 128))


def first_rows(sel, x):
    width = x.shape[-1]
    return pl.pallas_call(
        first_kernel,
        out_shape=jax.ShapeDtypeStruct((2, 1024, 128), BF16),
        in_specs=[SM, VM],
        out_specs=VM,
        scratch_shapes=[pltpu.VMEM((width + 8, 128), F32)],
        compiler_params=pltpu.CompilerParams(vmem_limit_bytes=16 << 20),
        cost_estimate=cost(1e+09, 1e+06),
        name="first_rows",
    )(sel, x)


def forward_kernel(sel, x, *refs):
    a_own, u_own, near, far = refs[:4]
    pieces = refs[4 : 4 + 2 * len(PIECES)]
    nl, slope, scale, wt, auv, gg, out, wv, xs, tile, sems = refs[4 + 2 * len(PIECES) :]
    av, uv = auv.at[0], auv.at[1]
    width = x.shape[-1]
    per = pieces[0].shape[-2]
    h, r = sel[2, 0], sel[2, 1]
    core, z, y = r % 2, (r // 2) % 4, r // 8
    small = []
    for i, (src, dst) in enumerate(
        ((a_own, av.at[0]), (u_own, uv.at[0]), (near, auv.at[core, 1]), (far, auv.at[1 - core, 1]))
    ):
        small.append(pltpu.make_async_copy(src, dst, sems.at[32 + i]))
    for copy in small:
        copy.start()
    for block in range(2):
        for i, ref in enumerate(pieces):
            dy, dz, held = PIECES[i // 2]
            if held is not None and held != block:
                continue
            place = jnp.bitwise_xor(y, dy) * 8 + (z + dz) % 4 * 2 + jnp.bitwise_xor(core, i % 2)
            dst = wv.at[block, pl.ds(pl.multiple_of(place * per, 16), per), :]
            src = ref.at[block] if held is None else ref
            pltpu.make_async_copy(src, dst, sems.at[block * 16 + place]).start()
    big = []
    for block in range(2):
        for place in range(16):
            dst = wv.at[block, pl.ds(place * per, per), :]
            big.append(pltpu.make_async_copy(dst, dst, sems.at[block * 16 + place]))
    gg[...] = jnp.zeros_like(gg)
    for o in range(2):
        xs[o] = x[o]
    here = 0
    for block in range(2):
        for t in range(width // TILE):
            while here < 16 * block + min(16, -(-(t + 1) * TILE // per)):
                big[here].wait()
                here += 1
            wt[block, :, pl.ds(t * TILE, TILE)] = wv[block, pl.ds(t * TILE, TILE), :].T
    for copy in small:
        copy.wait()
    for k in range(2):
        rows = jnp.concatenate([xs[0], xs[1]], axis=0).astype(F32)
        sc = lax.rsqrt(jnp.mean(rows * rows, axis=-1, keepdims=True) + EPS)
        nm = (rows * sc).astype(BF16)
        if k == 1:
            row_blocks(nm, tile, out, h, pl.ds(0, 128))
        for o in range(2):
            part = slice(o * 64, (o + 1) * 64)
            scale[o, k] = jnp.broadcast_to(sc[part], scale.shape[2:])
            mine = nm[part]
            nl[o, k, :, pl.ds(0, width)] = mine
            low = dot(mine, av[o, k]).astype(BF16)
            nl[o, k, :, pl.ds(width, 128)] = low
            if o == 1:
                for t in range(width // 128):
                    out[1, pl.ds(1024 + t * 128 + k * 64, 64), :] = mine[:, t * 128 : t * 128 + 128]
                out[1, pl.ds(1024 + width + k * 64, 64), :] = low
            block = sel[o, k]
            for t in range(width // TILE):
                cols = pl.ds(t * TILE, TILE)
                pre = dot(mine, wv[block, :, cols]) + dot(low, uv[o, k, cols, :], NT)
                sigma = 1.0 / (1.0 + jnp.exp(-pre))
                slope[o, k, :, cols] = sigma * (1.0 + pre * (1.0 - sigma))
                if k == 0:
                    xs[o, :, cols] = (xs[o, :, cols].astype(F32) + pre * sigma).astype(BF16)


def forward(sel, x, weights):
    rows, width = x.shape[1:]
    rank = weights[0].shape[-1]
    return pl.pallas_call(
        forward_kernel,
        out_shape=(
            pltpu.VMEM((2, 2, rows, width + rank), BF16),
            pltpu.VMEM((2, 2, rows, width), F32),
            pltpu.VMEM((2, 2, rows, 128), F32),
            pltpu.VMEM((2, width, width), BF16),
            pltpu.VMEM((2, 2, 2, width, rank), BF16),
            pltpu.VMEM((2, 3, rows, width + rank), BF16),
            jax.ShapeDtypeStruct((2, 1024 + width + rank, 128), BF16),
        ),
        in_specs=[SM, VM] + [HB] * len(weights),
        out_specs=(VM,) * 7,
        scratch_shapes=[
            pltpu.VMEM((2, width, width), BF16),
            pltpu.VMEM((2, rows, width), BF16),
            pltpu.VMEM((width + 8, 128), F32),
            pltpu.SemaphoreType.DMA((36,)),
        ],
        compiler_params=pltpu.CompilerParams(vmem_limit_bytes=28 << 20),
        cost_estimate=cost(1.5e+10, 2e+07),
        name="forward",
    )(sel, x, *[in_hbm(w) for w in weights])


def backward_kernel(at_place, sel, c, nl, slope, scale, wt, auv, old_gg, gg, send, gn):
    width = c.shape[-1]
    av, uv = auv.at[0], auv.at[1]

    @pl.when(sel[3, 0] == at_place)
    def _():
        h = sel[2, 0]
        cur = c[...]
        for j in (1, 0):
            o = jnp.bitwise_xor(h, j)
            for k in (1, 0):
                c32 = cur.astype(F32)
                g = (c32 * slope[o, k]).astype(BF16)
                gg[o, k, :, pl.ds(0, width)] = g
                low = dot(g, uv[o, k]).astype(BF16)
                gg[o, k, :, pl.ds(width, 128)] = low
                block = sel[o, k]
                total = jnp.zeros((g.shape[0], 1), F32)
                for t in range(width // TILE):
                    cols = pl.ds(t * TILE, TILE)
                    part = dot(g, wt[block, :, cols]) + dot(low, av[o, k, cols, :], NT)
                    gn[:, cols] = part
                    total = total + jnp.sum(part * nl[o, k, :, cols].astype(F32), axis=-1, keepdims=True)
                mean = total / width
                z = nl[o, k, :, pl.ds(0, width)].astype(F32)
                sc = scale[o, k, :, 0:1]
                cur = (c32 + sc * (gn[...] - z * mean)).astype(BF16)
            gg[o, 2, :, pl.ds(0, width)] = cur
        send[...] = cur


def backward(at_place, sel, c, kept, gg):
    rows, width = c.shape
    kept = [pinned(a) for a in kept]
    return pl.pallas_call(
        functools.partial(backward_kernel, at_place),
        out_shape=(jax.ShapeDtypeStruct(gg.shape, BF16), jax.ShapeDtypeStruct((rows, width), BF16)),
        in_specs=[SM, VM] + [VM] * 6,
        out_specs=(VM, VM),
        scratch_shapes=[pltpu.VMEM((rows, width), F32)],
        input_output_aliases={7: 0},
        compiler_params=pltpu.CompilerParams(vmem_limit_bytes=12 << 20),
        cost_estimate=cost(9e+09, 2e+07),
        name="backward",
    )(sel, c, *kept, pinned(gg))


def transpose_kernel(places, sel, gp, out):
    quarter = (gp.shape[-1] - 128) // 4

    @pl.when((sel[3, 0] >= places[0]) & (sel[3, 0] <= places[-1]))
    def _():
        for k in range(2):
            lanes = pl.ds(k * 128, 128)
            both = jnp.concatenate([gp[0, k], gp[1, k]], axis=0)[:, : 4 * quarter]
            for q in range(4):
                d = (q + 4 - sel[3, 0]) % 4
                for t in range(0, quarter, 64):
                    out[d, pl.ds(t, 64), lanes] = both[:, q * quarter + t : q * quarter + t + 64].T
            side = lax.broadcasted_iota(jnp.int32, (16, 128), 1) // 64
            mark = jnp.where(side == 0, sel[0, k], sel[1, k])
            for q in range(4):
                out[q, pl.ds(quarter, 16), lanes] = mark.astype(F32).astype(BF16)


def transposed(places, sel, gp):
    quarter = (gp.shape[-1] - 128) // 4
    return pl.pallas_call(
        functools.partial(transpose_kernel, places),
        out_shape=jax.ShapeDtypeStruct((4, quarter + 16, 256), BF16),
        in_specs=[SM, VM],
        out_specs=VM,
        compiler_params=pltpu.CompilerParams(vmem_limit_bytes=12 << 20),
        cost_estimate=cost(1.8e+09, 4e+06),
        name="transposed",
    )(sel, pinned(gp))


def choose_kernel(places, sel, quarters, one, two, three, out):
    for i, place in enumerate(places):
        away = (sel[3, 0] + 4 - place) % 4

        @pl.when(away == 0)
        def _(i=i):
            out[i] = quarters[0]

        for d, got in ((1, one), (2, two), (3, three)):

            @pl.when(away == d)
            def _(i=i, got=got):
                out[i] = got[...]


def choose(places, sel, quarters, got):
    return pl.pallas_call(
        functools.partial(choose_kernel, places),
        out_shape=jax.ShapeDtypeStruct((len(places),) + quarters.shape[1:], BF16),
        in_specs=[SM] + [VM] * 4,
        out_specs=VM,
        compiler_params=pltpu.CompilerParams(vmem_limit_bytes=8 << 20),
        cost_estimate=cost(1e+09, 1e+06),
        name="choose",
    )(sel, quarters, *got)


def gradient_kernel(*refs):
    sel, low, low_peer, high, high_peer, firsts = refs[:6]
    seconds = refs[6:10]
    out, left, right, sems = refs[10:]
    pieces = [ref.at[i] for mine, peer in ((low, low_peer), (high, high_peer)) for i in range(2) for ref in (mine, peer)]
    copies = []
    for d in range(4):
        source = (sel[3, 0] + 4 - d) % 4
        for side in range(2):
            for k, rows in enumerate((firsts.at[source], seconds[d])):
                lanes = pl.ds(pl.multiple_of(source * 512, 128) + (side * 2 + k) * 128, 128)
                copies.append(pltpu.make_async_copy(rows.at[side], left.at[:, lanes], sems.at[len(copies)]))
    for copy in copies:
        copy.start()
    quarter = low.shape[1] - 16
    for i, piece in enumerate(pieces):
        lanes = pl.ds(i * 256, 256)
        whole = piece[pl.ds(0, quarter), :].astype(F32)
        second = whole * piece[pl.ds(quarter, 16), :][0:1].astype(F32)
        right[pl.ds(0, quarter), lanes] = (whole - second).astype(BF16)
        right[pl.ds(quarter, quarter), lanes] = second.astype(BF16)
    for copy in copies:
        copy.wait()
    for m in range(left.shape[0] // TILE):
        part = dot(left[pl.ds(m * TILE, TILE), :], right[...], NT).astype(BF16)
        for i in range(4):
            at_chunk = m * 4 + i
            out[at_chunk // 8, at_chunk // 2 % 4, at_chunk % 2, pl.ds(0, 64), :] = part[i * 64 : i * 64 + 64]


def gradient(sel, firsts, seconds, pieces):
    rows = firsts.shape[2]
    cols = 2 * (pieces[0].shape[1] - 16)
    return pl.pallas_call(
        gradient_kernel,
        out_shape=jax.ShapeDtypeStruct((2, 4, 2, 64, cols), BF16),
        in_specs=[SM] + [VM] * 4 + [HB] * 5,
        out_specs=VM,
        scratch_shapes=[
            pltpu.VMEM((rows, 2048), BF16),
            pltpu.VMEM((cols, 2048), BF16),
            pltpu.SemaphoreType.DMA((16,)),
        ],
        compiler_params=pltpu.CompilerParams(vmem_limit_bytes=32 << 20),
        cost_estimate=cost(9e+09, 2e+07),
        name="gradient",
    )(sel, *pieces, *[in_hbm(a) for a in (firsts, *seconds)])


def adapter_kernel(nl, gg, nl_peer, gg_peer, out):
    width = nl.shape[-1] - 128
    for k in range(2):
        peer = [nl_peer[pl.ds(t * 128 + k * 64, 64), :] for t in range(nl.shape[-1] // 128)]
        n = jnp.concatenate([nl[0, k], jnp.concatenate(peer, axis=1)], axis=0)
        g = jnp.concatenate([gg[0, k], gg_peer[k]], axis=0)
        for i, (lhs, rhs) in enumerate(((n, g[:, width:]), (g, n[:, width:]))):
            term = dot(lhs[:, :width], rhs, TN).astype(BF16)
            rows = pl.ds((2 * i + k) * 16, 16)
            for r in range(16):
                for t in range(7):
                    out[r % 2, r // 8, (r // 2) % 4, rows, pl.ds(t * 128, 128)] = (
                        term[r * 112 + t * 16 : r * 112 + t * 16 + 16]
                    )


def adapter_terms(nl, gg, nl_peer, gg_peer):
    return pl.pallas_call(
        adapter_kernel,
        out_shape=jax.ShapeDtypeStruct((2, 2, 4, 64, 896), BF16),
        in_specs=[VM] * 4,
        out_specs=VM,
        compiler_params=pltpu.CompilerParams(vmem_limit_bytes=16 << 20),
        cost_estimate=cost(2e9, 4e6),
        name="adapter_terms",
    )(pinned(nl), pinned(gg), nl_peer, gg_peer)


def at(array, index):
    return lax.dynamic_index_in_dim(array, index, 0, keepdims=False)


def move(array, dy=0, dz=0, flip=0):
    pairs = []
    for x in range(4):
        for y in range(4):
            for z in range(4):
                for core in range(2):
                    to_y, to_z = (y + dy) % 4, (z + dz) % 4
                    src = (x * 2 + y // 2) * 16 + y % 2 * 8 + z * 2 + core
                    dst = (x * 2 + to_y // 2) * 16 + to_y % 2 * 8 + to_z * 2 + (core ^ flip)
                    pairs.append((src, dst))
    return lax.ppermute(array, ("pipe", "dp"), pairs)


def over_y(part):
    return lax.ppermute(part, "dp", [(i, i ^ 8) for i in range(16)]).astype(F32)


def over_z(part, z):
    total = at(part, z).astype(F32)
    for d in range(1, 4):
        pairs = [(i, i // 8 * 8 + (i + 2 * d) % 8) for i in range(16)]
        total = total + lax.ppermute(at(part, (z + d) % 4), "dp", pairs).astype(F32)
    return total


def over_cores(part, core):
    got = lax.ppermute(at(part, 1 - core), "dp", [(i, i ^ 1) for i in range(16)])
    return (at(part, core).astype(F32) + got.astype(F32)).astype(BF16)


def shards(stored, common, down, up, selection, final_c):
    n_pipe, n_dp = lax.axis_size("pipe"), lax.axis_size("dp")
    together = lax.optimization_barrier
    p = lax.axis_index("pipe")
    r = lax.axis_index("dp")
    x_at, h, core = p // 2, p % 2, r % 2
    swap = [(i, i ^ 1) for i in range(n_pipe)]
    turns = [[(i, (i + 2 * d) % n_pipe) for i in range(n_pipe)] for d in range(4)]
    own = stored[0]
    rows, width = own.shape
    half = rows // 2
    a_own, u_own = down[0], up[0]
    rank = a_own.shape[-1]

    def swapped(array):
        return lax.ppermute(array, "pipe", swap)

    def onward(array):
        return lax.ppermute(array, "pipe", turns[1])

    def flip(array):
        return move(array, flip=1)

    def after(value, other):
        return together((value, other))[0]

    mixed = common.transpose(1, 0, 2)
    up_z, down_z = move(mixed, dz=1), move(mixed, dz=-1)
    y_a, y_b = move(mixed[0], dy=1), move(mixed[1], dy=-1)
    x_mine = lax.dynamic_slice_in_dim(own, h * half, half, 0)
    x_other = lax.dynamic_slice_in_dim(own, (1 - h) * half, half, 0)
    c = lax.dynamic_slice_in_dim(final_c, h * half, half, 0)
    marks = jnp.broadcast_to(jnp.pad(selection[0], (0, width - 2)).astype(BF16), (16, width))
    x_peer = swapped(jnp.concatenate([x_other, marks]))
    sel_peer = x_peer[half:, :2][:1].astype(F32).astype(jnp.int32)
    sel = jnp.concatenate([selection, sel_peer, jnp.stack([h, r, x_at, x_at]).astype(jnp.int32).reshape(2, 2)])
    entered = jnp.stack([x_mine, x_peer[:half]])
    near = jnp.where(core == 0, a_own, u_own)
    first = first_rows(sel, entered)
    first_peer = swapped(first[1])
    up_z, down_z, y_a, y_b, near, sel, c, entered, first_peer = together(
        (up_z, down_z, y_a, y_b, near, sel, c, entered, first_peer)
    )
    firsts = lax.all_gather(
        jnp.stack([first[0], first_peer]), "pipe", axis_index_groups=[[0, 2, 4, 6], [1, 3, 5, 7]]
    )
    yz_a, yz_b = move(up_z, dy=1), move(down_z, dy=-1)
    z_a, z_b = move(up_z[0], dz=1), move(down_z[1], dz=-1)
    yz_a, yz_b, z_a, z_b, near, mixed, up_z, down_z, y_a, y_b = together(
        (yz_a, yz_b, z_a, z_b, near, mixed, up_z, down_z, y_a, y_b)
    )
    near = move(near, dy=2)
    yf_a, yf_b = move(yz_a[0], dz=1), move(yz_b[1], dz=-1)
    flips = [flip(a) for a in (mixed, up_z, down_z, y_a, y_b, z_a, z_b, yz_a, yz_b)]
    yf_a, yf_b, near, flips = together((yf_a, yf_b, near, flips))
    flips += [flip(a) for a in (yf_a, yf_b, near)]
    direct = (mixed, up_z, down_z, y_a, y_b, z_a, z_b, yz_a, yz_b, yf_a, yf_b)
    pieces = [q for pair in zip(direct, flips) for q in pair]
    entered, firsts = together((entered, firsts))
    *kept, gg, second = forward(sel, entered, (a_own, u_own, near, flips[-1], *pieces))
    nl = kept[0]

    def hop(send, place):
        return lax.ppermute(send, "pipe", [(2 * place + i, 2 * place - 2 + i) for i in range(2)])

    def quarters_of(places, gg):
        parts = transposed(places, sel, gg)
        got = []
        for d in range(1, 4):
            pairs = [(2 * place + i, 2 * ((place + d) % 4) + i) for place in places for i in range(2)]
            got.append(lax.ppermute(parts[d], "pipe", pairs))
        return parts, got

    sent = swapped(second[1])
    gg, send = backward(3, sel, c, kept, gg)
    c = hop(send, 3)
    gg, send = backward(2, sel, c, kept, gg)
    c = hop(send, 2)
    sent, gg, c = together((sent, gg, c))
    second_peer, nl_peer = sent[:1024], sent[1024:]
    ring = [jnp.stack([second[0, :1024], second_peer])]
    ring.append(onward(ring[0]))
    parts, got = quarters_of((2, 3), gg)
    gg, send = backward(1, sel, c, kept, gg)
    c = hop(send, 1)
    got, ring[1] = after((got, ring[1]), gg)
    ring.append(onward(ring[1]))
    high = choose((2, 3), sel, parts, got)
    high_peer = swapped(high)
    c, high = together((c, high))
    gg, _ = backward(0, sel, c, kept, gg)
    high_peer, ring[2] = after((high_peer, ring[2]), gg)
    ring.append(onward(ring[2]))
    parts, got = quarters_of((0, 1), gg)
    gg_peer = swapped(after(gg, parts)[1, :2])
    low = choose((0, 1), sel, parts, got)
    low_peer = swapped(low)
    low, x_at, r = together((low, x_at, r))
    pieces = (low, low_peer, high, high_peer)
    tile = gradient(sel, firsts, ring, pieces)
    core, z, y = r % 2, (r // 2) % 4, r // 8
    gg = after(gg, tile)
    terms = over_cores(adapter_terms(nl, gg, nl_peer, gg_peer), core)
    terms = (at(terms, y).astype(F32) + over_y(at(terms, 1 - y))).astype(BF16)
    terms = over_z(terms, z)
    tile = over_z(over_cores(tile, core), z).astype(BF16)
    tile = at(tile, y).astype(F32) + over_y(at(tile, 1 - y))
    tile = tile.astype(BF16).reshape(4, 16, -1)
    ct = gg[:, 2, :, :width]
    placed = jnp.stack(
        [at(tile, x_at)]
        + [lax.ppermute(at(tile, (x_at + d) % 4), "pipe", turns[d]) for d in range(1, 4)]
    )
    placed = jnp.stack([at(placed, (x_at - s) % 4) for s in range(4)], axis=1)
    each = width // (n_pipe * n_dp)
    shared = placed[:each].reshape(each, 4, 2, width // 4).transpose(0, 2, 1, 3)
    shared = shared.reshape(each, 2, width).astype(F32)

    ours, theirs = ct[0], swapped(ct[1])
    result = jnp.where(
        h == 0, jnp.concatenate([ours, theirs]), jnp.concatenate([theirs, ours])
    )
    both = terms.reshape(4, 16, 7, rank).transpose(0, 2, 1, 3).reshape(4, 112, rank)
    return result[None], shared, both[None, :2], both[None, 2:]


def solution(mesh):
    return jax.shard_map(
        shards,
        mesh=mesh,
        in_specs=(
            P("pipe", "dp", None),
            P("dp", None, None),
            P("pipe", None, None, None),
            P("pipe", None, None, None),
            P("pipe", None),
            P("dp", None),
        ),
        out_specs=(
            P("pipe", "dp", None),
            P(("pipe", "dp"), None, None),
            P("pipe", None, "dp", None),
            P("pipe", None, "dp", None),
        ),
        check_vma=False,
    )
```

```python
import functools

import jax
import jax.numpy as jnp
from jax import lax
from jax.experimental import pallas as pl
from jax.experimental.pallas import tpu as pltpu
from jax.sharding import PartitionSpec as P

EPS = 1e-06
TILE = 256
F32 = jnp.float32
BF16 = jnp.bfloat16
NT = (((1,), (1,)), ((), ()))
TN = (((0,), (0,)), ((), ()))
HB = pl.BlockSpec(memory_space=pltpu.HBM)
VM = pl.BlockSpec(memory_space=pltpu.VMEM)
SM = pl.BlockSpec(memory_space=pltpu.SMEM)


def dot(a, b, dims=(((1,), (0,)), ((), ()))):
    return lax.dot_general(a, b, dims, preferred_element_type=F32)


def cost(flops, bytes_accessed):
    return pl.CostEstimate(flops=int(flops), bytes_accessed=int(bytes_accessed), transcendentals=0)


def pinned(array):
    return pltpu.with_memory_space_constraint(array, pltpu.VMEM)


def in_hbm(array):
    return pltpu.with_memory_space_constraint(array, pltpu.HBM)


PIECES = ((0, 0, None), (0, 3, None), (0, 1, None), (1, 0, 0), (1, 0, 1), (0, 2, 0), (0, 2, 1)) + (
    (1, 3, None), (1, 1, None), (1, 2, 0), (1, 2, 1)
)


def row_blocks(src, tile, dst, h, lanes):
    width = src.shape[1]
    for t in range(width // TILE):
        tile[pl.ds(t * TILE, TILE), :] = src[:, t * TILE : (t + 1) * TILE].astype(F32).T
    tile[pl.ds(width, 8), :] = jnp.zeros((8, tile.shape[1]), F32)
    for p in range(8):
        x, half = p // 2, p % 2
        slot = jnp.bitwise_xor(h, half)
        for r in range(16):
            core, z, y = r % 2, (r // 2) % 4, r // 8
            at_row = (((core * 4 + z) * 2 + y) * 4 + x) * 16
            dst[slot, pl.ds(at_row, 16), lanes] = tile[pl.ds((p * 16 + r) * 14, 16), :].astype(BF16)


def first_kernel(sel, x, out, tile):
    rows = jnp.concatenate([x[0], x[1]], axis=0).astype(F32)
    sc = lax.rsqrt(jnp.mean(rows * rows, axis=-1, keepdims=True) + EPS)
    row_blocks((rows * sc).astype(BF16), tile, out, sel[2, 0], pl.ds(0, 128))


def first_rows(sel, x):
    width = x.shape[-1]
    return pl.pallas_call(
        first_kernel,
        out_shape=jax.ShapeDtypeStruct((2, 1024, 128), BF16),
        in_specs=[SM, VM],
        out_specs=VM,
        scratch_shapes=[pltpu.VMEM((width + 8, 128), F32)],
        compiler_params=pltpu.CompilerParams(vmem_limit_bytes=16 << 20),
        cost_estimate=cost(1e+09, 1e+06),
        name="first_rows",
    )(sel, x)


def forward_kernel(sel, x, *refs):
    a_own, u_own, near, far = refs[:4]
    pieces = refs[4 : 4 + 2 * len(PIECES)]
    nl, slope, scale, wt, auv, gg, out, wv, xs, tile, sems = refs[4 + 2 * len(PIECES) :]
    av, uv = auv.at[0], auv.at[1]
    width = x.shape[-1]
    per = pieces[0].shape[-2]
    h, r = sel[2, 0], sel[2, 1]
    core, z, y = r % 2, (r // 2) % 4, r // 8
    small = []
    for i, (src, dst) in enumerate(
        ((a_own, av.at[0]), (u_own, uv.at[0]), (near, auv.at[core, 1]), (far, auv.at[1 - core, 1]))
    ):
        small.append(pltpu.make_async_copy(src, dst, sems.at[32 + i]))
    for copy in small:
        copy.start()
    for block in range(2):
        for i, ref in enumerate(pieces):
            dy, dz, held = PIECES[i // 2]
            if held is not None and held != block:
                continue
            place = jnp.bitwise_xor(y, dy) * 8 + (z + dz) % 4 * 2 + jnp.bitwise_xor(core, i % 2)
            dst = wv.at[block, pl.ds(pl.multiple_of(place * per, 16), per), :]
            src = ref.at[block] if held is None else ref
            pltpu.make_async_copy(src, dst, sems.at[block * 16 + place]).start()
    big = []
    for block in range(2):
        for place in range(16):
            dst = wv.at[block, pl.ds(place * per, per), :]
            big.append(pltpu.make_async_copy(dst, dst, sems.at[block * 16 + place]))
    gg[...] = jnp.zeros_like(gg)
    for o in range(2):
        xs[o] = x[o]
    here = 0
    for block in range(2):
        for t in range(width // TILE):
            while here < 16 * block + min(16, -(-(t + 1) * TILE // per)):
                big[here].wait()
                here += 1
            wt[block, :, pl.ds(t * TILE, TILE)] = wv[block, pl.ds(t * TILE, TILE), :].T
    for copy in small:
        copy.wait()
    for k in range(2):
        rows = jnp.concatenate([xs[0], xs[1]], axis=0).astype(F32)
        sc = lax.rsqrt(jnp.mean(rows * rows, axis=-1, keepdims=True) + EPS)
        nm = (rows * sc).astype(BF16)
        if k == 1:
            row_blocks(nm, tile, out, h, pl.ds(0, 128))
        for o in range(2):
            part = slice(o * 64, (o + 1) * 64)
            scale[o, k] = jnp.broadcast_to(sc[part], scale.shape[2:])
            mine = nm[part]
            nl[o, k, :, pl.ds(0, width)] = mine
            low = dot(mine, av[o, k]).astype(BF16)
            nl[o, k, :, pl.ds(width, 128)] = low
            block = sel[o, k]
            for t in range(width // TILE):
                cols = pl.ds(t * TILE, TILE)
                pre = dot(mine, wv[block, :, cols]) + dot(low, uv[o, k, cols, :], NT)
                sigma = 1.0 / (1.0 + jnp.exp(-pre))
                slope[o, k, :, cols] = sigma * (1.0 + pre * (1.0 - sigma))
                if k == 0:
                    xs[o, :, cols] = (xs[o, :, cols].astype(F32) + pre * sigma).astype(BF16)


def forward(sel, x, weights):
    rows, width = x.shape[1:]
    rank = weights[0].shape[-1]
    return pl.pallas_call(
        forward_kernel,
        out_shape=(
            pltpu.VMEM((2, 2, rows, width + rank), BF16),
            pltpu.VMEM((2, 2, rows, width), F32),
            pltpu.VMEM((2, 2, rows, 128), F32),
            pltpu.VMEM((2, width, width), BF16),
            pltpu.VMEM((2, 2, 2, width, rank), BF16),
            pltpu.VMEM((2, 3, rows, width + rank), BF16),
            jax.ShapeDtypeStruct((2, 1024, 128), BF16),
        ),
        in_specs=[SM, VM] + [HB] * len(weights),
        out_specs=(VM,) * 7,
        scratch_shapes=[
            pltpu.VMEM((2, width, width), BF16),
            pltpu.VMEM((2, rows, width), BF16),
            pltpu.VMEM((width + 8, 128), F32),
            pltpu.SemaphoreType.DMA((36,)),
        ],
        compiler_params=pltpu.CompilerParams(vmem_limit_bytes=22 << 20),
        cost_estimate=cost(1.5e+10, 2e+07),
        name="forward",
    )(sel, x, *[in_hbm(w) for w in weights])


def backward_kernel(at_place, sel, c, nl, slope, scale, wt, auv, old_gg, gg, send, gn):
    width = c.shape[-1]
    av, uv = auv.at[0], auv.at[1]

    @pl.when(sel[3, 0] == at_place)
    def _():
        h = sel[2, 0]
        cur = c[...]
        for j in (1, 0):
            o = jnp.bitwise_xor(h, j)
            for k in (1, 0):
                c32 = cur.astype(F32)
                g = (c32 * slope[o, k]).astype(BF16)
                gg[o, k, :, pl.ds(0, width)] = g
                low = dot(g, uv[o, k]).astype(BF16)
                gg[o, k, :, pl.ds(width, 128)] = low
                block = sel[o, k]
                total = jnp.zeros((g.shape[0], 1), F32)
                for t in range(width // TILE):
                    cols = pl.ds(t * TILE, TILE)
                    part = dot(g, wt[block, :, cols]) + dot(low, av[o, k, cols, :], NT)
                    gn[:, cols] = part
                    total = total + jnp.sum(part * nl[o, k, :, cols].astype(F32), axis=-1, keepdims=True)
                mean = total / width
                z = nl[o, k, :, pl.ds(0, width)].astype(F32)
                sc = scale[o, k, :, 0:1]
                cur = (c32 + sc * (gn[...] - z * mean)).astype(BF16)
            gg[o, 2, :, pl.ds(0, width)] = cur
        send[...] = cur


def backward(at_place, sel, c, kept, gg):
    rows, width = c.shape
    kept = [pinned(a) for a in kept]
    return pl.pallas_call(
        functools.partial(backward_kernel, at_place),
        out_shape=(jax.ShapeDtypeStruct(gg.shape, BF16), jax.ShapeDtypeStruct((rows, width), BF16)),
        in_specs=[SM, VM] + [VM] * 6,
        out_specs=(VM, VM),
        scratch_shapes=[pltpu.VMEM((rows, width), F32)],
        input_output_aliases={7: 0},
        compiler_params=pltpu.CompilerParams(vmem_limit_bytes=6 << 20),
        cost_estimate=cost(9e+09, 2e+07),
        name="backward",
    )(sel, c, *kept, pinned(gg))


def transpose_kernel(places, sel, gp, out):
    quarter = (gp.shape[-1] - 128) // 4

    @pl.when((sel[3, 0] >= places[0]) & (sel[3, 0] <= places[-1]))
    def _():
        for k in range(2):
            lanes = pl.ds(k * 128, 128)
            both = jnp.concatenate([gp[0, k], gp[1, k]], axis=0)[:, : 4 * quarter]
            for q in range(4):
                d = (q + 4 - sel[3, 0]) % 4
                for t in range(0, quarter, 64):
                    out[d, pl.ds(t, 64), lanes] = both[:, q * quarter + t : q * quarter + t + 64].T
            side = lax.broadcasted_iota(jnp.int32, (16, 128), 1) // 64
            mark = jnp.where(side == 0, sel[0, k], sel[1, k])
            for q in range(4):
                out[q, pl.ds(quarter, 16), lanes] = mark.astype(F32).astype(BF16)


def transposed(places, sel, gp):
    quarter = (gp.shape[-1] - 128) // 4
    return pl.pallas_call(
        functools.partial(transpose_kernel, places),
        out_shape=jax.ShapeDtypeStruct((4, quarter + 16, 256), BF16),
        in_specs=[SM, VM],
        out_specs=VM,
        compiler_params=pltpu.CompilerParams(vmem_limit_bytes=6 << 20),
        cost_estimate=cost(1.8e+09, 4e+06),
        name="transposed",
    )(sel, pinned(gp))


def choose_kernel(places, sel, quarters, one, two, three, out):
    for i, place in enumerate(places):
        away = (sel[3, 0] + 4 - place) % 4

        @pl.when(away == 0)
        def _(i=i):
            out[i] = quarters[0]

        for d, got in ((1, one), (2, two), (3, three)):

            @pl.when(away == d)
            def _(i=i, got=got):
                out[i] = got[...]


def choose(places, sel, quarters, got):
    return pl.pallas_call(
        functools.partial(choose_kernel, places),
        out_shape=jax.ShapeDtypeStruct((len(places),) + quarters.shape[1:], BF16),
        in_specs=[SM] + [VM] * 4,
        out_specs=VM,
        compiler_params=pltpu.CompilerParams(vmem_limit_bytes=8 << 20),
        cost_estimate=cost(1e+09, 1e+06),
        name="choose",
    )(sel, quarters, *got)


def gradient_kernel(*refs):
    sel, low, low_peer, high, high_peer, firsts = refs[:6]
    seconds = refs[6:10]
    out, left, right, sems = refs[10:]
    pieces = [ref.at[i] for mine, peer in ((low, low_peer), (high, high_peer)) for i in range(2) for ref in (mine, peer)]
    copies = []
    for d in range(4):
        source = (sel[3, 0] + 4 - d) % 4
        for side in range(2):
            for k, rows in enumerate((firsts.at[source], seconds[d])):
                lanes = pl.ds(pl.multiple_of(source * 512, 128) + (side * 2 + k) * 128, 128)
                copies.append(pltpu.make_async_copy(rows.at[side], left.at[:, lanes], sems.at[len(copies)]))
    for copy in copies:
        copy.start()
    quarter = low.shape[1] - 16
    for i, piece in enumerate(pieces):
        lanes = pl.ds(i * 256, 256)
        whole = piece[pl.ds(0, quarter), :].astype(F32)
        second = whole * piece[pl.ds(quarter, 16), :][0:1].astype(F32)
        right[pl.ds(0, quarter), lanes] = (whole - second).astype(BF16)
        right[pl.ds(quarter, quarter), lanes] = second.astype(BF16)
    for copy in copies:
        copy.wait()
    for m in range(left.shape[0] // TILE):
        part = dot(left[pl.ds(m * TILE, TILE), :], right[...], NT).astype(BF16)
        for i in range(4):
            at_chunk = m * 4 + i
            out[at_chunk // 8, at_chunk // 2 % 4, at_chunk % 2, pl.ds(0, 64), :] = part[i * 64 : i * 64 + 64]


def gradient(sel, firsts, seconds, pieces):
    rows = firsts.shape[2]
    cols = 2 * (pieces[0].shape[1] - 16)
    return pl.pallas_call(
        gradient_kernel,
        out_shape=jax.ShapeDtypeStruct((2, 4, 2, 64, cols), BF16),
        in_specs=[SM] + [VM] * 4 + [HB] * 5,
        out_specs=VM,
        scratch_shapes=[
            pltpu.VMEM((rows, 2048), BF16),
            pltpu.VMEM((cols, 2048), BF16),
            pltpu.SemaphoreType.DMA((16,)),
        ],
        compiler_params=pltpu.CompilerParams(vmem_limit_bytes=20 << 20),
        cost_estimate=cost(9e+09, 2e+07),
        name="gradient",
    )(sel, *pieces, *[in_hbm(a) for a in (firsts, *seconds)])


def adapter_kernel(nl, gg, nl_peer, gg_peer, out):
    width = nl.shape[-1] - 128
    for k in range(2):
        n = jnp.concatenate([nl[0, k], nl_peer[k]], axis=0)
        g = jnp.concatenate([gg[0, k], gg_peer[k]], axis=0)
        for i, (lhs, rhs) in enumerate(((n, g[:, width:]), (g, n[:, width:]))):
            term = dot(lhs[:, :width], rhs, TN).astype(BF16)
            rows = pl.ds((2 * i + k) * 16, 16)
            for r in range(16):
                for t in range(7):
                    out[r % 2, r // 8, (r // 2) % 4, rows, pl.ds(t * 128, 128)] = (
                        term[r * 112 + t * 16 : r * 112 + t * 16 + 16]
                    )


def adapter_terms(nl, gg, nl_peer, gg_peer):
    return pl.pallas_call(
        adapter_kernel,
        out_shape=jax.ShapeDtypeStruct((2, 2, 4, 64, 896), BF16),
        in_specs=[VM] * 4,
        out_specs=VM,
        compiler_params=pltpu.CompilerParams(vmem_limit_bytes=16 << 20),
        cost_estimate=cost(2e9, 4e6),
        name="adapter_terms",
    )(pinned(nl), pinned(gg), nl_peer, gg_peer)


def at(array, index):
    return lax.dynamic_index_in_dim(array, index, 0, keepdims=False)


def move(array, dy=0, dz=0, flip=0):
    pairs = []
    for x in range(4):
        for y in range(4):
            for z in range(4):
                for core in range(2):
                    to_y, to_z = (y + dy) % 4, (z + dz) % 4
                    src = (x * 2 + y // 2) * 16 + y % 2 * 8 + z * 2 + core
                    dst = (x * 2 + to_y // 2) * 16 + to_y % 2 * 8 + to_z * 2 + (core ^ flip)
                    pairs.append((src, dst))
    return lax.ppermute(array, ("pipe", "dp"), pairs)


def over_y(part):
    return lax.ppermute(part, "dp", [(i, i ^ 8) for i in range(16)]).astype(F32)


def over_z(part, zs):
    total = at(part, zs[0]).astype(F32)
    for d in range(1, 4):
        pairs = [(i, i // 8 * 8 + (i + 2 * d) % 8) for i in range(16)]
        total = total + lax.ppermute(at(part, zs[d]), "dp", pairs).astype(F32)
    return total


def over_cores(part, cores):
    got = lax.ppermute(at(part, cores[1]), "dp", [(i, i ^ 1) for i in range(16)])
    return (at(part, cores[0]).astype(F32) + got.astype(F32)).astype(BF16)


def shards(stored, common, down, up, selection, final_c):
    n_pipe, n_dp = lax.axis_size("pipe"), lax.axis_size("dp")
    together = lax.optimization_barrier
    p = lax.axis_index("pipe")
    r = lax.axis_index("dp")
    x_at, h, core = p // 2, p % 2, r % 2
    swap = [(i, i ^ 1) for i in range(n_pipe)]
    turns = [[(i, (i + 2 * d) % n_pipe) for i in range(n_pipe)] for d in range(4)]
    own = stored[0]
    rows, width = own.shape
    half = rows // 2
    a_own, u_own = down[0], up[0]
    rank = a_own.shape[-1]

    def swapped(array):
        return lax.ppermute(array, "pipe", swap)

    def onward(array):
        return lax.ppermute(array, "pipe", turns[1])

    def flip(array):
        return move(array, flip=1)

    def after(value, other):
        return together((value, other))[0]

    mixed = common.transpose(1, 0, 2)
    up_z, down_z = move(mixed, dz=1), move(mixed, dz=-1)
    y_a, y_b = move(mixed[0], dy=1), move(mixed[1], dy=-1)
    x_mine = lax.dynamic_slice_in_dim(own, h * half, half, 0)
    x_other = lax.dynamic_slice_in_dim(own, (1 - h) * half, half, 0)
    c = lax.dynamic_slice_in_dim(final_c, h * half, half, 0)
    marks = jnp.broadcast_to(jnp.pad(selection[0], (0, width - 2)).astype(BF16), (16, width))
    x_peer = swapped(jnp.concatenate([x_other, marks]))
    sel_peer = x_peer[half:, :2][:1].astype(F32).astype(jnp.int32)
    sel = jnp.concatenate([selection, sel_peer, jnp.stack([h, r, x_at, x_at]).astype(jnp.int32).reshape(2, 2)])
    entered = jnp.stack([x_mine, x_peer[:half]])
    near = jnp.where(core == 0, a_own, u_own)
    first = first_rows(sel, entered)
    first_peer = swapped(first[1])
    up_z, down_z, y_a, y_b, near, sel, c, entered, first_peer = together(
        (up_z, down_z, y_a, y_b, near, sel, c, entered, first_peer)
    )
    firsts = lax.all_gather(
        jnp.stack([first[0], first_peer]), "pipe", axis_index_groups=[[0, 2, 4, 6], [1, 3, 5, 7]]
    )
    yz_a, yz_b = move(up_z, dy=1), move(down_z, dy=-1)
    z_a, z_b = move(up_z[0], dz=1), move(down_z[1], dz=-1)
    early, _ = together(((mixed, up_z, down_z, y_a, y_b), (z_a, z_b)))
    flips = [flip(a) for a in early]
    yz_a, yz_b, z_a, z_b, near, flips = together((yz_a, yz_b, z_a, z_b, near, flips))
    near = move(near, dy=2)
    yf_a, yf_b = move(yz_a[0], dz=1), move(yz_b[1], dz=-1)
    yf_a, yf_b, z_a, z_b, yz_a, yz_b = together((yf_a, yf_b, z_a, z_b, yz_a, yz_b))
    flips += [flip(a) for a in (z_a, z_b, yz_a, yz_b, yf_a, yf_b, near)]
    direct = (mixed, up_z, down_z, y_a, y_b, z_a, z_b, yz_a, yz_b, yf_a, yf_b)
    pieces = [q for pair in zip(direct, flips) for q in pair]
    z, y = (r // 2) % 4, r // 8
    places = ([core, 1 - core], [(z + d) % 4 for d in range(4)], [y, 1 - y])
    places += ([(x_at + d) % 4 for d in range(4)], [(x_at - s) % 4 for s in range(4)])
    entered, firsts, places = together((entered, firsts, places))
    cores, zs, ys, xs, sources = places
    *kept, gg, second = forward(sel, entered, (a_own, u_own, near, flips[-1], *pieces))
    nl = kept[0]

    def hop(send, place):
        return lax.ppermute(send, "pipe", [(2 * place + i, 2 * place - 2 + i) for i in range(2)])

    def quarters_of(places, gg):
        parts = transposed(places, sel, gg)
        got = []
        for d in range(1, 4):
            pairs = [(2 * place + i, 2 * ((place + d) % 4) + i) for place in places for i in range(2)]
            got.append(lax.ppermute(parts[d], "pipe", pairs))
        return parts, got

    second_peer = swapped(second[1])
    gg, send = backward(3, sel, c, kept, gg)
    c = hop(send, 3)
    second_peer, gg = together((second_peer, gg))
    ring = [jnp.stack([second[0], second_peer])]
    ring.append(onward(ring[0]))
    gg, send = backward(2, sel, c, kept, gg)
    c = hop(send, 2)
    ring[1] = after(ring[1], gg)
    ring.append(onward(ring[1]))
    nl_peer = swapped(after(nl, gg)[1])
    gg, c = together((gg, c))
    parts, got = quarters_of((2, 3), gg)
    gg, send = backward(1, sel, c, kept, gg)
    c = hop(send, 1)
    got, ring[2], nl_peer = after((got, ring[2], nl_peer), gg)
    ring.append(onward(ring[2]))
    high = choose((2, 3), sel, parts, got)
    high_peer = swapped(high)
    c, high = together((c, high))
    gg, _ = backward(0, sel, c, kept, gg)
    high_peer, gg = together((high_peer, gg))
    parts, got = quarters_of((0, 1), gg)
    got, ring[3] = together((got, ring[3]))
    low = choose((0, 1), sel, parts, got)
    low_peer = swapped(low)
    gg_peer = swapped(after(gg, low_peer)[1, :2])
    pieces = (low, low_peer, high, high_peer)
    tile = gradient(sel, firsts, ring, pieces)
    gg = after(gg, tile)
    terms = over_cores(adapter_terms(nl, gg, nl_peer, gg_peer), cores)
    terms = (at(terms, ys[0]).astype(F32) + over_y(at(terms, ys[1]))).astype(BF16)
    terms = over_z(terms, zs)
    tile = over_z(over_cores(tile, cores), zs).astype(BF16)
    tile = at(tile, ys[0]).astype(F32) + over_y(at(tile, ys[1]))
    tile = tile.astype(BF16).reshape(4, 16, -1)
    ct = gg[:, 2, :, :width]
    placed = jnp.stack(
        [at(tile, xs[0])] + [lax.ppermute(at(tile, xs[d]), "pipe", turns[d]) for d in range(1, 4)]
    )
    placed = jnp.stack([at(placed, source) for source in sources], axis=1)
    each = width // (n_pipe * n_dp)
    shared = placed[:each].reshape(each, 4, 2, width // 4).transpose(0, 2, 1, 3)
    shared = shared.reshape(each, 2, width).astype(F32)

    ours, theirs = ct[0], swapped(ct[1])
    result = jnp.where(
        h == 0, jnp.concatenate([ours, theirs]), jnp.concatenate([theirs, ours])
    )
    both = terms.reshape(4, 16, 7, rank).transpose(0, 2, 1, 3).reshape(4, 112, rank)
    return result[None], shared, both[None, :2], both[None, 2:]


def solution(mesh):
    return jax.shard_map(
        shards,
        mesh=mesh,
        in_specs=(
            P("pipe", "dp", None),
            P("dp", None, None),
            P("pipe", None, None, None),
            P("pipe", None, None, None),
            P("pipe", None),
            P("dp", None),
        ),
        out_specs=(
            P("pipe", "dp", None),
            P(("pipe", "dp"), None, None),
            P("pipe", None, "dp", None),
            P("pipe", None, "dp", None),
        ),
        check_vma=False,
    )
```

```python
import functools

import jax
import jax.numpy as jnp
from jax import lax
from jax.experimental import pallas as pl
from jax.experimental.pallas import tpu as pltpu
from jax.sharding import PartitionSpec as P

EPS = 1e-06
TILE = 256
F32 = jnp.float32
BF16 = jnp.bfloat16
NT = (((1,), (1,)), ((), ()))
TN = (((0,), (0,)), ((), ()))
HB = pl.BlockSpec(memory_space=pltpu.HBM)
VM = pl.BlockSpec(memory_space=pltpu.VMEM)
SM = pl.BlockSpec(memory_space=pltpu.SMEM)


def dot(a, b, dims=(((1,), (0,)), ((), ()))):
    return lax.dot_general(a, b, dims, preferred_element_type=F32)


def cost(flops, bytes_accessed):
    return pl.CostEstimate(flops=int(flops), bytes_accessed=int(bytes_accessed), transcendentals=0)


def pinned(array):
    return pltpu.with_memory_space_constraint(array, pltpu.VMEM)


def in_hbm(array):
    return pltpu.with_memory_space_constraint(array, pltpu.HBM)


PIECES = ((0, 0, None), (0, 3, None), (0, 1, None), (1, 0, 0), (1, 0, 1), (0, 2, 0), (0, 2, 1)) + (
    (1, 3, None), (1, 1, None), (1, 2, 0), (1, 2, 1)
)


def row_blocks(src, tile, dst, h, lanes):
    width = src.shape[1]
    for t in range(width // TILE):
        tile[pl.ds(t * TILE, TILE), :] = src[:, t * TILE : (t + 1) * TILE].astype(F32).T
    tile[pl.ds(width, 8), :] = jnp.zeros((8, tile.shape[1]), F32)
    for p in range(8):
        x, half = p // 2, p % 2
        slot = jnp.bitwise_xor(h, half)
        for r in range(16):
            core, z, y = r % 2, (r // 2) % 4, r // 8
            at_row = (((core * 4 + z) * 2 + y) * 4 + x) * 16
            dst[slot, pl.ds(at_row, 16), lanes] = tile[pl.ds((p * 16 + r) * 14, 16), :].astype(BF16)


def first_kernel(sel, x, out, tile):
    rows = jnp.concatenate([x[0], x[1]], axis=0).astype(F32)
    sc = lax.rsqrt(jnp.mean(rows * rows, axis=-1, keepdims=True) + EPS)
    row_blocks((rows * sc).astype(BF16), tile, out, sel[2, 0], pl.ds(0, 128))


def first_rows(sel, x):
    width = x.shape[-1]
    return pl.pallas_call(
        first_kernel,
        out_shape=jax.ShapeDtypeStruct((2, 1024, 128), BF16),
        in_specs=[SM, VM],
        out_specs=VM,
        scratch_shapes=[pltpu.VMEM((width + 8, 128), F32)],
        compiler_params=pltpu.CompilerParams(vmem_limit_bytes=16 << 20),
        cost_estimate=cost(1e+09, 1e+06),
        name="first_rows",
    )(sel, x)


def forward_kernel(sel, x, *refs):
    a_own, u_own, near, far = refs[:4]
    pieces = refs[4 : 4 + 2 * len(PIECES)]
    nl, slope, scale, wt, auv, gg, out, wv, xs, tile, sems = refs[4 + 2 * len(PIECES) :]
    av, uv = auv.at[0], auv.at[1]
    width = x.shape[-1]
    per = pieces[0].shape[-2]
    h, r = sel[2, 0], sel[2, 1]
    core, z, y = r % 2, (r // 2) % 4, r // 8
    small = []
    for i, (src, dst) in enumerate(
        ((a_own, av.at[0]), (u_own, uv.at[0]), (near, auv.at[core, 1]), (far, auv.at[1 - core, 1]))
    ):
        small.append(pltpu.make_async_copy(src, dst, sems.at[32 + i]))
    for copy in small:
        copy.start()
    for block in range(2):
        for i, ref in enumerate(pieces):
            dy, dz, held = PIECES[i // 2]
            if held is not None and held != block:
                continue
            place = jnp.bitwise_xor(y, dy) * 8 + (z + dz) % 4 * 2 + jnp.bitwise_xor(core, i % 2)
            dst = wv.at[block, pl.ds(pl.multiple_of(place * per, 16), per), :]
            src = ref.at[block] if held is None else ref
            pltpu.make_async_copy(src, dst, sems.at[block * 16 + place]).start()
    big = []
    for block in range(2):
        for place in range(16):
            dst = wv.at[block, pl.ds(place * per, per), :]
            big.append(pltpu.make_async_copy(dst, dst, sems.at[block * 16 + place]))
    gg[...] = jnp.zeros_like(gg)
    for o in range(2):
        xs[o] = x[o]
    here = 0
    for block in range(2):
        for t in range(width // TILE):
            while here < 16 * block + min(16, -(-(t + 1) * TILE // per)):
                big[here].wait()
                here += 1
            wt[block, :, pl.ds(t * TILE, TILE)] = wv[block, pl.ds(t * TILE, TILE), :].T
    for copy in small:
        copy.wait()
    for k in range(2):
        rows = jnp.concatenate([xs[0], xs[1]], axis=0).astype(F32)
        sc = lax.rsqrt(jnp.mean(rows * rows, axis=-1, keepdims=True) + EPS)
        nm = (rows * sc).astype(BF16)
        if k == 1:
            row_blocks(nm, tile, out, h, pl.ds(0, 128))
        for o in range(2):
            part = slice(o * 64, (o + 1) * 64)
            scale[o, k] = jnp.broadcast_to(sc[part], scale.shape[2:])
            mine = nm[part]
            nl[o, k, :, pl.ds(0, width)] = mine
            low = dot(mine, av[o, k]).astype(BF16)
            nl[o, k, :, pl.ds(width, 128)] = low
            block = sel[o, k]
            for t in range(width // TILE):
                cols = pl.ds(t * TILE, TILE)
                pre = dot(mine, wv[block, :, cols]) + dot(low, uv[o, k, cols, :], NT)
                sigma = 1.0 / (1.0 + jnp.exp(-pre))
                slope[o, k, :, cols] = sigma * (1.0 + pre * (1.0 - sigma))
                if k == 0:
                    xs[o, :, cols] = (xs[o, :, cols].astype(F32) + pre * sigma).astype(BF16)


def forward(sel, x, weights):
    rows, width = x.shape[1:]
    rank = weights[0].shape[-1]
    return pl.pallas_call(
        forward_kernel,
        out_shape=(
            pltpu.VMEM((2, 2, rows, width + rank), BF16),
            pltpu.VMEM((2, 2, rows, width), F32),
            pltpu.VMEM((2, 2, rows, 128), F32),
            pltpu.VMEM((2, width, width), BF16),
            pltpu.VMEM((2, 2, 2, width, rank), BF16),
            pltpu.VMEM((2, 3, rows, width + rank), BF16),
            jax.ShapeDtypeStruct((2, 1024, 128), BF16),
        ),
        in_specs=[SM, VM] + [HB] * len(weights),
        out_specs=(VM,) * 7,
        scratch_shapes=[
            pltpu.VMEM((2, width, width), BF16),
            pltpu.VMEM((2, rows, width), BF16),
            pltpu.VMEM((width + 8, 128), F32),
            pltpu.SemaphoreType.DMA((36,)),
        ],
        compiler_params=pltpu.CompilerParams(vmem_limit_bytes=22 << 20),
        cost_estimate=cost(1.5e+10, 2e+07),
        name="forward",
    )(sel, x, *[in_hbm(w) for w in weights])


def backward_kernel(at_place, sel, c, nl, slope, scale, wt, auv, old_gg, gg, send, gn):
    width = c.shape[-1]
    av, uv = auv.at[0], auv.at[1]

    @pl.when(sel[3, 0] == at_place)
    def _():
        h = sel[2, 0]
        cur = c[...]
        for j in (1, 0):
            o = jnp.bitwise_xor(h, j)
            for k in (1, 0):
                c32 = cur.astype(F32)
                g = (c32 * slope[o, k]).astype(BF16)
                gg[o, k, :, pl.ds(0, width)] = g
                low = dot(g, uv[o, k]).astype(BF16)
                gg[o, k, :, pl.ds(width, 128)] = low
                block = sel[o, k]
                total = jnp.zeros((g.shape[0], 1), F32)
                for t in range(width // TILE):
                    cols = pl.ds(t * TILE, TILE)
                    part = dot(g, wt[block, :, cols]) + dot(low, av[o, k, cols, :], NT)
                    gn[:, cols] = part
                    total = total + jnp.sum(part * nl[o, k, :, cols].astype(F32), axis=-1, keepdims=True)
                mean = total / width
                z = nl[o, k, :, pl.ds(0, width)].astype(F32)
                sc = scale[o, k, :, 0:1]
                cur = (c32 + sc * (gn[...] - z * mean)).astype(BF16)
            gg[o, 2, :, pl.ds(0, width)] = cur
        send[...] = cur


def backward(at_place, sel, c, kept, gg):
    rows, width = c.shape
    kept = [pinned(a) for a in kept]
    return pl.pallas_call(
        functools.partial(backward_kernel, at_place),
        out_shape=(jax.ShapeDtypeStruct(gg.shape, BF16), jax.ShapeDtypeStruct((rows, width), BF16)),
        in_specs=[SM, VM] + [VM] * 6,
        out_specs=(VM, VM),
        scratch_shapes=[pltpu.VMEM((rows, width), F32)],
        input_output_aliases={7: 0},
        compiler_params=pltpu.CompilerParams(vmem_limit_bytes=6 << 20),
        cost_estimate=cost(9e+09, 2e+07),
        name="backward",
    )(sel, c, *kept, pinned(gg))


def transpose_kernel(places, sel, gp, out):
    quarter = (gp.shape[-1] - 128) // 4

    @pl.when((sel[3, 0] >= places[0]) & (sel[3, 0] <= places[-1]))
    def _():
        for k in range(2):
            lanes = pl.ds(k * 128, 128)
            both = jnp.concatenate([gp[0, k], gp[1, k]], axis=0)[:, : 4 * quarter]
            for q in range(4):
                d = (q + 4 - sel[3, 0]) % 4
                for t in range(0, quarter, 64):
                    out[d, pl.ds(t, 64), lanes] = both[:, q * quarter + t : q * quarter + t + 64].T
            side = lax.broadcasted_iota(jnp.int32, (16, 128), 1) // 64
            mark = jnp.where(side == 0, sel[0, k], sel[1, k])
            for q in range(4):
                out[q, pl.ds(quarter, 16), lanes] = mark.astype(F32).astype(BF16)


def transposed(places, sel, gp):
    quarter = (gp.shape[-1] - 128) // 4
    return pl.pallas_call(
        functools.partial(transpose_kernel, places),
        out_shape=jax.ShapeDtypeStruct((4, quarter + 16, 256), BF16),
        in_specs=[SM, VM],
        out_specs=VM,
        compiler_params=pltpu.CompilerParams(vmem_limit_bytes=6 << 20),
        cost_estimate=cost(1.8e+09, 4e+06),
        name="transposed",
    )(sel, pinned(gp))


def choose_kernel(places, sel, quarters, one, two, three, out):
    for i, place in enumerate(places):
        away = (sel[3, 0] + 4 - place) % 4

        @pl.when(away == 0)
        def _(i=i):
            out[i] = quarters[0]

        for d, got in ((1, one), (2, two), (3, three)):

            @pl.when(away == d)
            def _(i=i, got=got):
                out[i] = got[...]


def choose(places, sel, quarters, got):
    return pl.pallas_call(
        functools.partial(choose_kernel, places),
        out_shape=jax.ShapeDtypeStruct((len(places),) + quarters.shape[1:], BF16),
        in_specs=[SM] + [VM] * 4,
        out_specs=VM,
        compiler_params=pltpu.CompilerParams(vmem_limit_bytes=8 << 20),
        cost_estimate=cost(1e+09, 1e+06),
        name="choose",
    )(sel, quarters, *got)


def gradient_kernel(*refs):
    sel, low, low_peer, high, high_peer, firsts = refs[:6]
    seconds = refs[6:10]
    out, left, right, sems = refs[10:]
    pieces = [ref.at[i] for mine, peer in ((low, low_peer), (high, high_peer)) for i in range(2) for ref in (mine, peer)]
    copies = []
    for d in range(4):
        source = (sel[3, 0] + 4 - d) % 4
        for side in range(2):
            for k, rows in enumerate((firsts.at[source], seconds[d])):
                lanes = pl.ds(pl.multiple_of(source * 512, 128) + (side * 2 + k) * 128, 128)
                copies.append(pltpu.make_async_copy(rows.at[side], left.at[:, lanes], sems.at[len(copies)]))
    for copy in copies:
        copy.start()
    quarter = low.shape[1] - 16
    for i, piece in enumerate(pieces):
        lanes = pl.ds(i * 256, 256)
        whole = piece[pl.ds(0, quarter), :].astype(F32)
        second = whole * piece[pl.ds(quarter, 16), :][0:1].astype(F32)
        right[pl.ds(0, quarter), lanes] = (whole - second).astype(BF16)
        right[pl.ds(quarter, quarter), lanes] = second.astype(BF16)
    for copy in copies:
        copy.wait()
    for m in range(left.shape[0] // TILE):
        part = dot(left[pl.ds(m * TILE, TILE), :], right[...], NT).astype(BF16)
        for i in range(4):
            at_chunk = m * 4 + i
            out[at_chunk // 8, at_chunk // 2 % 4, at_chunk % 2, pl.ds(0, 64), :] = part[i * 64 : i * 64 + 64]


def gradient(sel, firsts, seconds, pieces):
    rows = firsts.shape[2]
    cols = 2 * (pieces[0].shape[1] - 16)
    return pl.pallas_call(
        gradient_kernel,
        out_shape=jax.ShapeDtypeStruct((2, 4, 2, 64, cols), BF16),
        in_specs=[SM] + [VM] * 4 + [HB] * 5,
        out_specs=VM,
        scratch_shapes=[
            pltpu.VMEM((rows, 2048), BF16),
            pltpu.VMEM((cols, 2048), BF16),
            pltpu.SemaphoreType.DMA((16,)),
        ],
        compiler_params=pltpu.CompilerParams(vmem_limit_bytes=20 << 20),
        cost_estimate=cost(9e+09, 2e+07),
        name="gradient",
    )(sel, *pieces, *[in_hbm(a) for a in (firsts, *seconds)])


def adapter_kernel(nl, gg, nl_peer, gg_peer, out):
    width = nl.shape[-1] - 128
    for k in range(2):
        n = jnp.concatenate([nl[0, k], nl_peer[k]], axis=0)
        g = jnp.concatenate([gg[0, k], gg_peer[k]], axis=0)
        for i, (lhs, rhs) in enumerate(((n, g[:, width:]), (g, n[:, width:]))):
            term = dot(lhs[:, :width], rhs, TN).astype(BF16)
            rows = pl.ds((2 * i + k) * 16, 16)
            for r in range(16):
                for t in range(7):
                    out[r % 2, r // 8, (r // 2) % 4, rows, pl.ds(t * 128, 128)] = (
                        term[r * 112 + t * 16 : r * 112 + t * 16 + 16]
                    )


def adapter_terms(nl, gg, nl_peer, gg_peer):
    return pl.pallas_call(
        adapter_kernel,
        out_shape=jax.ShapeDtypeStruct((2, 2, 4, 64, 896), BF16),
        in_specs=[VM] * 4,
        out_specs=VM,
        compiler_params=pltpu.CompilerParams(vmem_limit_bytes=16 << 20),
        cost_estimate=cost(2e9, 4e6),
        name="adapter_terms",
    )(pinned(nl), pinned(gg), nl_peer, gg_peer)


def at(array, index):
    return lax.dynamic_index_in_dim(array, index, 0, keepdims=False)


def move(array, dy=0, dz=0, flip=0):
    pairs = []
    for x in range(4):
        for y in range(4):
            for z in range(4):
                for core in range(2):
                    to_y, to_z = (y + dy) % 4, (z + dz) % 4
                    src = (x * 2 + y // 2) * 16 + y % 2 * 8 + z * 2 + core
                    dst = (x * 2 + to_y // 2) * 16 + to_y % 2 * 8 + to_z * 2 + (core ^ flip)
                    pairs.append((src, dst))
    return lax.ppermute(array, ("pipe", "dp"), pairs)


def over_y(part):
    return lax.ppermute(part, "dp", [(i, i ^ 8) for i in range(16)]).astype(F32)


def over_z(part, zs):
    total = at(part, zs[0]).astype(F32)
    for d in range(1, 4):
        pairs = [(i, i // 8 * 8 + (i + 2 * d) % 8) for i in range(16)]
        total = total + lax.ppermute(at(part, zs[d]), "dp", pairs).astype(F32)
    return total


def over_cores(part, cores):
    got = lax.ppermute(at(part, cores[1]), "dp", [(i, i ^ 1) for i in range(16)])
    return (at(part, cores[0]).astype(F32) + got.astype(F32)).astype(BF16)


def shards(stored, common, down, up, selection, final_c):
    n_pipe, n_dp = lax.axis_size("pipe"), lax.axis_size("dp")
    together = lax.optimization_barrier
    p = lax.axis_index("pipe")
    r = lax.axis_index("dp")
    x_at, h, core = p // 2, p % 2, r % 2
    swap = [(i, i ^ 1) for i in range(n_pipe)]
    turns = [[(i, (i + 2 * d) % n_pipe) for i in range(n_pipe)] for d in range(4)]
    own = stored[0]
    rows, width = own.shape
    half = rows // 2
    a_own, u_own = down[0], up[0]
    rank = a_own.shape[-1]

    def swapped(array):
        return lax.ppermute(array, "pipe", swap)

    def onward(array):
        return lax.ppermute(array, "pipe", turns[1])

    def flip(array):
        return move(array, flip=1)

    def after(value, other):
        return together((value, other))[0]

    mixed = common.transpose(1, 0, 2)
    up_z, down_z = move(mixed, dz=1), move(mixed, dz=-1)
    y_a, y_b = move(mixed[0], dy=1), move(mixed[1], dy=-1)
    x_mine = lax.dynamic_slice_in_dim(own, h * half, half, 0)
    x_other = lax.dynamic_slice_in_dim(own, (1 - h) * half, half, 0)
    c = lax.dynamic_slice_in_dim(final_c, h * half, half, 0)
    marks = jnp.broadcast_to(jnp.pad(selection[0], (0, width - 2)).astype(BF16), (16, width))
    x_peer = swapped(jnp.concatenate([x_other, marks]))
    sel_peer = x_peer[half:, :2][:1].astype(F32).astype(jnp.int32)
    sel = jnp.concatenate([selection, sel_peer, jnp.stack([h, r, x_at, x_at]).astype(jnp.int32).reshape(2, 2)])
    entered = jnp.stack([x_mine, x_peer[:half]])
    near = move(jnp.where(core == 0, a_own, u_own), dy=2)
    first = first_rows(sel, entered)
    first_peer = swapped(first[1])
    up_z, down_z, y_a, y_b, sel, c, entered, first_peer = together(
        (up_z, down_z, y_a, y_b, sel, c, entered, first_peer)
    )
    firsts = lax.all_gather(
        jnp.stack([first[0], first_peer]), "pipe", axis_index_groups=[[0, 2, 4, 6], [1, 3, 5, 7]]
    )
    yz_a, yz_b = move(up_z, dy=1), move(down_z, dy=-1)
    z_a, z_b = move(up_z[0], dz=1), move(down_z[1], dz=-1)
    early = (mixed, up_z, down_z, y_a, y_b)
    yz_a, yz_b, z_a, z_b, early = together((yz_a, yz_b, z_a, z_b, early))
    flips = [flip(a) for a in early]
    yf_a, yf_b = move(yz_a[0], dz=1), move(yz_b[1], dz=-1)
    yf_a, yf_b, z_a, z_b, yz_a, yz_b = together((yf_a, yf_b, z_a, z_b, yz_a, yz_b))
    flips += [flip(a) for a in (z_a, z_b, yz_a, yz_b, yf_a, yf_b, near)]
    direct = (mixed, up_z, down_z, y_a, y_b, z_a, z_b, yz_a, yz_b, yf_a, yf_b)
    pieces = [q for pair in zip(direct, flips) for q in pair]
    z, y = (r // 2) % 4, r // 8
    places = ([core, 1 - core], [(z + d) % 4 for d in range(4)], [y, 1 - y])
    places += ([(x_at + d) % 4 for d in range(4)], [(x_at - s) % 4 for s in range(4)])
    places = [[index.astype(jnp.uint32) for index in group] for group in places]
    entered, firsts, places = together((entered, firsts, places))
    cores, zs, ys, xs, sources = places
    *kept, gg, second = forward(sel, entered, (a_own, u_own, near, flips[-1], *pieces))
    nl = kept[0]

    def hop(send, place):
        return lax.ppermute(send, "pipe", [(2 * place + i, 2 * place - 2 + i) for i in range(2)])

    def quarters_of(places, gg):
        parts = transposed(places, sel, gg)
        got = []
        for d in range(1, 4):
            pairs = [(2 * place + i, 2 * ((place + d) % 4) + i) for place in places for i in range(2)]
            got.append(lax.ppermute(parts[d], "pipe", pairs))
        return parts, got

    second_peer = swapped(second[1])
    gg, send = backward(3, sel, c, kept, gg)
    c = hop(send, 3)
    second_peer, gg = together((second_peer, gg))
    ring = [jnp.stack([second[0], second_peer])]
    ring.append(onward(ring[0]))
    gg, send = backward(2, sel, c, kept, gg)
    c = hop(send, 2)
    ring[1] = after(ring[1], gg)
    ring.append(onward(ring[1]))
    nl_peer = swapped(after(nl, gg)[1])
    gg, c = together((gg, c))
    parts, got = quarters_of((2, 3), gg)
    gg, send = backward(1, sel, c, kept, gg)
    c = hop(send, 1)
    got = [after(a, gg) for a in got]
    ring[2] = after(ring[2], gg)
    nl_peer = after(nl_peer, gg)
    ring.append(onward(ring[2]))
    high = choose((2, 3), sel, parts, got)
    high_peer = swapped(high)
    c, high = together((c, high))
    gg, _ = backward(0, sel, c, kept, gg)
    high_peer, gg = together((high_peer, gg))
    parts, got = quarters_of((0, 1), gg)
    low = choose((0, 1), sel, parts, got)
    low_peer = swapped(low)
    gg_peer = swapped(gg[1, :2])
    pieces = (low, low_peer, high, high_peer)
    tile = gradient(sel, firsts, ring, pieces)
    terms = over_cores(adapter_terms(nl, gg, nl_peer, gg_peer), cores)
    terms = (at(terms, ys[0]).astype(F32) + over_y(at(terms, ys[1]))).astype(BF16)
    terms = over_z(terms, zs)
    tile = over_z(over_cores(tile, cores), zs).astype(BF16)
    tile = at(tile, ys[0]).astype(F32) + over_y(at(tile, ys[1]))
    tile = tile.astype(BF16).reshape(4, 16, -1)
    ct = gg[:, 2, :, :width]
    placed = jnp.stack(
        [at(tile, xs[0])] + [lax.ppermute(at(tile, xs[d]), "pipe", turns[d]) for d in range(1, 4)]
    )
    placed = jnp.stack([at(placed, source) for source in sources], axis=1)
    each = width // (n_pipe * n_dp)
    shared = placed[:each].reshape(each, 4, 2, width // 4).transpose(0, 2, 1, 3)
    shared = shared.reshape(each, 2, width).astype(F32)

    ours, theirs = ct[0], swapped(ct[1])
    result = jnp.where(
        h == 0, jnp.concatenate([ours, theirs]), jnp.concatenate([theirs, ours])
    )
    both = terms.reshape(4, 16, 7, rank).transpose(0, 2, 1, 3).reshape(4, 112, rank)
    return result[None], shared, both[None, :2], both[None, 2:]


def solution(mesh):
    return jax.shard_map(
        shards,
        mesh=mesh,
        in_specs=(
            P("pipe", "dp", None),
            P("dp", None, None),
            P("pipe", None, None, None),
            P("pipe", None, None, None),
            P("pipe", None),
            P("dp", None),
        ),
        out_specs=(
            P("pipe", "dp", None),
            P(("pipe", "dp"), None, None),
            P("pipe", None, "dp", None),
            P("pipe", None, "dp", None),
        ),
        check_vma=False,
    )
```

```python
import functools

import jax
import jax.numpy as jnp
from jax import lax
from jax.experimental import pallas as pl
from jax.experimental.pallas import tpu as pltpu
from jax.sharding import PartitionSpec as P

EPS = 1e-06
TILE = 256
F32 = jnp.float32
BF16 = jnp.bfloat16
NT = (((1,), (1,)), ((), ()))
TN = (((0,), (0,)), ((), ()))
HB = pl.BlockSpec(memory_space=pltpu.HBM)
VM = pl.BlockSpec(memory_space=pltpu.VMEM)
SM = pl.BlockSpec(memory_space=pltpu.SMEM)


def dot(a, b, dims=(((1,), (0,)), ((), ()))):
    return lax.dot_general(a, b, dims, preferred_element_type=F32)


def cost(flops, bytes_accessed):
    return pl.CostEstimate(flops=int(flops), bytes_accessed=int(bytes_accessed), transcendentals=0)


def pinned(array):
    return pltpu.with_memory_space_constraint(array, pltpu.VMEM)


def in_hbm(array):
    return pltpu.with_memory_space_constraint(array, pltpu.HBM)


PIECES = ((0, 0, None), (0, 3, None), (0, 1, None), (1, 0, 0), (1, 0, 1), (0, 2, 0), (0, 2, 1)) + (
    (1, 3, None), (1, 1, None), (1, 2, 0), (1, 2, 1)
)


def row_blocks(src, tile, dst, h, lanes):
    width = src.shape[1]
    for t in range(width // TILE):
        tile[pl.ds(t * TILE, TILE), :] = src[:, t * TILE : (t + 1) * TILE].astype(F32).T
    tile[pl.ds(width, 8), :] = jnp.zeros((8, tile.shape[1]), F32)
    for p in range(8):
        x, half = p // 2, p % 2
        slot = jnp.bitwise_xor(h, half)
        for r in range(16):
            core, z, y = r % 2, (r // 2) % 4, r // 8
            at_row = (((core * 4 + z) * 2 + y) * 4 + x) * 16
            dst[slot, pl.ds(at_row, 16), lanes] = tile[pl.ds((p * 16 + r) * 14, 16), :].astype(BF16)


def first_kernel(sel, x, out, tile):
    rows = jnp.concatenate([x[0], x[1]], axis=0).astype(F32)
    sc = lax.rsqrt(jnp.mean(rows * rows, axis=-1, keepdims=True) + EPS)
    row_blocks((rows * sc).astype(BF16), tile, out, sel[2, 0], pl.ds(0, 128))


def first_rows(sel, x):
    width = x.shape[-1]
    return pl.pallas_call(
        first_kernel,
        out_shape=jax.ShapeDtypeStruct((2, 1024, 128), BF16),
        in_specs=[SM, VM],
        out_specs=VM,
        scratch_shapes=[pltpu.VMEM((width + 8, 128), F32)],
        compiler_params=pltpu.CompilerParams(vmem_limit_bytes=16 << 20),
        cost_estimate=cost(1e+09, 1e+06),
        name="first_rows",
    )(sel, x)


def forward_kernel(sel, x, *refs):
    a_own, u_own, near, far = refs[:4]
    pieces = refs[4 : 4 + 2 * len(PIECES)]
    nl, slope, scale, wt, auv, gg, out, wv, xs, tile, sems = refs[4 + 2 * len(PIECES) :]
    av, uv = auv.at[0], auv.at[1]
    width = x.shape[-1]
    per = pieces[0].shape[-2]
    h, r = sel[2, 0], sel[2, 1]
    core, z, y = r % 2, (r // 2) % 4, r // 8
    small = []
    for i, (src, dst) in enumerate(
        ((a_own, av.at[0]), (u_own, uv.at[0]), (near, auv.at[core, 1]), (far, auv.at[1 - core, 1]))
    ):
        small.append(pltpu.make_async_copy(src, dst, sems.at[32 + i]))
    for copy in small:
        copy.start()
    for block in range(2):
        for i, ref in enumerate(pieces):
            dy, dz, held = PIECES[i // 2]
            if held is not None and held != block:
                continue
            place = jnp.bitwise_xor(y, dy) * 8 + (z + dz) % 4 * 2 + jnp.bitwise_xor(core, i % 2)
            dst = wv.at[block, pl.ds(pl.multiple_of(place * per, 16), per), :]
            src = ref.at[block] if held is None else ref
            pltpu.make_async_copy(src, dst, sems.at[block * 16 + place]).start()
    big = []
    for block in range(2):
        for place in range(16):
            dst = wv.at[block, pl.ds(place * per, per), :]
            big.append(pltpu.make_async_copy(dst, dst, sems.at[block * 16 + place]))
    gg[...] = jnp.zeros_like(gg)
    for o in range(2):
        xs[o] = x[o]
    here = 0
    for block in range(2):
        for t in range(width // TILE):
            while here < 16 * block + min(16, -(-(t + 1) * TILE // per)):
                big[here].wait()
                here += 1
            wt[block, :, pl.ds(t * TILE, TILE)] = wv[block, pl.ds(t * TILE, TILE), :].T
    for copy in small:
        copy.wait()
    for k in range(2):
        rows = jnp.concatenate([xs[0], xs[1]], axis=0).astype(F32)
        sc = lax.rsqrt(jnp.mean(rows * rows, axis=-1, keepdims=True) + EPS)
        nm = (rows * sc).astype(BF16)
        if k == 1:
            row_blocks(nm, tile, out, h, pl.ds(0, 128))
        for o in range(2):
            part = slice(o * 64, (o + 1) * 64)
            scale[o, k] = jnp.broadcast_to(sc[part], scale.shape[2:])
            mine = nm[part]
            nl[o, k, :, pl.ds(0, width)] = mine
            low = dot(mine, av[o, k]).astype(BF16)
            nl[o, k, :, pl.ds(width, 128)] = low
            block = sel[o, k]
            for t in range(width // TILE):
                cols = pl.ds(t * TILE, TILE)
                pre = dot(mine, wv[block, :, cols]) + dot(low, uv[o, k, cols, :], NT)
                sigma = 1.0 / (1.0 + jnp.exp(-pre))
                slope[o, k, :, cols] = sigma * (1.0 + pre * (1.0 - sigma))
                if k == 0:
                    xs[o, :, cols] = (xs[o, :, cols].astype(F32) + pre * sigma).astype(BF16)


def forward(sel, x, weights):
    rows, width = x.shape[1:]
    rank = weights[0].shape[-1]
    return pl.pallas_call(
        forward_kernel,
        out_shape=(
            pltpu.VMEM((2, 2, rows, width + rank), BF16),
            pltpu.VMEM((2, 2, rows, width), F32),
            pltpu.VMEM((2, 2, rows, 128), F32),
            pltpu.VMEM((2, width, width), BF16),
            pltpu.VMEM((2, 2, 2, width, rank), BF16),
            pltpu.VMEM((2, 3, rows, width + rank), BF16),
            jax.ShapeDtypeStruct((2, 1024, 128), BF16),
        ),
        in_specs=[SM, VM] + [HB] * len(weights),
        out_specs=(VM,) * 7,
        scratch_shapes=[
            pltpu.VMEM((2, width, width), BF16),
            pltpu.VMEM((2, rows, width), BF16),
            pltpu.VMEM((width + 8, 128), F32),
            pltpu.SemaphoreType.DMA((36,)),
        ],
        compiler_params=pltpu.CompilerParams(vmem_limit_bytes=22 << 20),
        cost_estimate=cost(1.5e+10, 2e+07),
        name="forward",
    )(sel, x, *[in_hbm(w) for w in weights])


def backward_kernel(at_place, sel, c, nl, slope, scale, wt, auv, old_gg, gg, send, gn):
    width = c.shape[-1]
    av, uv = auv.at[0], auv.at[1]

    @pl.when(sel[3, 0] == at_place)
    def _():
        h = sel[2, 0]
        cur = c[...]
        for j in (1, 0):
            o = jnp.bitwise_xor(h, j)
            for k in (1, 0):
                c32 = cur.astype(F32)
                g = (c32 * slope[o, k]).astype(BF16)
                gg[o, k, :, pl.ds(0, width)] = g
                low = dot(g, uv[o, k]).astype(BF16)
                gg[o, k, :, pl.ds(width, 128)] = low
                block = sel[o, k]
                total = jnp.zeros((g.shape[0], 1), F32)
                for t in range(width // TILE):
                    cols = pl.ds(t * TILE, TILE)
                    part = dot(g, wt[block, :, cols]) + dot(low, av[o, k, cols, :], NT)
                    gn[:, cols] = part
                    total = total + jnp.sum(part * nl[o, k, :, cols].astype(F32), axis=-1, keepdims=True)
                mean = total / width
                z = nl[o, k, :, pl.ds(0, width)].astype(F32)
                sc = scale[o, k, :, 0:1]
                cur = (c32 + sc * (gn[...] - z * mean)).astype(BF16)
            gg[o, 2, :, pl.ds(0, width)] = cur
        send[...] = cur


def backward(at_place, sel, c, kept, gg):
    rows, width = c.shape
    kept = [pinned(a) for a in kept]
    return pl.pallas_call(
        functools.partial(backward_kernel, at_place),
        out_shape=(jax.ShapeDtypeStruct(gg.shape, BF16), jax.ShapeDtypeStruct((rows, width), BF16)),
        in_specs=[SM, VM] + [VM] * 6,
        out_specs=(VM, VM),
        scratch_shapes=[pltpu.VMEM((rows, width), F32)],
        input_output_aliases={7: 0},
        compiler_params=pltpu.CompilerParams(vmem_limit_bytes=6 << 20),
        cost_estimate=cost(9e+09, 2e+07),
        name="backward",
    )(sel, c, *kept, pinned(gg))


def transpose_kernel(places, sel, gp, out):
    quarter = (gp.shape[-1] - 128) // 4

    @pl.when((sel[3, 0] >= places[0]) & (sel[3, 0] <= places[-1]))
    def _():
        for k in range(2):
            lanes = pl.ds(k * 128, 128)
            both = jnp.concatenate([gp[0, k], gp[1, k]], axis=0)[:, : 4 * quarter]
            for q in range(4):
                d = (q + 4 - sel[3, 0]) % 4
                for t in range(0, quarter, 64):
                    out[d, pl.ds(t, 64), lanes] = both[:, q * quarter + t : q * quarter + t + 64].T
            side = lax.broadcasted_iota(jnp.int32, (16, 128), 1) // 64
            mark = jnp.where(side == 0, sel[0, k], sel[1, k])
            for q in range(4):
                out[q, pl.ds(quarter, 16), lanes] = mark.astype(F32).astype(BF16)


def transposed(places, sel, gp):
    quarter = (gp.shape[-1] - 128) // 4
    return pl.pallas_call(
        functools.partial(transpose_kernel, places),
        out_shape=jax.ShapeDtypeStruct((4, quarter + 16, 256), BF16),
        in_specs=[SM, VM],
        out_specs=VM,
        compiler_params=pltpu.CompilerParams(vmem_limit_bytes=6 << 20),
        cost_estimate=cost(1.8e+09, 4e+06),
        name="transposed",
    )(sel, pinned(gp))


def choose_kernel(places, sel, quarters, one, two, three, out):
    for i, place in enumerate(places):
        away = (sel[3, 0] + 4 - place) % 4

        @pl.when(away == 0)
        def _(i=i):
            out[i] = quarters[0]

        for d, got in ((1, one), (2, two), (3, three)):

            @pl.when(away == d)
            def _(i=i, got=got):
                out[i] = got[...]


def choose(places, sel, quarters, got):
    return pl.pallas_call(
        functools.partial(choose_kernel, places),
        out_shape=jax.ShapeDtypeStruct((len(places),) + quarters.shape[1:], BF16),
        in_specs=[SM] + [VM] * 4,
        out_specs=VM,
        compiler_params=pltpu.CompilerParams(vmem_limit_bytes=8 << 20),
        cost_estimate=cost(1e+09, 1e+06),
        name="choose",
    )(sel, quarters, *got)


def gradient_kernel(*refs):
    sel, low, low_peer, high, high_peer, firsts = refs[:6]
    seconds = refs[6:10]
    out, left, right, sems = refs[10:]
    pieces = [ref.at[i] for mine, peer in ((low, low_peer), (high, high_peer)) for i in range(2) for ref in (mine, peer)]
    copies = []
    for d in range(4):
        source = (sel[3, 0] + 4 - d) % 4
        for side in range(2):
            for k, rows in enumerate((firsts.at[source], seconds[d])):
                lanes = pl.ds(pl.multiple_of(source * 512, 128) + (side * 2 + k) * 128, 128)
                copies.append(pltpu.make_async_copy(rows.at[side], left.at[:, lanes], sems.at[len(copies)]))
    for copy in copies:
        copy.start()
    quarter = low.shape[1] - 16
    for i, piece in enumerate(pieces):
        lanes = pl.ds(i * 256, 256)
        whole = piece[pl.ds(0, quarter), :].astype(F32)
        second = whole * piece[pl.ds(quarter, 16), :][0:1].astype(F32)
        right[pl.ds(0, quarter), lanes] = (whole - second).astype(BF16)
        right[pl.ds(quarter, quarter), lanes] = second.astype(BF16)
    for copy in copies:
        copy.wait()
    for m in range(left.shape[0] // TILE):
        part = dot(left[pl.ds(m * TILE, TILE), :], right[...], NT).astype(BF16)
        for i in range(4):
            at_chunk = m * 4 + i
            out[at_chunk // 8, at_chunk // 2 % 4, at_chunk % 2, pl.ds(0, 64), :] = part[i * 64 : i * 64 + 64]


def gradient(sel, firsts, seconds, pieces):
    rows = firsts.shape[2]
    cols = 2 * (pieces[0].shape[1] - 16)
    return pl.pallas_call(
        gradient_kernel,
        out_shape=jax.ShapeDtypeStruct((2, 4, 2, 64, cols), BF16),
        in_specs=[SM] + [VM] * 4 + [HB] * 5,
        out_specs=VM,
        scratch_shapes=[
            pltpu.VMEM((rows, 2048), BF16),
            pltpu.VMEM((cols, 2048), BF16),
            pltpu.SemaphoreType.DMA((16,)),
        ],
        compiler_params=pltpu.CompilerParams(vmem_limit_bytes=20 << 20),
        cost_estimate=cost(9e+09, 2e+07),
        name="gradient",
    )(sel, *pieces, *[in_hbm(a) for a in (firsts, *seconds)])


def adapter_kernel(nl, gg, nl_peer, gg_peer, out):
    width = nl.shape[-1] - 128
    for k in range(2):
        n = jnp.concatenate([nl[0, k], nl_peer[k]], axis=0)
        g = jnp.concatenate([gg[0, k], gg_peer[k]], axis=0)
        for i, (lhs, rhs) in enumerate(((n, g[:, width:]), (g, n[:, width:]))):
            term = dot(lhs[:, :width], rhs, TN).astype(BF16)
            rows = pl.ds((2 * i + k) * 16, 16)
            for r in range(16):
                for t in range(7):
                    out[r % 2, r // 8, (r // 2) % 4, rows, pl.ds(t * 128, 128)] = (
                        term[r * 112 + t * 16 : r * 112 + t * 16 + 16]
                    )


def adapter_terms(nl, gg, nl_peer, gg_peer):
    return pl.pallas_call(
        adapter_kernel,
        out_shape=jax.ShapeDtypeStruct((2, 2, 4, 64, 896), BF16),
        in_specs=[VM] * 4,
        out_specs=VM,
        compiler_params=pltpu.CompilerParams(vmem_limit_bytes=16 << 20),
        cost_estimate=cost(2e9, 4e6),
        name="adapter_terms",
    )(pinned(nl), pinned(gg), nl_peer, gg_peer)


def at(array, index):
    return lax.dynamic_index_in_dim(array, index, 0, keepdims=False)


def move(array, dy=0, dz=0, flip=0):
    pairs = []
    for x in range(4):
        for y in range(4):
            for z in range(4):
                for core in range(2):
                    to_y, to_z = (y + dy) % 4, (z + dz) % 4
                    src = (x * 2 + y // 2) * 16 + y % 2 * 8 + z * 2 + core
                    dst = (x * 2 + to_y // 2) * 16 + to_y % 2 * 8 + to_z * 2 + (core ^ flip)
                    pairs.append((src, dst))
    return lax.ppermute(array, ("pipe", "dp"), pairs)


def over_y(part):
    return lax.ppermute(part, "dp", [(i, i ^ 8) for i in range(16)]).astype(F32)


def over_z(part, zs):
    total = at(part, zs[0]).astype(F32)
    for d in range(1, 4):
        pairs = [(i, i // 8 * 8 + (i + 2 * d) % 8) for i in range(16)]
        total = total + lax.ppermute(at(part, zs[d]), "dp", pairs).astype(F32)
    return total


def over_cores(part, cores):
    got = lax.ppermute(at(part, cores[1]), "dp", [(i, i ^ 1) for i in range(16)])
    return (at(part, cores[0]).astype(F32) + got.astype(F32)).astype(BF16)


def shards(stored, common, down, up, selection, final_c):
    n_pipe, n_dp = lax.axis_size("pipe"), lax.axis_size("dp")
    together = lax.optimization_barrier
    p = lax.axis_index("pipe")
    r = lax.axis_index("dp")
    x_at, h, core = p // 2, p % 2, r % 2
    swap = [(i, i ^ 1) for i in range(n_pipe)]
    turns = [[(i, (i + 2 * d) % n_pipe) for i in range(n_pipe)] for d in range(4)]
    own = stored[0]
    rows, width = own.shape
    half = rows // 2
    a_own, u_own = down[0], up[0]
    rank = a_own.shape[-1]

    def swapped(array):
        return lax.ppermute(array, "pipe", swap)

    def onward(array):
        return lax.ppermute(array, "pipe", turns[1])

    def flip(array):
        return move(array, flip=1)

    def after(value, other):
        return together((value, other))[0]

    mixed = common.transpose(1, 0, 2)
    up_z, down_z = move(mixed, dz=1), move(mixed, dz=-1)
    y_a, y_b = move(mixed[0], dy=1), move(mixed[1], dy=-1)
    x_mine = lax.dynamic_slice_in_dim(own, h * half, half, 0)
    x_other = lax.dynamic_slice_in_dim(own, (1 - h) * half, half, 0)
    c = lax.dynamic_slice_in_dim(final_c, h * half, half, 0)
    marks = jnp.broadcast_to(jnp.pad(selection[0], (0, width - 2)).astype(BF16), (16, width))
    x_peer = swapped(jnp.concatenate([x_other, marks]))
    sel_peer = x_peer[half:, :2][:1].astype(F32).astype(jnp.int32)
    sel = jnp.concatenate([selection, sel_peer, jnp.stack([h, r, x_at, x_at]).astype(jnp.int32).reshape(2, 2)])
    entered = jnp.stack([x_mine, x_peer[:half]])
    near = move(jnp.where(core == 0, a_own, u_own), dy=2)
    first = first_rows(sel, entered)
    first_peer = swapped(first[1])
    up_z, down_z, y_a, y_b, sel, c, entered, first_peer = together(
        (up_z, down_z, y_a, y_b, sel, c, entered, first_peer)
    )
    firsts = lax.all_gather(
        jnp.stack([first[0], first_peer]), "pipe", axis_index_groups=[[0, 2, 4, 6], [1, 3, 5, 7]]
    )
    yz_a, yz_b = move(up_z, dy=1), move(down_z, dy=-1)
    z_a, z_b = move(up_z[0], dz=1), move(down_z[1], dz=-1)
    flips = [flip(after(a, near)) for a in (mixed, up_z, down_z, y_a, y_b)]
    yz_a, yz_b, z_a, z_b, flips = together((yz_a, yz_b, z_a, z_b, flips))
    yf_a, yf_b = move(yz_a[0], dz=1), move(yz_b[1], dz=-1)
    yf_a, yf_b, z_a, z_b, yz_a, yz_b = together((yf_a, yf_b, z_a, z_b, yz_a, yz_b))
    flips += [flip(a) for a in (z_a, z_b, yz_a, yz_b, yf_a, yf_b, near)]
    direct = (mixed, up_z, down_z, y_a, y_b, z_a, z_b, yz_a, yz_b, yf_a, yf_b)
    pieces = [q for pair in zip(direct, flips) for q in pair]
    z, y = (r // 2) % 4, r // 8
    places = ([core, 1 - core], [(z + d) % 4 for d in range(4)], [y, 1 - y])
    places += ([(x_at + d) % 4 for d in range(4)], [(x_at - s) % 4 for s in range(4)])
    places = [[index.astype(jnp.uint32) for index in group] for group in places]
    entered, firsts, places = together((entered, firsts, places))
    cores, zs, ys, xs, sources = places
    *kept, gg, second = forward(sel, entered, (a_own, u_own, near, flips[-1], *pieces))
    nl = kept[0]

    def hop(send, place):
        return lax.ppermute(send, "pipe", [(2 * place + i, 2 * place - 2 + i) for i in range(2)])

    def quarters_of(places, gg):
        parts = transposed(places, sel, gg)
        got = []
        for d in range(1, 4):
            pairs = [(2 * place + i, 2 * ((place + d) % 4) + i) for place in places for i in range(2)]
            got.append(lax.ppermute(parts[d], "pipe", pairs))
        return parts, got

    second_peer = swapped(second[1])
    gg, send = backward(3, sel, c, kept, gg)
    c = hop(send, 3)
    second_peer, gg = together((second_peer, gg))
    ring = [jnp.stack([second[0], second_peer])]
    ring.append(onward(ring[0]))
    gg, send = backward(2, sel, c, kept, gg)
    c = hop(send, 2)
    nl_peer = swapped(after(nl, gg)[1])
    gg, c = together((gg, c))
    parts, got = quarters_of((2, 3), gg)
    gg, send = backward(1, sel, c, kept, gg)
    c = hop(send, 1)
    got = [after(a, gg) for a in got]
    ring[1] = after(ring[1], gg)
    nl_peer = after(nl_peer, gg)
    ring.append(onward(ring[1]))
    high = choose((2, 3), sel, parts, got)
    high_peer = swapped(high)
    c, high = together((c, high))
    gg, _ = backward(0, sel, c, kept, gg)
    ring.append(onward(after(ring[2], gg)))
    high_peer, gg = together((high_peer, gg))
    parts, got = quarters_of((0, 1), gg)
    low = choose((0, 1), sel, parts, got)
    low_peer = swapped(low)
    gg_peer = swapped(gg[1, :2])
    pieces = (low, low_peer, high, high_peer)
    tile = gradient(sel, firsts, ring, pieces)
    terms = over_cores(adapter_terms(nl, gg, nl_peer, gg_peer), cores)
    terms = (at(terms, ys[0]).astype(F32) + over_y(at(terms, ys[1]))).astype(BF16)
    terms = over_z(terms, zs)
    tile = over_z(over_cores(tile, cores), zs).astype(BF16)
    tile = at(tile, ys[0]).astype(F32) + over_y(at(tile, ys[1]))
    tile = tile.astype(BF16).reshape(4, 16, -1)
    ct = gg[:, 2, :, :width]
    placed = jnp.stack(
        [at(tile, xs[0])] + [lax.ppermute(at(tile, xs[d]), "pipe", turns[d]) for d in range(1, 4)]
    )
    placed = jnp.stack([at(placed, source) for source in sources], axis=1)
    each = width // (n_pipe * n_dp)
    shared = placed[:each].reshape(each, 4, 2, width // 4).transpose(0, 2, 1, 3)
    shared = shared.reshape(each, 2, width).astype(F32)

    ours, theirs = ct[0], swapped(ct[1])
    result = jnp.where(
        h == 0, jnp.concatenate([ours, theirs]), jnp.concatenate([theirs, ours])
    )
    both = terms.reshape(4, 16, 7, rank).transpose(0, 2, 1, 3).reshape(4, 112, rank)
    return result[None], shared, both[None, :2], both[None, 2:]


def solution(mesh):
    return jax.shard_map(
        shards,
        mesh=mesh,
        in_specs=(
            P("pipe", "dp", None),
            P("dp", None, None),
            P("pipe", None, None, None),
            P("pipe", None, None, None),
            P("pipe", None),
            P("dp", None),
        ),
        out_specs=(
            P("pipe", "dp", None),
            P(("pipe", "dp"), None, None),
            P("pipe", None, "dp", None),
            P("pipe", None, "dp", None),
        ),
        check_vma=False,
    )
```

```python
import functools

import jax
import jax.numpy as jnp
from jax import lax
from jax.experimental import pallas as pl
from jax.experimental.pallas import tpu as pltpu
from jax.sharding import PartitionSpec as P

EPS = 1e-06
TILE = 256
F32 = jnp.float32
BF16 = jnp.bfloat16
NT = (((1,), (1,)), ((), ()))
TN = (((0,), (0,)), ((), ()))
HB = pl.BlockSpec(memory_space=pltpu.HBM)
VM = pl.BlockSpec(memory_space=pltpu.VMEM)
SM = pl.BlockSpec(memory_space=pltpu.SMEM)


def dot(a, b, dims=(((1,), (0,)), ((), ()))):
    return lax.dot_general(a, b, dims, preferred_element_type=F32)


def cost(flops, bytes_accessed):
    return pl.CostEstimate(flops=int(flops), bytes_accessed=int(bytes_accessed), transcendentals=0)


def pinned(array):
    return pltpu.with_memory_space_constraint(array, pltpu.VMEM)


def in_hbm(array):
    return pltpu.with_memory_space_constraint(array, pltpu.HBM)


PIECES = ((0, 0, None), (0, 3, None), (0, 1, None), (1, 0, 0), (1, 0, 1), (0, 2, 0), (0, 2, 1)) + (
    (1, 3, None), (1, 1, None), (1, 2, 0), (1, 2, 1)
)


def row_blocks(src, tile, dst, h, lanes):
    width = src.shape[1]
    for t in range(width // TILE):
        tile[pl.ds(t * TILE, TILE), :] = src[:, t * TILE : (t + 1) * TILE].astype(F32).T
    tile[pl.ds(width, 8), :] = jnp.zeros((8, tile.shape[1]), F32)
    for p in range(8):
        x, half = p // 2, p % 2
        slot = jnp.bitwise_xor(h, half)
        for r in range(16):
            core, z, y = r % 2, (r // 2) % 4, r // 8
            at_row = (((core * 4 + z) * 2 + y) * 4 + x) * 16
            dst[slot, pl.ds(at_row, 16), lanes] = tile[pl.ds((p * 16 + r) * 14, 16), :].astype(BF16)


def first_kernel(sel, x, out, tile):
    rows = jnp.concatenate([x[0], x[1]], axis=0).astype(F32)
    sc = lax.rsqrt(jnp.mean(rows * rows, axis=-1, keepdims=True) + EPS)
    row_blocks((rows * sc).astype(BF16), tile, out, sel[2, 0], pl.ds(0, 128))


def first_rows(sel, x):
    width = x.shape[-1]
    return pl.pallas_call(
        first_kernel,
        out_shape=jax.ShapeDtypeStruct((2, 1024, 128), BF16),
        in_specs=[SM, VM],
        out_specs=VM,
        scratch_shapes=[pltpu.VMEM((width + 8, 128), F32)],
        compiler_params=pltpu.CompilerParams(vmem_limit_bytes=16 << 20),
        cost_estimate=cost(1e+09, 1e+06),
        name="first_rows",
    )(sel, x)


def forward_kernel(sel, x, *refs):
    a_own, u_own, near, far = refs[:4]
    pieces = refs[4 : 4 + 2 * len(PIECES)]
    nl, slope, scale, wt, auv, gg, out, wv, xs, tile, sems = refs[4 + 2 * len(PIECES) :]
    av, uv = auv.at[0], auv.at[1]
    width = x.shape[-1]
    per = pieces[0].shape[-2]
    h, r = sel[2, 0], sel[2, 1]
    core, z, y = r % 2, (r // 2) % 4, r // 8
    small = []
    for i, (src, dst) in enumerate(
        ((a_own, av.at[0]), (u_own, uv.at[0]), (near, auv.at[core, 1]), (far, auv.at[1 - core, 1]))
    ):
        small.append(pltpu.make_async_copy(src, dst, sems.at[32 + i]))
    for copy in small:
        copy.start()
    for block in range(2):
        for i, ref in enumerate(pieces):
            dy, dz, held = PIECES[i // 2]
            if held is not None and held != block:
                continue
            place = jnp.bitwise_xor(y, dy) * 8 + (z + dz) % 4 * 2 + jnp.bitwise_xor(core, i % 2)
            dst = wv.at[block, pl.ds(pl.multiple_of(place * per, 16), per), :]
            src = ref.at[block] if held is None else ref
            pltpu.make_async_copy(src, dst, sems.at[block * 16 + place]).start()
    big = []
    for block in range(2):
        for place in range(16):
            dst = wv.at[block, pl.ds(place * per, per), :]
            big.append(pltpu.make_async_copy(dst, dst, sems.at[block * 16 + place]))
    gg[...] = jnp.zeros_like(gg)
    for o in range(2):
        xs[o] = x[o]
    here = 0
    for block in range(2):
        for t in range(width // TILE):
            while here < 16 * block + min(16, -(-(t + 1) * TILE // per)):
                big[here].wait()
                here += 1
            wt[block, :, pl.ds(t * TILE, TILE)] = wv[block, pl.ds(t * TILE, TILE), :].T
    for copy in small:
        copy.wait()
    for k in range(2):
        rows = jnp.concatenate([xs[0], xs[1]], axis=0).astype(F32)
        sc = lax.rsqrt(jnp.mean(rows * rows, axis=-1, keepdims=True) + EPS)
        nm = (rows * sc).astype(BF16)
        if k == 1:
            row_blocks(nm, tile, out, h, pl.ds(0, 128))
        for o in range(2):
            part = slice(o * 64, (o + 1) * 64)
            scale[o, k] = jnp.broadcast_to(sc[part], scale.shape[2:])
            mine = nm[part]
            nl[o, k, :, pl.ds(0, width)] = mine
            low = dot(mine, av[o, k]).astype(BF16)
            nl[o, k, :, pl.ds(width, 128)] = low
            block = sel[o, k]
            for t in range(width // TILE):
                cols = pl.ds(t * TILE, TILE)
                pre = dot(mine, wv[block, :, cols]) + dot(low, uv[o, k, cols, :], NT)
                sigma = 1.0 / (1.0 + jnp.exp(-pre))
                slope[o, k, :, cols] = sigma * (1.0 + pre * (1.0 - sigma))
                if k == 0:
                    xs[o, :, cols] = (xs[o, :, cols].astype(F32) + pre * sigma).astype(BF16)


def forward(sel, x, weights):
    rows, width = x.shape[1:]
    rank = weights[0].shape[-1]
    return pl.pallas_call(
        forward_kernel,
        out_shape=(
            pltpu.VMEM((2, 2, rows, width + rank), BF16),
            pltpu.VMEM((2, 2, rows, width), F32),
            pltpu.VMEM((2, 2, rows, 128), F32),
            pltpu.VMEM((2, width, width), BF16),
            pltpu.VMEM((2, 2, 2, width, rank), BF16),
            pltpu.VMEM((2, 3, rows, width + rank), BF16),
            jax.ShapeDtypeStruct((2, 1024, 128), BF16),
        ),
        in_specs=[SM, VM] + [HB] * len(weights),
        out_specs=(VM,) * 7,
        scratch_shapes=[
            pltpu.VMEM((2, width, width), BF16),
            pltpu.VMEM((2, rows, width), BF16),
            pltpu.VMEM((width + 8, 128), F32),
            pltpu.SemaphoreType.DMA((36,)),
        ],
        compiler_params=pltpu.CompilerParams(vmem_limit_bytes=22 << 20),
        cost_estimate=cost(1.5e+10, 2e+07),
        name="forward",
    )(sel, x, *[in_hbm(w) for w in weights])


def backward_kernel(at_place, sel, c, nl, slope, scale, wt, auv, old_gg, gg, send, gn):
    width = c.shape[-1]
    av, uv = auv.at[0], auv.at[1]

    @pl.when(sel[3, 0] == at_place)
    def _():
        h = sel[2, 0]
        cur = c[...]
        for j in (1, 0):
            o = jnp.bitwise_xor(h, j)
            for k in (1, 0):
                c32 = cur.astype(F32)
                g = (c32 * slope[o, k]).astype(BF16)
                gg[o, k, :, pl.ds(0, width)] = g
                low = dot(g, uv[o, k]).astype(BF16)
                gg[o, k, :, pl.ds(width, 128)] = low
                block = sel[o, k]
                total = jnp.zeros((g.shape[0], 1), F32)
                for t in range(width // TILE):
                    cols = pl.ds(t * TILE, TILE)
                    part = dot(g, wt[block, :, cols]) + dot(low, av[o, k, cols, :], NT)
                    gn[:, cols] = part
                    total = total + jnp.sum(part * nl[o, k, :, cols].astype(F32), axis=-1, keepdims=True)
                mean = total / width
                z = nl[o, k, :, pl.ds(0, width)].astype(F32)
                sc = scale[o, k, :, 0:1]
                cur = (c32 + sc * (gn[...] - z * mean)).astype(BF16)
            gg[o, 2, :, pl.ds(0, width)] = cur
        send[...] = cur


def backward(at_place, sel, c, kept, gg):
    rows, width = c.shape
    kept = [pinned(a) for a in kept]
    return pl.pallas_call(
        functools.partial(backward_kernel, at_place),
        out_shape=(jax.ShapeDtypeStruct(gg.shape, BF16), jax.ShapeDtypeStruct((rows, width), BF16)),
        in_specs=[SM, VM] + [VM] * 6,
        out_specs=(VM, VM),
        scratch_shapes=[pltpu.VMEM((rows, width), F32)],
        input_output_aliases={7: 0},
        compiler_params=pltpu.CompilerParams(vmem_limit_bytes=6 << 20),
        cost_estimate=cost(9e+09, 2e+07),
        name="backward",
    )(sel, c, *kept, pinned(gg))


def transpose_kernel(places, sel, gp, out):
    quarter = (gp.shape[-1] - 128) // 4

    @pl.when((sel[3, 0] >= places[0]) & (sel[3, 0] <= places[-1]))
    def _():
        for k in range(2):
            lanes = pl.ds(k * 128, 128)
            both = jnp.concatenate([gp[0, k], gp[1, k]], axis=0)[:, : 4 * quarter]
            for q in range(4):
                d = (q + 4 - sel[3, 0]) % 4
                for t in range(0, quarter, 64):
                    out[d, pl.ds(t, 64), lanes] = both[:, q * quarter + t : q * quarter + t + 64].T
            side = lax.broadcasted_iota(jnp.int32, (16, 128), 1) // 64
            mark = jnp.where(side == 0, sel[0, k], sel[1, k])
            for q in range(4):
                out[q, pl.ds(quarter, 16), lanes] = mark.astype(F32).astype(BF16)


def transposed(places, sel, gp):
    quarter = (gp.shape[-1] - 128) // 4
    return pl.pallas_call(
        functools.partial(transpose_kernel, places),
        out_shape=jax.ShapeDtypeStruct((4, quarter + 16, 256), BF16),
        in_specs=[SM, VM],
        out_specs=VM,
        compiler_params=pltpu.CompilerParams(vmem_limit_bytes=6 << 20),
        cost_estimate=cost(1.8e+09, 4e+06),
        name="transposed",
    )(sel, pinned(gp))


def choose_kernel(places, sel, quarters, one, two, three, out):
    for i, place in enumerate(places):
        away = (sel[3, 0] + 4 - place) % 4

        @pl.when(away == 0)
        def _(i=i):
            out[i] = quarters[0]

        for d, got in ((1, one), (2, two), (3, three)):

            @pl.when(away == d)
            def _(i=i, got=got):
                out[i] = got[...]


def choose(places, sel, quarters, got):
    return pl.pallas_call(
        functools.partial(choose_kernel, places),
        out_shape=jax.ShapeDtypeStruct((len(places),) + quarters.shape[1:], BF16),
        in_specs=[SM] + [VM] * 4,
        out_specs=VM,
        compiler_params=pltpu.CompilerParams(vmem_limit_bytes=8 << 20),
        cost_estimate=cost(1e+09, 1e+06),
        name="choose",
    )(sel, quarters, *got)


def gradient_kernel(*refs):
    sel, low, low_peer, high, high_peer, firsts = refs[:6]
    seconds = refs[6:10]
    out, left, right, sems = refs[10:]
    pieces = [ref.at[i] for mine, peer in ((low, low_peer), (high, high_peer)) for i in range(2) for ref in (mine, peer)]
    copies = []
    for d in range(4):
        source = (sel[3, 0] + 4 - d) % 4
        for side in range(2):
            for k, rows in enumerate((firsts.at[source], seconds[d])):
                lanes = pl.ds(pl.multiple_of(source * 512, 128) + (side * 2 + k) * 128, 128)
                copies.append(pltpu.make_async_copy(rows.at[side], left.at[:, lanes], sems.at[len(copies)]))
    for copy in copies:
        copy.start()
    quarter = low.shape[1] - 16
    for i, piece in enumerate(pieces):
        lanes = pl.ds(i * 256, 256)
        whole = piece[pl.ds(0, quarter), :].astype(F32)
        second = whole * piece[pl.ds(quarter, 16), :][0:1].astype(F32)
        right[pl.ds(0, quarter), lanes] = (whole - second).astype(BF16)
        right[pl.ds(quarter, quarter), lanes] = second.astype(BF16)
    for copy in copies:
        copy.wait()
    for m in range(left.shape[0] // TILE):
        part = dot(left[pl.ds(m * TILE, TILE), :], right[...], NT).astype(BF16)
        for i in range(4):
            at_chunk = m * 4 + i
            out[at_chunk // 8, at_chunk // 2 % 4, at_chunk % 2, pl.ds(0, 64), :] = part[i * 64 : i * 64 + 64]


def gradient(sel, firsts, seconds, pieces):
    rows = firsts.shape[2]
    cols = 2 * (pieces[0].shape[1] - 16)
    return pl.pallas_call(
        gradient_kernel,
        out_shape=jax.ShapeDtypeStruct((2, 4, 2, 64, cols), BF16),
        in_specs=[SM] + [VM] * 4 + [HB] * 5,
        out_specs=VM,
        scratch_shapes=[
            pltpu.VMEM((rows, 2048), BF16),
            pltpu.VMEM((cols, 2048), BF16),
            pltpu.SemaphoreType.DMA((16,)),
        ],
        compiler_params=pltpu.CompilerParams(vmem_limit_bytes=20 << 20),
        cost_estimate=cost(9e+09, 2e+07),
        name="gradient",
    )(sel, *pieces, *[in_hbm(a) for a in (firsts, *seconds)])


def adapter_kernel(nl, gg, nl_peer, gg_peer, out):
    width = nl.shape[-1] - 128
    for k in range(2):
        n = jnp.concatenate([nl[0, k], nl_peer[k]], axis=0)
        g = jnp.concatenate([gg[0, k], gg_peer[k]], axis=0)
        for i, (lhs, rhs) in enumerate(((n, g[:, width:]), (g, n[:, width:]))):
            term = dot(lhs[:, :width], rhs, TN).astype(BF16)
            rows = pl.ds((2 * i + k) * 16, 16)
            for r in range(16):
                for t in range(7):
                    out[r % 2, r // 8, (r // 2) % 4, rows, pl.ds(t * 128, 128)] = (
                        term[r * 112 + t * 16 : r * 112 + t * 16 + 16]
                    )


def adapter_terms(nl, gg, nl_peer, gg_peer):
    return pl.pallas_call(
        adapter_kernel,
        out_shape=jax.ShapeDtypeStruct((2, 2, 4, 64, 896), BF16),
        in_specs=[VM] * 4,
        out_specs=VM,
        compiler_params=pltpu.CompilerParams(vmem_limit_bytes=16 << 20),
        cost_estimate=cost(2e9, 4e6),
        name="adapter_terms",
    )(pinned(nl), pinned(gg), nl_peer, gg_peer)


def at(array, index):
    return lax.dynamic_index_in_dim(array, index, 0, keepdims=False)


def move(array, dy=0, dz=0, flip=0):
    pairs = []
    for x in range(4):
        for y in range(4):
            for z in range(4):
                for core in range(2):
                    to_y, to_z = (y + dy) % 4, (z + dz) % 4
                    src = (x * 2 + y // 2) * 16 + y % 2 * 8 + z * 2 + core
                    dst = (x * 2 + to_y // 2) * 16 + to_y % 2 * 8 + to_z * 2 + (core ^ flip)
                    pairs.append((src, dst))
    return lax.ppermute(array, ("pipe", "dp"), pairs)


def over_y(part):
    return lax.ppermute(part, "dp", [(i, i ^ 8) for i in range(16)]).astype(F32)


def over_z(part, zs):
    total = at(part, zs[0]).astype(F32)
    for d in range(1, 4):
        pairs = [(i, i // 8 * 8 + (i + 2 * d) % 8) for i in range(16)]
        total = total + lax.ppermute(at(part, zs[d]), "dp", pairs).astype(F32)
    return total


def over_cores(part, cores):
    got = lax.ppermute(at(part, cores[1]), "dp", [(i, i ^ 1) for i in range(16)])
    return (at(part, cores[0]).astype(F32) + got.astype(F32)).astype(BF16)


def shards(stored, common, down, up, selection, final_c):
    n_pipe, n_dp = lax.axis_size("pipe"), lax.axis_size("dp")
    together = lax.optimization_barrier
    p = lax.axis_index("pipe")
    r = lax.axis_index("dp")
    x_at, h, core = p // 2, p % 2, r % 2
    swap = [(i, i ^ 1) for i in range(n_pipe)]
    turns = [[(i, (i + 2 * d) % n_pipe) for i in range(n_pipe)] for d in range(4)]
    own = stored[0]
    rows, width = own.shape
    half = rows // 2
    a_own, u_own = down[0], up[0]
    rank = a_own.shape[-1]

    def swapped(array):
        return lax.ppermute(array, "pipe", swap)

    def onward(array):
        return lax.ppermute(array, "pipe", turns[1])

    def flip(array):
        return move(array, flip=1)

    def after(value, other):
        return together((value, other))[0]

    mixed = common.transpose(1, 0, 2)
    up_z, down_z = move(mixed, dz=1), move(mixed, dz=-1)
    y_a, y_b = move(mixed[0], dy=1), move(mixed[1], dy=-1)
    x_mine = lax.dynamic_slice_in_dim(own, h * half, half, 0)
    x_other = lax.dynamic_slice_in_dim(own, (1 - h) * half, half, 0)
    c = lax.dynamic_slice_in_dim(final_c, h * half, half, 0)
    marks = jnp.broadcast_to(jnp.pad(selection[0], (0, width - 2)).astype(BF16), (16, width))
    x_peer = swapped(jnp.concatenate([x_other, marks]))
    sel_peer = x_peer[half:, :2][:1].astype(F32).astype(jnp.int32)
    sel = jnp.concatenate([selection, sel_peer, jnp.stack([h, r, x_at, x_at]).astype(jnp.int32).reshape(2, 2)])
    entered = jnp.stack([x_mine, x_peer[:half]])
    near = move(jnp.where(core == 0, a_own, u_own), dy=2)
    first = first_rows(sel, entered)
    first_peer = swapped(first[1])
    up_z, down_z, y_a, y_b, sel, c, entered, first_peer, near = together(
        (up_z, down_z, y_a, y_b, sel, c, entered, first_peer, near)
    )
    firsts = lax.all_gather(
        jnp.stack([first[0], first_peer]), "pipe", axis_index_groups=[[0, 2, 4, 6], [1, 3, 5, 7]]
    )
    yz_a, yz_b = move(up_z, dy=1), move(down_z, dy=-1)
    z_a, z_b = move(up_z[0], dz=1), move(down_z[1], dz=-1)
    flips = [flip(after(a, (z_a, z_b))) for a in (mixed, up_z, down_z)]
    flips += [flip(after(a, (yz_a, yz_b))) for a in (y_a, y_b)]
    yz_a, yz_b, z_a, z_b, flips = together((yz_a, yz_b, z_a, z_b, flips))
    yf_a, yf_b = move(yz_a[0], dz=1), move(yz_b[1], dz=-1)
    late = [flip(a) for a in (z_a, z_b, yz_a, yz_b, near)]
    yf_a, yf_b, late = together((yf_a, yf_b, late))
    flips += [*late[:4], flip(yf_a), flip(yf_b), late[4]]
    direct = (mixed, up_z, down_z, y_a, y_b, z_a, z_b, yz_a, yz_b, yf_a, yf_b)
    pieces = [q for pair in zip(direct, flips) for q in pair]
    z, y = (r // 2) % 4, r // 8
    places = ([core, 1 - core], [(z + d) % 4 for d in range(4)], [y, 1 - y])
    places += ([(x_at + d) % 4 for d in range(4)], [(x_at - s) % 4 for s in range(4)])
    places = [[index.astype(jnp.uint32) for index in group] for group in places]
    entered, firsts, places = together((entered, firsts, places))
    cores, zs, ys, xs, sources = places
    *kept, gg, second = forward(sel, entered, (a_own, u_own, near, flips[-1], *pieces))
    nl = kept[0]

    def hop(send, place):
        return lax.ppermute(send, "pipe", [(2 * place + i, 2 * place - 2 + i) for i in range(2)])

    def quarters_of(places, gg):
        parts = transposed(places, sel, gg)
        got = []
        for d in range(1, 4):
            pairs = [(2 * place + i, 2 * ((place + d) % 4) + i) for place in places for i in range(2)]
            got.append(lax.ppermute(parts[d], "pipe", pairs))
        return parts, got

    second_peer = swapped(second[1])
    gg, send = backward(3, sel, c, kept, gg)
    c = hop(send, 3)
    second_peer, gg = together((second_peer, gg))
    ring = [jnp.stack([second[0], second_peer])]
    ring.append(onward(ring[0]))
    gg, send = backward(2, sel, c, kept, gg)
    c = hop(send, 2)
    nl_peer = swapped(after(nl, gg)[1])
    gg, c = together((gg, c))
    parts, got = quarters_of((2, 3), gg)
    gg, send = backward(1, sel, c, kept, gg)
    c = hop(send, 1)
    got = [after(a, gg) for a in got]
    ring[1] = after(ring[1], gg)
    nl_peer = after(nl_peer, gg)
    ring.append(onward(ring[1]))
    high = choose((2, 3), sel, parts, got)
    high_peer = swapped(high)
    c, high = together((c, high))
    gg, _ = backward(0, sel, c, kept, gg)
    ring.append(onward(after(ring[2], gg)))
    high_peer, gg = together((high_peer, gg))
    parts, got = quarters_of((0, 1), gg)
    low = choose((0, 1), sel, parts, got)
    low_peer = swapped(low)
    gg_peer = swapped(gg[1, :2])
    pieces = (low, low_peer, high, high_peer)
    tile = gradient(sel, firsts, ring, pieces)
    terms = over_cores(adapter_terms(nl, gg, nl_peer, gg_peer), cores)
    terms = (at(terms, ys[0]).astype(F32) + over_y(at(terms, ys[1]))).astype(BF16)
    terms = over_z(terms, zs)
    tile = over_z(over_cores(tile, cores), zs).astype(BF16)
    tile = at(tile, ys[0]).astype(F32) + over_y(at(tile, ys[1]))
    tile = tile.astype(BF16).reshape(4, 16, -1)
    ct = gg[:, 2, :, :width]
    placed = jnp.stack(
        [at(tile, xs[0])] + [lax.ppermute(at(tile, xs[d]), "pipe", turns[d]) for d in range(1, 4)]
    )
    placed = jnp.stack([at(placed, source) for source in sources], axis=1)
    each = width // (n_pipe * n_dp)
    shared = placed[:each].reshape(each, 4, 2, width // 4).transpose(0, 2, 1, 3)
    shared = shared.reshape(each, 2, width).astype(F32)

    ours, theirs = ct[0], swapped(ct[1])
    result = jnp.where(
        h == 0, jnp.concatenate([ours, theirs]), jnp.concatenate([theirs, ours])
    )
    both = terms.reshape(4, 16, 7, rank).transpose(0, 2, 1, 3).reshape(4, 112, rank)
    return result[None], shared, both[None, :2], both[None, 2:]


def solution(mesh):
    return jax.shard_map(
        shards,
        mesh=mesh,
        in_specs=(
            P("pipe", "dp", None),
            P("dp", None, None),
            P("pipe", None, None, None),
            P("pipe", None, None, None),
            P("pipe", None),
            P("dp", None),
        ),
        out_specs=(
            P("pipe", "dp", None),
            P(("pipe", "dp"), None, None),
            P("pipe", None, "dp", None),
            P("pipe", None, "dp", None),
        ),
        check_vma=False,
    )
```

```python
import functools

import jax
import jax.numpy as jnp
from jax import lax
from jax.experimental import pallas as pl
from jax.experimental.pallas import tpu as pltpu
from jax.sharding import PartitionSpec as P

EPS = 1e-06
TILE = 256
F32 = jnp.float32
BF16 = jnp.bfloat16
NT = (((1,), (1,)), ((), ()))
TN = (((0,), (0,)), ((), ()))
HB = pl.BlockSpec(memory_space=pltpu.HBM)
VM = pl.BlockSpec(memory_space=pltpu.VMEM)
SM = pl.BlockSpec(memory_space=pltpu.SMEM)


def dot(a, b, dims=(((1,), (0,)), ((), ()))):
    return lax.dot_general(a, b, dims, preferred_element_type=F32)


def cost(flops, bytes_accessed):
    return pl.CostEstimate(flops=int(flops), bytes_accessed=int(bytes_accessed), transcendentals=0)


def pinned(array):
    return pltpu.with_memory_space_constraint(array, pltpu.VMEM)


def in_hbm(array):
    return pltpu.with_memory_space_constraint(array, pltpu.HBM)


PIECES = ((0, 0, None), (0, 3, None), (0, 1, None), (1, 0, 0), (1, 0, 1), (0, 2, 0), (0, 2, 1)) + (
    (1, 3, None), (1, 1, None), (1, 2, 0), (1, 2, 1)
)


def row_blocks(src, tile, dst, h, lanes):
    width = src.shape[1]
    for t in range(width // TILE):
        tile[pl.ds(t * TILE, TILE), :] = src[:, t * TILE : (t + 1) * TILE].astype(F32).T
    tile[pl.ds(width, 8), :] = jnp.zeros((8, tile.shape[1]), F32)
    for p in range(8):
        x, half = p // 2, p % 2
        slot = jnp.bitwise_xor(h, half)
        for r in range(16):
            core, z, y = r % 2, (r // 2) % 4, r // 8
            at_row = (((core * 4 + z) * 2 + y) * 4 + x) * 16
            dst[slot, pl.ds(at_row, 16), lanes] = tile[pl.ds((p * 16 + r) * 14, 16), :].astype(BF16)


def first_kernel(sel, x, out, tile):
    rows = jnp.concatenate([x[0], x[1]], axis=0).astype(F32)
    sc = lax.rsqrt(jnp.mean(rows * rows, axis=-1, keepdims=True) + EPS)
    row_blocks((rows * sc).astype(BF16), tile, out, sel[2, 0], pl.ds(0, 128))


def first_rows(sel, x):
    width = x.shape[-1]
    return pl.pallas_call(
        first_kernel,
        out_shape=jax.ShapeDtypeStruct((2, 1024, 128), BF16),
        in_specs=[SM, VM],
        out_specs=VM,
        scratch_shapes=[pltpu.VMEM((width + 8, 128), F32)],
        compiler_params=pltpu.CompilerParams(vmem_limit_bytes=16 << 20),
        cost_estimate=cost(1e+09, 1e+06),
        name="first_rows",
    )(sel, x)


def forward_kernel(sel, x, *refs):
    a_own, u_own, near, far = refs[:4]
    pieces = refs[4 : 4 + 2 * len(PIECES)]
    nl, slope, scale, wt, auv, gg, out, wv, xs, tile, sems = refs[4 + 2 * len(PIECES) :]
    av, uv = auv.at[0], auv.at[1]
    width = x.shape[-1]
    per = pieces[0].shape[-2]
    h, r = sel[2, 0], sel[2, 1]
    core, z, y = r % 2, (r // 2) % 4, r // 8
    small = []
    for i, (src, dst) in enumerate(
        ((a_own, av.at[0]), (u_own, uv.at[0]), (near, auv.at[core, 1]), (far, auv.at[1 - core, 1]))
    ):
        small.append(pltpu.make_async_copy(src, dst, sems.at[32 + i]))
    for copy in small:
        copy.start()
    for block in range(2):
        for i, ref in enumerate(pieces):
            dy, dz, held = PIECES[i // 2]
            if held is not None and held != block:
                continue
            place = jnp.bitwise_xor(y, dy) * 8 + (z + dz) % 4 * 2 + jnp.bitwise_xor(core, i % 2)
            dst = wv.at[block, pl.ds(pl.multiple_of(place * per, 16), per), :]
            src = ref.at[block] if held is None else ref
            pltpu.make_async_copy(src, dst, sems.at[block * 16 + place]).start()
    big = []
    for block in range(2):
        for place in range(16):
            dst = wv.at[block, pl.ds(place * per, per), :]
            big.append(pltpu.make_async_copy(dst, dst, sems.at[block * 16 + place]))
    gg[...] = jnp.zeros_like(gg)
    for o in range(2):
        xs[o] = x[o]
    here = 0
    for block in range(2):
        for t in range(width // TILE):
            while here < 16 * block + min(16, -(-(t + 1) * TILE // per)):
                big[here].wait()
                here += 1
            wt[block, :, pl.ds(t * TILE, TILE)] = wv[block, pl.ds(t * TILE, TILE), :].T
    for copy in small:
        copy.wait()
    for k in range(2):
        rows = jnp.concatenate([xs[0], xs[1]], axis=0).astype(F32)
        sc = lax.rsqrt(jnp.mean(rows * rows, axis=-1, keepdims=True) + EPS)
        nm = (rows * sc).astype(BF16)
        if k == 1:
            row_blocks(nm, tile, out, h, pl.ds(0, 128))
        for o in range(2):
            part = slice(o * 64, (o + 1) * 64)
            scale[o, k] = jnp.broadcast_to(sc[part], scale.shape[2:])
            mine = nm[part]
            nl[o, k, :, pl.ds(0, width)] = mine
            low = dot(mine, av[o, k]).astype(BF16)
            nl[o, k, :, pl.ds(width, 128)] = low
            block = sel[o, k]
            for t in range(width // TILE):
                cols = pl.ds(t * TILE, TILE)
                pre = dot(mine, wv[block, :, cols]) + dot(low, uv[o, k, cols, :], NT)
                sigma = 1.0 / (1.0 + jnp.exp(-pre))
                slope[o, k, :, cols] = sigma * (1.0 + pre * (1.0 - sigma))
                if k == 0:
                    xs[o, :, cols] = (xs[o, :, cols].astype(F32) + pre * sigma).astype(BF16)


def forward(sel, x, weights):
    rows, width = x.shape[1:]
    rank = weights[0].shape[-1]
    return pl.pallas_call(
        forward_kernel,
        out_shape=(
            pltpu.VMEM((2, 2, rows, width + rank), BF16),
            pltpu.VMEM((2, 2, rows, width), F32),
            pltpu.VMEM((2, 2, rows, 128), F32),
            pltpu.VMEM((2, width, width), BF16),
            pltpu.VMEM((2, 2, 2, width, rank), BF16),
            pltpu.VMEM((2, 3, rows, width + rank), BF16),
            jax.ShapeDtypeStruct((2, 1024, 128), BF16),
        ),
        in_specs=[SM, VM] + [HB] * len(weights),
        out_specs=(VM,) * 7,
        scratch_shapes=[
            pltpu.VMEM((2, width, width), BF16),
            pltpu.VMEM((2, rows, width), BF16),
            pltpu.VMEM((width + 8, 128), F32),
            pltpu.SemaphoreType.DMA((36,)),
        ],
        compiler_params=pltpu.CompilerParams(vmem_limit_bytes=22 << 20),
        cost_estimate=cost(1.5e+10, 2e+07),
        name="forward",
    )(sel, x, *[in_hbm(w) for w in weights])


def backward_kernel(at_place, sel, c, nl, slope, scale, wt, auv, old_gg, gg, send, gn):
    width = c.shape[-1]
    av, uv = auv.at[0], auv.at[1]

    @pl.when(sel[3, 0] == at_place)
    def _():
        h = sel[2, 0]
        cur = c[...]
        for j in (1, 0):
            o = jnp.bitwise_xor(h, j)
            for k in (1, 0):
                c32 = cur.astype(F32)
                g = (c32 * slope[o, k]).astype(BF16)
                gg[o, k, :, pl.ds(0, width)] = g
                low = dot(g, uv[o, k]).astype(BF16)
                gg[o, k, :, pl.ds(width, 128)] = low
                block = sel[o, k]
                total = jnp.zeros((g.shape[0], 1), F32)
                for t in range(width // TILE):
                    cols = pl.ds(t * TILE, TILE)
                    part = dot(g, wt[block, :, cols]) + dot(low, av[o, k, cols, :], NT)
                    gn[:, cols] = part
                    total = total + jnp.sum(part * nl[o, k, :, cols].astype(F32), axis=-1, keepdims=True)
                mean = total / width
                z = nl[o, k, :, pl.ds(0, width)].astype(F32)
                sc = scale[o, k, :, 0:1]
                cur = (c32 + sc * (gn[...] - z * mean)).astype(BF16)
            gg[o, 2, :, pl.ds(0, width)] = cur
        send[...] = cur


def backward(at_place, sel, c, kept, gg):
    rows, width = c.shape
    kept = [pinned(a) for a in kept]
    return pl.pallas_call(
        functools.partial(backward_kernel, at_place),
        out_shape=(jax.ShapeDtypeStruct(gg.shape, BF16), jax.ShapeDtypeStruct((rows, width), BF16)),
        in_specs=[SM, VM] + [VM] * 6,
        out_specs=(VM, VM),
        scratch_shapes=[pltpu.VMEM((rows, width), F32)],
        input_output_aliases={7: 0},
        compiler_params=pltpu.CompilerParams(vmem_limit_bytes=6 << 20),
        cost_estimate=cost(9e+09, 2e+07),
        name="backward",
    )(sel, c, *kept, pinned(gg))


def transpose_kernel(places, sel, gp, out):
    quarter = (gp.shape[-1] - 128) // 4

    @pl.when((sel[3, 0] >= places[0]) & (sel[3, 0] <= places[-1]))
    def _():
        for k in range(2):
            lanes = pl.ds(k * 128, 128)
            both = jnp.concatenate([gp[0, k], gp[1, k]], axis=0)[:, : 4 * quarter]
            for q in range(4):
                d = (q + 4 - sel[3, 0]) % 4
                for t in range(0, quarter, 64):
                    out[d, pl.ds(t, 64), lanes] = both[:, q * quarter + t : q * quarter + t + 64].T
            side = lax.broadcasted_iota(jnp.int32, (16, 128), 1) // 64
            mark = jnp.where(side == 0, sel[0, k], sel[1, k])
            for q in range(4):
                out[q, pl.ds(quarter, 16), lanes] = mark.astype(F32).astype(BF16)


def transposed(places, sel, gp):
    quarter = (gp.shape[-1] - 128) // 4
    return pl.pallas_call(
        functools.partial(transpose_kernel, places),
        out_shape=jax.ShapeDtypeStruct((4, quarter + 16, 256), BF16),
        in_specs=[SM, VM],
        out_specs=VM,
        compiler_params=pltpu.CompilerParams(vmem_limit_bytes=6 << 20),
        cost_estimate=cost(1.8e+09, 4e+06),
        name="transposed",
    )(sel, pinned(gp))


def choose_kernel(places, sel, quarters, one, two, three, out):
    for i, place in enumerate(places):
        away = (sel[3, 0] + 4 - place) % 4

        @pl.when(away == 0)
        def _(i=i):
            out[i] = quarters[0]

        for d, got in ((1, one), (2, two), (3, three)):

            @pl.when(away == d)
            def _(i=i, got=got):
                out[i] = got[...]


def choose(places, sel, quarters, got):
    return pl.pallas_call(
        functools.partial(choose_kernel, places),
        out_shape=jax.ShapeDtypeStruct((len(places),) + quarters.shape[1:], BF16),
        in_specs=[SM] + [VM] * 4,
        out_specs=VM,
        compiler_params=pltpu.CompilerParams(vmem_limit_bytes=8 << 20),
        cost_estimate=cost(1e+09, 1e+06),
        name="choose",
    )(sel, quarters, *got)


def gradient_kernel(*refs):
    sel, low, low_peer, high, high_peer, firsts, firsts_peer = refs[:7]
    seconds = refs[7:11]
    out, left, right, sems = refs[11:]
    pieces = [ref.at[i] for mine, peer in ((low, low_peer), (high, high_peer)) for i in range(2) for ref in (mine, peer)]
    copies = []
    for d in range(4):
        source = (sel[3, 0] + 4 - d) % 4
        for side in range(2):
            first = firsts_peer.at[source] if side else firsts.at[source, 0]
            for k, rows in enumerate((first, seconds[d].at[side])):
                lanes = pl.ds(pl.multiple_of(source * 512, 128) + (side * 2 + k) * 128, 128)
                copies.append(pltpu.make_async_copy(rows, left.at[:, lanes], sems.at[len(copies)]))
    for copy in copies:
        copy.start()
    quarter = low.shape[1] - 16
    for i, piece in enumerate(pieces):
        lanes = pl.ds(i * 256, 256)
        whole = piece[pl.ds(0, quarter), :].astype(F32)
        second = whole * piece[pl.ds(quarter, 16), :][0:1].astype(F32)
        right[pl.ds(0, quarter), lanes] = (whole - second).astype(BF16)
        right[pl.ds(quarter, quarter), lanes] = second.astype(BF16)
    for copy in copies:
        copy.wait()
    for m in range(left.shape[0] // TILE):
        part = dot(left[pl.ds(m * TILE, TILE), :], right[...], NT).astype(BF16)
        for i in range(4):
            at_chunk = m * 4 + i
            out[at_chunk // 8, at_chunk // 2 % 4, at_chunk % 2, pl.ds(0, 64), :] = part[i * 64 : i * 64 + 64]


def gradient(sel, firsts, firsts_peer, seconds, pieces):
    rows = firsts.shape[2]
    cols = 2 * (pieces[0].shape[1] - 16)
    return pl.pallas_call(
        gradient_kernel,
        out_shape=jax.ShapeDtypeStruct((2, 4, 2, 64, cols), BF16),
        in_specs=[SM] + [VM] * 4 + [HB] * 6,
        out_specs=VM,
        scratch_shapes=[
            pltpu.VMEM((rows, 2048), BF16),
            pltpu.VMEM((cols, 2048), BF16),
            pltpu.SemaphoreType.DMA((16,)),
        ],
        compiler_params=pltpu.CompilerParams(vmem_limit_bytes=20 << 20),
        cost_estimate=cost(9e+09, 2e+07),
        name="gradient",
    )(sel, *pieces, *[in_hbm(a) for a in (firsts, firsts_peer, *seconds)])


def adapter_kernel(nl, gg, nl_peer, gg_peer, out):
    width = nl.shape[-1] - 128
    for k in range(2):
        n = jnp.concatenate([nl[0, k], nl_peer[k]], axis=0)
        g = jnp.concatenate([gg[0, k], gg_peer[k]], axis=0)
        for i, (lhs, rhs) in enumerate(((n, g[:, width:]), (g, n[:, width:]))):
            term = dot(lhs[:, :width], rhs, TN).astype(BF16)
            rows = pl.ds((2 * i + k) * 16, 16)
            for r in range(16):
                for t in range(7):
                    out[r % 2, r // 8, (r // 2) % 4, rows, pl.ds(t * 128, 128)] = (
                        term[r * 112 + t * 16 : r * 112 + t * 16 + 16]
                    )


def adapter_terms(nl, gg, nl_peer, gg_peer):
    return pl.pallas_call(
        adapter_kernel,
        out_shape=jax.ShapeDtypeStruct((2, 2, 4, 64, 896), BF16),
        in_specs=[VM] * 4,
        out_specs=VM,
        compiler_params=pltpu.CompilerParams(vmem_limit_bytes=16 << 20),
        cost_estimate=cost(2e9, 4e6),
        name="adapter_terms",
    )(pinned(nl), pinned(gg), nl_peer, gg_peer)


def at(array, index):
    return lax.dynamic_index_in_dim(array, index, 0, keepdims=False)


def move(array, dy=0, dz=0, flip=0):
    pairs = []
    for x in range(4):
        for y in range(4):
            for z in range(4):
                for core in range(2):
                    to_y, to_z = (y + dy) % 4, (z + dz) % 4
                    src = (x * 2 + y // 2) * 16 + y % 2 * 8 + z * 2 + core
                    dst = (x * 2 + to_y // 2) * 16 + to_y % 2 * 8 + to_z * 2 + (core ^ flip)
                    pairs.append((src, dst))
    return lax.ppermute(array, ("pipe", "dp"), pairs)


def over_y(part):
    return lax.ppermute(part, "dp", [(i, i ^ 8) for i in range(16)]).astype(F32)


def over_z(part, zs):
    total = at(part, zs[0]).astype(F32)
    for d in range(1, 4):
        pairs = [(i, i // 8 * 8 + (i + 2 * d) % 8) for i in range(16)]
        total = total + lax.ppermute(at(part, zs[d]), "dp", pairs).astype(F32)
    return total


def over_cores(part, cores):
    got = lax.ppermute(at(part, cores[1]), "dp", [(i, i ^ 1) for i in range(16)])
    return (at(part, cores[0]).astype(F32) + got.astype(F32)).astype(BF16)


def shards(stored, common, down, up, selection, final_c):
    n_pipe, n_dp = lax.axis_size("pipe"), lax.axis_size("dp")
    together = lax.optimization_barrier
    p = lax.axis_index("pipe")
    r = lax.axis_index("dp")
    x_at, h, core = p // 2, p % 2, r % 2
    swap = [(i, i ^ 1) for i in range(n_pipe)]
    turns = [[(i, (i + 2 * d) % n_pipe) for i in range(n_pipe)] for d in range(4)]
    own = stored[0]
    rows, width = own.shape
    half = rows // 2
    a_own, u_own = down[0], up[0]
    rank = a_own.shape[-1]

    def swapped(array):
        return lax.ppermute(array, "pipe", swap)

    def onward(array):
        return lax.ppermute(array, "pipe", turns[1])

    def flip(array):
        return move(array, flip=1)

    def after(value, other):
        return together((value, other))[0]

    mixed = common.transpose(1, 0, 2)
    up_z, down_z = move(mixed, dz=1), move(mixed, dz=-1)
    y_a, y_b = move(mixed[0], dy=1), move(mixed[1], dy=-1)
    x_mine = lax.dynamic_slice_in_dim(own, h * half, half, 0)
    x_other = lax.dynamic_slice_in_dim(own, (1 - h) * half, half, 0)
    c = lax.dynamic_slice_in_dim(final_c, h * half, half, 0)
    marks = jnp.broadcast_to(jnp.pad(selection[0], (0, width - 2)).astype(BF16), (16, width))
    x_peer = swapped(jnp.concatenate([x_other, marks]))
    sel_peer = x_peer[half:, :2][:1].astype(F32).astype(jnp.int32)
    sel = jnp.concatenate([selection, sel_peer, jnp.stack([h, r, x_at, x_at]).astype(jnp.int32).reshape(2, 2)])
    entered = jnp.stack([x_mine, x_peer[:half]])
    near = move(jnp.where(core == 0, a_own, u_own), dy=2)
    first = first_rows(sel, entered)
    firsts = lax.all_gather(first, "pipe", axis_index_groups=[[0, 2, 4, 6], [1, 3, 5, 7]])
    up_z, down_z, y_a, y_b, sel, c, entered = together((up_z, down_z, y_a, y_b, sel, c, entered))
    yz_a, yz_b = move(up_z, dy=1), move(down_z, dy=-1)
    z_a, z_b = move(up_z[0], dz=1), move(down_z[1], dz=-1)
    flips = [flip(after(a, (z_a, z_b))) for a in (mixed, up_z, down_z)]
    flips += [flip(after(a, (yz_a, yz_b))) for a in (y_a, y_b)]
    yz_a, yz_b, z_a, z_b, flips, firsts = together((yz_a, yz_b, z_a, z_b, flips, firsts))
    firsts_peer = swapped(firsts[:, 1])
    yf_a, yf_b = move(yz_a[0], dz=1), move(yz_b[1], dz=-1)
    late = [flip(a) for a in (z_a, z_b, yz_a, yz_b, near)]
    yf_a, yf_b, late = together((yf_a, yf_b, late))
    flips += [*late[:4], flip(yf_a), flip(yf_b), late[4]]
    direct = (mixed, up_z, down_z, y_a, y_b, z_a, z_b, yz_a, yz_b, yf_a, yf_b)
    pieces = [q for pair in zip(direct, flips) for q in pair]
    z, y = (r // 2) % 4, r // 8
    places = ([core, 1 - core], [(z + d) % 4 for d in range(4)], [y, 1 - y])
    places += ([(x_at + d) % 4 for d in range(4)], [(x_at - s) % 4 for s in range(4)])
    places = [[index.astype(jnp.uint32) for index in group] for group in places]
    entered, firsts, places = together((entered, firsts, places))
    cores, zs, ys, xs, sources = places
    *kept, gg, second = forward(sel, entered, (a_own, u_own, near, flips[-1], *pieces))
    nl = kept[0]

    def hop(send, place):
        return lax.ppermute(send, "pipe", [(2 * place + i, 2 * place - 2 + i) for i in range(2)])

    def quarters_of(places, gg):
        parts = transposed(places, sel, gg)
        got = []
        for d in range(1, 4):
            pairs = [(2 * place + i, 2 * ((place + d) % 4) + i) for place in places for i in range(2)]
            got.append(lax.ppermute(parts[d], "pipe", pairs))
        return parts, got

    second_peer = swapped(second[1])
    gg, send = backward(3, sel, c, kept, gg)
    c = hop(send, 3)
    second_peer, gg, firsts_peer = together((second_peer, gg, firsts_peer))
    ring = [jnp.stack([second[0], second_peer])]
    ring.append(onward(ring[0]))
    gg, send = backward(2, sel, c, kept, gg)
    c = hop(send, 2)
    nl_peer = swapped(after(nl, gg)[1])
    gg, c = together((gg, c))
    parts, got = quarters_of((2, 3), gg)
    gg, send = backward(1, sel, c, kept, gg)
    c = hop(send, 1)
    got = [after(a, gg) for a in got]
    ring[1] = after(ring[1], gg)
    nl_peer = after(nl_peer, gg)
    ring.append(onward(ring[1]))
    high = choose((2, 3), sel, parts, got)
    high_peer = swapped(high)
    c, high = together((c, high))
    gg, _ = backward(0, sel, c, kept, gg)
    ring.append(onward(after(ring[2], gg)))
    high_peer, gg = together((high_peer, gg))
    parts, got = quarters_of((0, 1), gg)
    low = choose((0, 1), sel, parts, got)
    low_peer = swapped(low)
    gg_peer = swapped(gg[1, :2])
    pieces = (low, low_peer, high, high_peer)
    tile = gradient(sel, firsts, firsts_peer, ring, pieces)
    terms = over_cores(adapter_terms(nl, gg, nl_peer, gg_peer), cores)
    terms = (at(terms, ys[0]).astype(F32) + over_y(at(terms, ys[1]))).astype(BF16)
    terms = over_z(terms, zs)
    tile = over_z(over_cores(tile, cores), zs).astype(BF16)
    tile = at(tile, ys[0]).astype(F32) + over_y(at(tile, ys[1]))
    tile = tile.astype(BF16).reshape(4, 16, -1)
    ct = gg[:, 2, :, :width]
    placed = jnp.stack(
        [at(tile, xs[0])] + [lax.ppermute(at(tile, xs[d]), "pipe", turns[d]) for d in range(1, 4)]
    )
    placed = jnp.stack([at(placed, source) for source in sources], axis=1)
    each = width // (n_pipe * n_dp)
    shared = placed[:each].reshape(each, 4, 2, width // 4).transpose(0, 2, 1, 3)
    shared = shared.reshape(each, 2, width).astype(F32)

    ours, theirs = ct[0], swapped(ct[1])
    result = jnp.where(
        h == 0, jnp.concatenate([ours, theirs]), jnp.concatenate([theirs, ours])
    )
    both = terms.reshape(4, 16, 7, rank).transpose(0, 2, 1, 3).reshape(4, 112, rank)
    return result[None], shared, both[None, :2], both[None, 2:]


def solution(mesh):
    return jax.shard_map(
        shards,
        mesh=mesh,
        in_specs=(
            P("pipe", "dp", None),
            P("dp", None, None),
            P("pipe", None, None, None),
            P("pipe", None, None, None),
            P("pipe", None),
            P("dp", None),
        ),
        out_specs=(
            P("pipe", "dp", None),
            P(("pipe", "dp"), None, None),
            P("pipe", None, "dp", None),
            P("pipe", None, "dp", None),
        ),
        check_vma=False,
    )
```

```python
import functools

import jax
import jax.numpy as jnp
from jax import lax
from jax.experimental import pallas as pl
from jax.experimental.pallas import tpu as pltpu
from jax.sharding import PartitionSpec as P

EPS = 1e-06
TILE = 256
F32 = jnp.float32
BF16 = jnp.bfloat16
NT = (((1,), (1,)), ((), ()))
TN = (((0,), (0,)), ((), ()))
HB = pl.BlockSpec(memory_space=pltpu.HBM)
VM = pl.BlockSpec(memory_space=pltpu.VMEM)
SM = pl.BlockSpec(memory_space=pltpu.SMEM)


def dot(a, b, dims=(((1,), (0,)), ((), ()))):
    return lax.dot_general(a, b, dims, preferred_element_type=F32)


def cost(flops, bytes_accessed):
    return pl.CostEstimate(flops=int(flops), bytes_accessed=int(bytes_accessed), transcendentals=0)


def pinned(array):
    return pltpu.with_memory_space_constraint(array, pltpu.VMEM)


def in_hbm(array):
    return pltpu.with_memory_space_constraint(array, pltpu.HBM)


PIECES = ((0, 0, None), (0, 3, None), (0, 1, None), (1, 0, 0), (1, 0, 1), (0, 2, 0), (0, 2, 1)) + (
    (1, 3, 0), (1, 1, 1), (1, 3, 1), (1, 1, 0), (1, 2, 0), (1, 2, 1)
)


def row_blocks(src, tile, dst, h, lanes):
    width = src.shape[1]
    for t in range(width // TILE):
        tile[pl.ds(t * TILE, TILE), :] = src[:, t * TILE : (t + 1) * TILE].astype(F32).T
    tile[pl.ds(width, 8), :] = jnp.zeros((8, tile.shape[1]), F32)
    for p in range(8):
        x, half = p // 2, p % 2
        slot = jnp.bitwise_xor(h, half)
        for r in range(16):
            core, z, y = r % 2, (r // 2) % 4, r // 8
            at_row = (((core * 4 + z) * 2 + y) * 4 + x) * 16
            dst[slot, pl.ds(at_row, 16), lanes] = tile[pl.ds((p * 16 + r) * 14, 16), :].astype(BF16)


def first_kernel(sel, x, out, tile):
    rows = jnp.concatenate([x[0], x[1]], axis=0).astype(F32)
    sc = lax.rsqrt(jnp.mean(rows * rows, axis=-1, keepdims=True) + EPS)
    row_blocks((rows * sc).astype(BF16), tile, out, sel[2, 0], pl.ds(0, 128))


def first_rows(sel, x):
    width = x.shape[-1]
    return pl.pallas_call(
        first_kernel,
        out_shape=jax.ShapeDtypeStruct((2, 1024, 128), BF16),
        in_specs=[SM, VM],
        out_specs=VM,
        scratch_shapes=[pltpu.VMEM((width + 8, 128), F32)],
        compiler_params=pltpu.CompilerParams(vmem_limit_bytes=16 << 20),
        cost_estimate=cost(1e+09, 1e+06),
        name="first_rows",
    )(sel, x)


def forward_kernel(sel, x, *refs):
    a_own, u_own, near, far = refs[:4]
    pieces = refs[4 : 4 + 2 * len(PIECES)]
    nl, slope, scale, wt, auv, gg, out, wv, xs, tile, sems = refs[4 + 2 * len(PIECES) :]
    av, uv = auv.at[0], auv.at[1]
    width = x.shape[-1]
    per = pieces[0].shape[-2]
    h, r = sel[2, 0], sel[2, 1]
    core, z, y = r % 2, (r // 2) % 4, r // 8
    small = []
    for i, (src, dst) in enumerate(
        ((a_own, av.at[0]), (u_own, uv.at[0]), (near, auv.at[core, 1]), (far, auv.at[1 - core, 1]))
    ):
        small.append(pltpu.make_async_copy(src, dst, sems.at[32 + i]))
    for copy in small:
        copy.start()
    for block in range(2):
        for i, ref in enumerate(pieces):
            dy, dz, held = PIECES[i // 2]
            if held is not None and held != block:
                continue
            place = jnp.bitwise_xor(y, dy) * 8 + (z + dz) % 4 * 2 + jnp.bitwise_xor(core, i % 2)
            dst = wv.at[block, pl.ds(pl.multiple_of(place * per, 16), per), :]
            src = ref.at[block] if held is None else ref
            pltpu.make_async_copy(src, dst, sems.at[block * 16 + place]).start()
    big = []
    for block in range(2):
        for place in range(16):
            dst = wv.at[block, pl.ds(place * per, per), :]
            big.append(pltpu.make_async_copy(dst, dst, sems.at[block * 16 + place]))
    gg[...] = jnp.zeros_like(gg)
    for o in range(2):
        xs[o] = x[o]
    here = 0
    for block in range(2):
        for t in range(width // TILE):
            while here < 16 * block + min(16, -(-(t + 1) * TILE // per)):
                big[here].wait()
                here += 1
            wt[block, :, pl.ds(t * TILE, TILE)] = wv[block, pl.ds(t * TILE, TILE), :].T
    for copy in small:
        copy.wait()
    for k in range(2):
        rows = jnp.concatenate([xs[0], xs[1]], axis=0).astype(F32)
        sc = lax.rsqrt(jnp.mean(rows * rows, axis=-1, keepdims=True) + EPS)
        nm = (rows * sc).astype(BF16)
        if k == 1:
            row_blocks(nm, tile, out, h, pl.ds(0, 128))
        for o in range(2):
            part = slice(o * 64, (o + 1) * 64)
            scale[o, k] = jnp.broadcast_to(sc[part], scale.shape[2:])
            mine = nm[part]
            nl[o, k, :, pl.ds(0, width)] = mine
            low = dot(mine, av[o, k]).astype(BF16)
            nl[o, k, :, pl.ds(width, 128)] = low
            block = sel[o, k]
            for t in range(width // TILE):
                cols = pl.ds(t * TILE, TILE)
                pre = dot(mine, wv[block, :, cols]) + dot(low, uv[o, k, cols, :], NT)
                sigma = 1.0 / (1.0 + jnp.exp(-pre))
                slope[o, k, :, cols] = sigma * (1.0 + pre * (1.0 - sigma))
                if k == 0:
                    xs[o, :, cols] = (xs[o, :, cols].astype(F32) + pre * sigma).astype(BF16)


def forward(sel, x, weights):
    rows, width = x.shape[1:]
    rank = weights[0].shape[-1]
    return pl.pallas_call(
        forward_kernel,
        out_shape=(
            pltpu.VMEM((2, 2, rows, width + rank), BF16),
            pltpu.VMEM((2, 2, rows, width), F32),
            pltpu.VMEM((2, 2, rows, 128), F32),
            pltpu.VMEM((2, width, width), BF16),
            pltpu.VMEM((2, 2, 2, width, rank), BF16),
            pltpu.VMEM((2, 3, rows, width + rank), BF16),
            jax.ShapeDtypeStruct((2, 1024, 128), BF16),
        ),
        in_specs=[SM, VM] + [HB] * len(weights),
        out_specs=(VM,) * 7,
        scratch_shapes=[
            pltpu.VMEM((2, width, width), BF16),
            pltpu.VMEM((2, rows, width), BF16),
            pltpu.VMEM((width + 8, 128), F32),
            pltpu.SemaphoreType.DMA((36,)),
        ],
        compiler_params=pltpu.CompilerParams(vmem_limit_bytes=22 << 20),
        cost_estimate=cost(1.5e+10, 2e+07),
        name="forward",
    )(sel, x, *[in_hbm(w) for w in weights])


def backward_kernel(at_place, sel, c, nl, slope, scale, wt, auv, old_gg, gg, send, gn):
    width = c.shape[-1]
    av, uv = auv.at[0], auv.at[1]

    @pl.when(sel[3, 0] == at_place)
    def _():
        h = sel[2, 0]
        cur = c[...]
        for j in (1, 0):
            o = jnp.bitwise_xor(h, j)
            for k in (1, 0):
                c32 = cur.astype(F32)
                g = (c32 * slope[o, k]).astype(BF16)
                gg[o, k, :, pl.ds(0, width)] = g
                low = dot(g, uv[o, k]).astype(BF16)
                gg[o, k, :, pl.ds(width, 128)] = low
                block = sel[o, k]
                total = jnp.zeros((g.shape[0], 1), F32)
                for t in range(width // TILE):
                    cols = pl.ds(t * TILE, TILE)
                    part = dot(g, wt[block, :, cols]) + dot(low, av[o, k, cols, :], NT)
                    gn[:, cols] = part
                    total = total + jnp.sum(part * nl[o, k, :, cols].astype(F32), axis=-1, keepdims=True)
                mean = total / width
                z = nl[o, k, :, pl.ds(0, width)].astype(F32)
                sc = scale[o, k, :, 0:1]
                cur = (c32 + sc * (gn[...] - z * mean)).astype(BF16)
            gg[o, 2, :, pl.ds(0, width)] = cur
        send[...] = cur


def backward(at_place, sel, c, kept, gg):
    rows, width = c.shape
    kept = [pinned(a) for a in kept]
    return pl.pallas_call(
        functools.partial(backward_kernel, at_place),
        out_shape=(jax.ShapeDtypeStruct(gg.shape, BF16), jax.ShapeDtypeStruct((rows, width), BF16)),
        in_specs=[SM, VM] + [VM] * 6,
        out_specs=(VM, VM),
        scratch_shapes=[pltpu.VMEM((rows, width), F32)],
        input_output_aliases={7: 0},
        compiler_params=pltpu.CompilerParams(vmem_limit_bytes=6 << 20),
        cost_estimate=cost(9e+09, 2e+07),
        name="backward",
    )(sel, c, *kept, pinned(gg))


def transpose_kernel(places, sel, gp, out):
    quarter = (gp.shape[-1] - 128) // 4

    @pl.when((sel[3, 0] >= places[0]) & (sel[3, 0] <= places[-1]))
    def _():
        for k in range(2):
            lanes = pl.ds(k * 128, 128)
            both = jnp.concatenate([gp[0, k], gp[1, k]], axis=0)[:, : 4 * quarter]
            for q in range(4):
                d = (q + 4 - sel[3, 0]) % 4
                for t in range(0, quarter, 64):
                    out[d, pl.ds(t, 64), lanes] = both[:, q * quarter + t : q * quarter + t + 64].T
            side = lax.broadcasted_iota(jnp.int32, (16, 128), 1) // 64
            mark = jnp.where(side == 0, sel[0, k], sel[1, k])
            for q in range(4):
                out[q, pl.ds(quarter, 16), lanes] = mark.astype(F32).astype(BF16)


def transposed(places, sel, gp):
    quarter = (gp.shape[-1] - 128) // 4
    return pl.pallas_call(
        functools.partial(transpose_kernel, places),
        out_shape=jax.ShapeDtypeStruct((4, quarter + 16, 256), BF16),
        in_specs=[SM, VM],
        out_specs=VM,
        compiler_params=pltpu.CompilerParams(vmem_limit_bytes=6 << 20),
        cost_estimate=cost(1.8e+09, 4e+06),
        name="transposed",
    )(sel, pinned(gp))


def choose_kernel(places, sel, quarters, one, two, three, out):
    for i, place in enumerate(places):
        away = (sel[3, 0] + 4 - place) % 4

        @pl.when(away == 0)
        def _(i=i):
            out[i] = quarters[0]

        for d, got in ((1, one), (2, two), (3, three)):

            @pl.when(away == d)
            def _(i=i, got=got):
                out[i] = got[...]


def choose(places, sel, quarters, got):
    return pl.pallas_call(
        functools.partial(choose_kernel, places),
        out_shape=jax.ShapeDtypeStruct((len(places),) + quarters.shape[1:], BF16),
        in_specs=[SM] + [VM] * 4,
        out_specs=VM,
        compiler_params=pltpu.CompilerParams(vmem_limit_bytes=8 << 20),
        cost_estimate=cost(1e+09, 1e+06),
        name="choose",
    )(sel, quarters, *got)


def gradient_kernel(*refs):
    sel, low, low_peer, high, high_peer, firsts, firsts_peer = refs[:7]
    seconds = refs[7:11]
    out, left, right, sems = refs[11:]
    pieces = [ref.at[i] for mine, peer in ((low, low_peer), (high, high_peer)) for i in range(2) for ref in (mine, peer)]
    copies = []
    for d in range(4):
        source = (sel[3, 0] + 4 - d) % 4
        for side in range(2):
            first = firsts_peer.at[source] if side else firsts.at[source, 0]
            for k, rows in enumerate((first, seconds[d].at[side])):
                lanes = pl.ds(pl.multiple_of(source * 512, 128) + (side * 2 + k) * 128, 128)
                copies.append(pltpu.make_async_copy(rows, left.at[:, lanes], sems.at[len(copies)]))
    for copy in copies:
        copy.start()
    quarter = low.shape[1] - 16
    for i, piece in enumerate(pieces):
        lanes = pl.ds(i * 256, 256)
        whole = piece[pl.ds(0, quarter), :].astype(F32)
        second = whole * piece[pl.ds(quarter, 16), :][0:1].astype(F32)
        right[pl.ds(0, quarter), lanes] = (whole - second).astype(BF16)
        right[pl.ds(quarter, quarter), lanes] = second.astype(BF16)
    for copy in copies:
        copy.wait()
    for m in range(left.shape[0] // TILE):
        part = dot(left[pl.ds(m * TILE, TILE), :], right[...], NT).astype(BF16)
        for i in range(4):
            at_chunk = m * 4 + i
            out[at_chunk // 8, at_chunk // 2 % 4, at_chunk % 2, pl.ds(0, 64), :] = part[i * 64 : i * 64 + 64]


def gradient(sel, firsts, firsts_peer, seconds, pieces):
    rows = firsts.shape[2]
    cols = 2 * (pieces[0].shape[1] - 16)
    return pl.pallas_call(
        gradient_kernel,
        out_shape=jax.ShapeDtypeStruct((2, 4, 2, 64, cols), BF16),
        in_specs=[SM] + [VM] * 4 + [HB] * 6,
        out_specs=VM,
        scratch_shapes=[
            pltpu.VMEM((rows, 2048), BF16),
            pltpu.VMEM((cols, 2048), BF16),
            pltpu.SemaphoreType.DMA((16,)),
        ],
        compiler_params=pltpu.CompilerParams(vmem_limit_bytes=20 << 20),
        cost_estimate=cost(9e+09, 2e+07),
        name="gradient",
    )(sel, *pieces, *[in_hbm(a) for a in (firsts, firsts_peer, *seconds)])


def adapter_kernel(nl, gg, nl_peer, gg_peer, out):
    width = nl.shape[-1] - 128
    for k in range(2):
        n = jnp.concatenate([nl[0, k], nl_peer[k]], axis=0)
        g = jnp.concatenate([gg[0, k], gg_peer[k]], axis=0)
        for i, (lhs, rhs) in enumerate(((n, g[:, width:]), (g, n[:, width:]))):
            term = dot(lhs[:, :width], rhs, TN).astype(BF16)
            rows = pl.ds((2 * i + k) * 16, 16)
            for r in range(16):
                for t in range(7):
                    out[r % 2, r // 8, (r // 2) % 4, rows, pl.ds(t * 128, 128)] = (
                        term[r * 112 + t * 16 : r * 112 + t * 16 + 16]
                    )


def adapter_terms(nl, gg, nl_peer, gg_peer):
    return pl.pallas_call(
        adapter_kernel,
        out_shape=jax.ShapeDtypeStruct((2, 2, 4, 64, 896), BF16),
        in_specs=[VM] * 4,
        out_specs=VM,
        compiler_params=pltpu.CompilerParams(vmem_limit_bytes=16 << 20),
        cost_estimate=cost(2e9, 4e6),
        name="adapter_terms",
    )(pinned(nl), pinned(gg), nl_peer, gg_peer)


def at(array, index):
    return lax.dynamic_index_in_dim(array, index, 0, keepdims=False)


def move(array, dy=0, dz=0, flip=0):
    pairs = []
    for x in range(4):
        for y in range(4):
            for z in range(4):
                for core in range(2):
                    to_y, to_z = (y + dy) % 4, (z + dz) % 4
                    src = (x * 2 + y // 2) * 16 + y % 2 * 8 + z * 2 + core
                    dst = (x * 2 + to_y // 2) * 16 + to_y % 2 * 8 + to_z * 2 + (core ^ flip)
                    pairs.append((src, dst))
    return lax.ppermute(array, ("pipe", "dp"), pairs)


def over_y(part):
    return lax.ppermute(part, "dp", [(i, i ^ 8) for i in range(16)]).astype(F32)


def over_z(part, zs):
    total = at(part, zs[0]).astype(F32)
    for d in range(1, 4):
        pairs = [(i, i // 8 * 8 + (i + 2 * d) % 8) for i in range(16)]
        total = total + lax.ppermute(at(part, zs[d]), "dp", pairs).astype(F32)
    return total


def over_cores(part, cores):
    got = lax.ppermute(at(part, cores[1]), "dp", [(i, i ^ 1) for i in range(16)])
    return (at(part, cores[0]).astype(F32) + got.astype(F32)).astype(BF16)


def shards(stored, common, down, up, selection, final_c):
    n_pipe, n_dp = lax.axis_size("pipe"), lax.axis_size("dp")
    together = lax.optimization_barrier
    p = lax.axis_index("pipe")
    r = lax.axis_index("dp")
    x_at, h, core = p // 2, p % 2, r % 2
    swap = [(i, i ^ 1) for i in range(n_pipe)]
    turns = [[(i, (i + 2 * d) % n_pipe) for i in range(n_pipe)] for d in range(4)]
    own = stored[0]
    rows, width = own.shape
    half = rows // 2
    a_own, u_own = down[0], up[0]
    rank = a_own.shape[-1]

    def swapped(array):
        return lax.ppermute(array, "pipe", swap)

    def onward(array):
        return lax.ppermute(array, "pipe", turns[1])

    def flip(array):
        return move(array, flip=1)

    def after(value, other):
        return together((value, other))[0]

    mixed = common.transpose(1, 0, 2)
    up_z, down_z = move(mixed, dz=1), move(mixed, dz=-1)
    y_a, y_b = move(mixed[0], dy=1), move(mixed[1], dy=-1)
    x_mine = lax.dynamic_slice_in_dim(own, h * half, half, 0)
    x_other = lax.dynamic_slice_in_dim(own, (1 - h) * half, half, 0)
    c = lax.dynamic_slice_in_dim(final_c, h * half, half, 0)
    marks = jnp.broadcast_to(jnp.pad(selection[0], (0, width - 2)).astype(BF16), (16, width))
    x_peer = swapped(jnp.concatenate([x_other, marks]))
    sel_peer = x_peer[half:, :2][:1].astype(F32).astype(jnp.int32)
    sel = jnp.concatenate([selection, sel_peer, jnp.stack([h, r, x_at, x_at]).astype(jnp.int32).reshape(2, 2)])
    entered = jnp.stack([x_mine, x_peer[:half]])
    near = move(jnp.where(core == 0, a_own, u_own), dy=2)
    first = first_rows(sel, entered)
    firsts = lax.all_gather(first, "pipe", axis_index_groups=[[0, 2, 4, 6], [1, 3, 5, 7]])
    up_z, down_z, y_a, y_b, sel, c, entered = together((up_z, down_z, y_a, y_b, sel, c, entered))
    up_0, down_1 = up_z[0], down_z[1]
    yz_a, yz_b = move(up_0, dy=1), move(down_1, dy=-1)
    z_a, z_b = move(up_0, dz=1), move(down_1, dz=-1)
    zy_a, zy_b = move(y_b, dz=1), move(y_a, dz=-1)
    flips = [flip(after(a, (z_a, z_b))) for a in (mixed, up_z, down_z)]
    flips += [flip(after(a, (yz_a, yz_b))) for a in (y_a, y_b)]
    yz_a, yz_b, z_a, z_b, zy_a, zy_b, flips, firsts = together((yz_a, yz_b, z_a, z_b, zy_a, zy_b, flips, firsts))
    firsts_peer = swapped(firsts[:, 1])
    yf_a, yf_b = move(yz_a, dz=1), move(yz_b, dz=-1)
    late = [flip(a) for a in (z_a, z_b, yz_a, yz_b, zy_a, zy_b, near)]
    yf_a, yf_b, late = together((yf_a, yf_b, late))
    flips += [*late[:6], flip(yf_a), flip(yf_b), late[6]]
    direct = (mixed, up_z, down_z, y_a, y_b, z_a, z_b, yz_a, yz_b, zy_a, zy_b, yf_a, yf_b)
    pieces = [q for pair in zip(direct, flips) for q in pair]
    z, y = (r // 2) % 4, r // 8
    places = ([core, 1 - core], [(z + d) % 4 for d in range(4)], [y, 1 - y])
    places += ([(x_at + d) % 4 for d in range(4)], [(x_at - s) % 4 for s in range(4)])
    places = [[index.astype(jnp.uint32) for index in group] for group in places]
    entered, firsts, places = together((entered, firsts, places))
    cores, zs, ys, xs, sources = places
    *kept, gg, second = forward(sel, entered, (a_own, u_own, near, flips[-1], *pieces))
    nl = kept[0]

    def hop(send, place):
        return lax.ppermute(send, "pipe", [(2 * place + i, 2 * place - 2 + i) for i in range(2)])

    def quarters_of(places, gg):
        parts = transposed(places, sel, gg)
        got = []
        for d in range(1, 4):
            pairs = [(2 * place + i, 2 * ((place + d) % 4) + i) for place in places for i in range(2)]
            got.append(lax.ppermute(parts[d], "pipe", pairs))
        return parts, got

    second_peer = swapped(second[1])
    gg, send = backward(3, sel, c, kept, gg)
    c = hop(send, 3)
    second_peer, gg, firsts_peer = together((second_peer, gg, firsts_peer))
    ring = [jnp.stack([second[0], second_peer])]
    ring.append(onward(ring[0]))
    gg, send = backward(2, sel, c, kept, gg)
    c = hop(send, 2)
    nl_peer = swapped(after(nl, gg)[1])
    gg, c = together((gg, c))
    parts, got = quarters_of((2, 3), gg)
    gg, send = backward(1, sel, c, kept, gg)
    c = hop(send, 1)
    got = [after(a, gg) for a in got]
    ring[1] = after(ring[1], gg)
    nl_peer = after(nl_peer, gg)
    ring.append(onward(ring[1]))
    high = choose((2, 3), sel, parts, got)
    high_peer = swapped(high)
    c, high = together((c, high))
    gg, _ = backward(0, sel, c, kept, gg)
    ring.append(onward(after(ring[2], gg)))
    high_peer, gg = together((high_peer, gg))
    parts, got = quarters_of((0, 1), gg)
    low = choose((0, 1), sel, parts, got)
    low_peer = swapped(low)
    gg_peer = swapped(gg[1])
    pieces = (low, low_peer, high, high_peer)
    tile = gradient(sel, firsts, firsts_peer, ring, pieces)
    terms = over_cores(adapter_terms(nl, gg, nl_peer, gg_peer), cores)
    terms = (at(terms, ys[0]).astype(F32) + over_y(at(terms, ys[1]))).astype(BF16)
    terms = over_z(terms, zs)
    tile = over_z(over_cores(tile, cores), zs).astype(BF16)
    tile = at(tile, ys[0]).astype(F32) + over_y(at(tile, ys[1]))
    tile = tile.astype(BF16).reshape(4, 16, -1)
    placed = jnp.stack(
        [at(tile, xs[0])] + [lax.ppermute(at(tile, xs[d]), "pipe", turns[d]) for d in range(1, 4)]
    )
    placed = jnp.stack([at(placed, source) for source in sources], axis=1)
    each = width // (n_pipe * n_dp)
    shared = placed[:each].reshape(each, 4, 2, width // 4).transpose(0, 2, 1, 3)
    shared = shared.reshape(each, 2, width).astype(F32)

    ours, theirs = gg[0, 2, :, :width], gg_peer[2, :, :width]
    result = jnp.where(
        h == 0, jnp.concatenate([ours, theirs]), jnp.concatenate([theirs, ours])
    )
    both = terms.reshape(4, 16, 7, rank).transpose(0, 2, 1, 3).reshape(4, 112, rank)
    return result[None], shared, both[None, :2], both[None, 2:]


def solution(mesh):
    return jax.shard_map(
        shards,
        mesh=mesh,
        in_specs=(
            P("pipe", "dp", None),
            P("dp", None, None),
            P("pipe", None, None, None),
            P("pipe", None, None, None),
            P("pipe", None),
            P("dp", None),
        ),
        out_specs=(
            P("pipe", "dp", None),
            P(("pipe", "dp"), None, None),
            P("pipe", None, "dp", None),
            P("pipe", None, "dp", None),
        ),
        check_vma=False,
    )
```

```python
import functools

import jax
import jax.numpy as jnp
from jax import lax
from jax.experimental import pallas as pl
from jax.experimental.pallas import tpu as pltpu
from jax.sharding import PartitionSpec as P

EPS = 1e-06
TILE = 256
F32 = jnp.float32
BF16 = jnp.bfloat16
NT = (((1,), (1,)), ((), ()))
TN = (((0,), (0,)), ((), ()))
HB = pl.BlockSpec(memory_space=pltpu.HBM)
VM = pl.BlockSpec(memory_space=pltpu.VMEM)
SM = pl.BlockSpec(memory_space=pltpu.SMEM)


def dot(a, b, dims=(((1,), (0,)), ((), ()))):
    return lax.dot_general(a, b, dims, preferred_element_type=F32)


def cost(flops, bytes_accessed):
    return pl.CostEstimate(flops=int(flops), bytes_accessed=int(bytes_accessed), transcendentals=0)


def pinned(array):
    return pltpu.with_memory_space_constraint(array, pltpu.VMEM)


def in_hbm(array):
    return pltpu.with_memory_space_constraint(array, pltpu.HBM)


PIECES = ((0, 0, None), (0, 3, None), (0, 1, None), (1, 0, 0), (1, 0, 1), (0, 2, 0), (0, 2, 1)) + (
    (1, 3, None), (1, 1, None), (1, 2, 0), (1, 2, 1)
)


def row_blocks(src, tile, dst, h, lanes):
    width = src.shape[1]
    for t in range(width // TILE):
        tile[pl.ds(t * TILE, TILE), :] = src[:, t * TILE : (t + 1) * TILE].astype(F32).T
    tile[pl.ds(width, 8), :] = jnp.zeros((8, tile.shape[1]), F32)
    for p in range(8):
        x, half = p // 2, p % 2
        slot = jnp.bitwise_xor(h, half)
        for r in range(16):
            core, z, y = r % 2, (r // 2) % 4, r // 8
            at_row = (((core * 4 + z) * 2 + y) * 4 + x) * 16
            dst[slot, pl.ds(at_row, 16), lanes] = tile[pl.ds((p * 16 + r) * 14, 16), :].astype(BF16)


def first_kernel(sel, x, out, tile):
    rows = jnp.concatenate([x[0], x[1]], axis=0).astype(F32)
    sc = lax.rsqrt(jnp.mean(rows * rows, axis=-1, keepdims=True) + EPS)
    row_blocks((rows * sc).astype(BF16), tile, out, sel[2, 0], pl.ds(0, 128))


def first_rows(sel, x):
    width = x.shape[-1]
    return pl.pallas_call(
        first_kernel,
        out_shape=jax.ShapeDtypeStruct((2, 1024, 128), BF16),
        in_specs=[SM, VM],
        out_specs=VM,
        scratch_shapes=[pltpu.VMEM((width + 8, 128), F32)],
        compiler_params=pltpu.CompilerParams(vmem_limit_bytes=16 << 20),
        cost_estimate=cost(1e+09, 1e+06),
        name="first_rows",
    )(sel, x)


def forward_kernel(sel, x, *refs):
    a_own, u_own, near, far = refs[:4]
    pieces = refs[4 : 4 + 2 * len(PIECES)]
    nl, slope, scale, wt, auv, gg, out, wv, xs, tile, sems = refs[4 + 2 * len(PIECES) :]
    av, uv = auv.at[0], auv.at[1]
    width = x.shape[-1]
    per = pieces[0].shape[-2]
    h, r = sel[2, 0], sel[2, 1]
    core, z, y = r % 2, (r // 2) % 4, r // 8
    small = []
    for i, (src, dst) in enumerate(
        ((a_own, av.at[0]), (u_own, uv.at[0]), (near, auv.at[core, 1]), (far, auv.at[1 - core, 1]))
    ):
        small.append(pltpu.make_async_copy(src, dst, sems.at[32 + i]))
    for copy in small:
        copy.start()
    for block in range(2):
        for i, ref in enumerate(pieces):
            dy, dz, held = PIECES[i // 2]
            if held is not None and held != block:
                continue
            place = jnp.bitwise_xor(y, dy) * 8 + (z + dz) % 4 * 2 + jnp.bitwise_xor(core, i % 2)
            dst = wv.at[block, pl.ds(pl.multiple_of(place * per, 16), per), :]
            src = ref.at[block] if held is None else ref
            pltpu.make_async_copy(src, dst, sems.at[block * 16 + place]).start()
    big = []
    for block in range(2):
        for place in range(16):
            dst = wv.at[block, pl.ds(place * per, per), :]
            big.append(pltpu.make_async_copy(dst, dst, sems.at[block * 16 + place]))
    gg[...] = jnp.zeros_like(gg)
    for o in range(2):
        xs[o] = x[o]
    here = 0
    for block in range(2):
        for t in range(width // TILE):
            while here < 16 * block + min(16, -(-(t + 1) * TILE // per)):
                big[here].wait()
                here += 1
            wt[block, :, pl.ds(t * TILE, TILE)] = wv[block, pl.ds(t * TILE, TILE), :].T
    for copy in small:
        copy.wait()
    for k in range(2):
        rows = jnp.concatenate([xs[0], xs[1]], axis=0).astype(F32)
        sc = lax.rsqrt(jnp.mean(rows * rows, axis=-1, keepdims=True) + EPS)
        nm = (rows * sc).astype(BF16)
        if k == 1:
            row_blocks(nm, tile, out, h, pl.ds(0, 128))
        for o in range(2):
            part = slice(o * 64, (o + 1) * 64)
            scale[o, k] = jnp.broadcast_to(sc[part], scale.shape[2:])
            mine = nm[part]
            nl[o, k, :, pl.ds(0, width)] = mine
            low = dot(mine, av[o, k]).astype(BF16)
            nl[o, k, :, pl.ds(width, 128)] = low
            block = sel[o, k]
            for t in range(width // TILE):
                cols = pl.ds(t * TILE, TILE)
                pre = dot(mine, wv[block, :, cols]) + dot(low, uv[o, k, cols, :], NT)
                sigma = 1.0 / (1.0 + jnp.exp(-pre))
                slope[o, k, :, cols] = sigma * (1.0 + pre * (1.0 - sigma))
                if k == 0:
                    xs[o, :, cols] = (xs[o, :, cols].astype(F32) + pre * sigma).astype(BF16)


def forward(sel, x, weights):
    rows, width = x.shape[1:]
    rank = weights[0].shape[-1]
    return pl.pallas_call(
        forward_kernel,
        out_shape=(
            pltpu.VMEM((2, 2, rows, width + rank), BF16),
            pltpu.VMEM((2, 2, rows, width), F32),
            pltpu.VMEM((2, 2, rows, 128), F32),
            pltpu.VMEM((2, width, width), BF16),
            pltpu.VMEM((2, 2, 2, width, rank), BF16),
            pltpu.VMEM((2, 3, rows, width + rank), BF16),
            jax.ShapeDtypeStruct((2, 1024, 128), BF16),
        ),
        in_specs=[SM, VM] + [HB] * len(weights),
        out_specs=(VM,) * 7,
        scratch_shapes=[
            pltpu.VMEM((2, width, width), BF16),
            pltpu.VMEM((2, rows, width), BF16),
            pltpu.VMEM((width + 8, 128), F32),
            pltpu.SemaphoreType.DMA((36,)),
        ],
        compiler_params=pltpu.CompilerParams(vmem_limit_bytes=22 << 20),
        cost_estimate=cost(1.5e+10, 2e+07),
        name="forward",
    )(sel, x, *[in_hbm(w) for w in weights])


def backward_kernel(at_place, sel, c, nl, slope, scale, wt, auv, old_gg, gg, send, gn):
    width = c.shape[-1]
    av, uv = auv.at[0], auv.at[1]

    @pl.when(sel[3, 0] == at_place)
    def _():
        h = sel[2, 0]
        cur = c[...]
        for j in (1, 0):
            o = jnp.bitwise_xor(h, j)
            for k in (1, 0):
                c32 = cur.astype(F32)
                g = (c32 * slope[o, k]).astype(BF16)
                gg[o, k, :, pl.ds(0, width)] = g
                low = dot(g, uv[o, k]).astype(BF16)
                gg[o, k, :, pl.ds(width, 128)] = low
                block = sel[o, k]
                total = jnp.zeros((g.shape[0], 1), F32)
                for t in range(width // TILE):
                    cols = pl.ds(t * TILE, TILE)
                    part = dot(g, wt[block, :, cols]) + dot(low, av[o, k, cols, :], NT)
                    gn[:, cols] = part
                    total = total + jnp.sum(part * nl[o, k, :, cols].astype(F32), axis=-1, keepdims=True)
                mean = total / width
                z = nl[o, k, :, pl.ds(0, width)].astype(F32)
                sc = scale[o, k, :, 0:1]
                cur = (c32 + sc * (gn[...] - z * mean)).astype(BF16)
            gg[o, 2, :, pl.ds(0, width)] = cur
        send[...] = cur


def backward(at_place, sel, c, kept, gg):
    rows, width = c.shape
    kept = [pinned(a) for a in kept]
    return pl.pallas_call(
        functools.partial(backward_kernel, at_place),
        out_shape=(jax.ShapeDtypeStruct(gg.shape, BF16), jax.ShapeDtypeStruct((rows, width), BF16)),
        in_specs=[SM, VM] + [VM] * 6,
        out_specs=(VM, VM),
        scratch_shapes=[pltpu.VMEM((rows, width), F32)],
        input_output_aliases={7: 0},
        compiler_params=pltpu.CompilerParams(vmem_limit_bytes=6 << 20),
        cost_estimate=cost(9e+09, 2e+07),
        name="backward",
    )(sel, c, *kept, pinned(gg))


def transpose_kernel(places, sel, gp, out):
    quarter = (gp.shape[-1] - 128) // 4

    @pl.when((sel[3, 0] >= places[0]) & (sel[3, 0] <= places[-1]))
    def _():
        for k in range(2):
            lanes = pl.ds(k * 128, 128)
            both = jnp.concatenate([gp[0, k], gp[1, k]], axis=0)[:, : 4 * quarter]
            for q in range(4):
                d = (q + 4 - sel[3, 0]) % 4
                for t in range(0, quarter, 64):
                    out[d, pl.ds(t, 64), lanes] = both[:, q * quarter + t : q * quarter + t + 64].T
            side = lax.broadcasted_iota(jnp.int32, (16, 128), 1) // 64
            mark = jnp.where(side == 0, sel[0, k], sel[1, k])
            for q in range(4):
                out[q, pl.ds(quarter, 16), lanes] = mark.astype(F32).astype(BF16)


def transposed(places, sel, gp):
    quarter = (gp.shape[-1] - 128) // 4
    return pl.pallas_call(
        functools.partial(transpose_kernel, places),
        out_shape=jax.ShapeDtypeStruct((4, quarter + 16, 256), BF16),
        in_specs=[SM, VM],
        out_specs=VM,
        compiler_params=pltpu.CompilerParams(vmem_limit_bytes=6 << 20),
        cost_estimate=cost(1.8e+09, 4e+06),
        name="transposed",
    )(sel, pinned(gp))


def choose_kernel(places, sel, quarters, one, two, three, out):
    for i, place in enumerate(places):
        away = (sel[3, 0] + 4 - place) % 4

        @pl.when(away == 0)
        def _(i=i):
            out[i] = quarters[0]

        for d, got in ((1, one), (2, two), (3, three)):

            @pl.when(away == d)
            def _(i=i, got=got):
                out[i] = got[...]


def choose(places, sel, quarters, got):
    return pl.pallas_call(
        functools.partial(choose_kernel, places),
        out_shape=jax.ShapeDtypeStruct((len(places),) + quarters.shape[1:], BF16),
        in_specs=[SM] + [VM] * 4,
        out_specs=VM,
        compiler_params=pltpu.CompilerParams(vmem_limit_bytes=8 << 20),
        cost_estimate=cost(1e+09, 1e+06),
        name="choose",
    )(sel, quarters, *got)


def gradient_kernel(*refs):
    sel, low, low_peer, high, high_peer, firsts, firsts_peer = refs[:7]
    seconds = refs[7:11]
    mine, sent, left, right, sems = refs[11:]
    pieces = [ref.at[i] for mine, peer in ((low, low_peer), (high, high_peer)) for i in range(2) for ref in (mine, peer)]
    copies = []
    for d in range(4):
        source = (sel[3, 0] + 4 - d) % 4
        for side in range(2):
            first = firsts_peer.at[source] if side else firsts.at[source, 0]
            for k, rows in enumerate((first, seconds[d].at[side])):
                lanes = pl.ds(pl.multiple_of(source * 512, 128) + (side * 2 + k) * 128, 128)
                copies.append(pltpu.make_async_copy(rows, left.at[:, lanes], sems.at[len(copies)]))
    for copy in copies:
        copy.start()
    quarter = low.shape[1] - 16
    for i, piece in enumerate(pieces):
        lanes = pl.ds(i * 256, 256)
        whole = piece[pl.ds(0, quarter), :].astype(F32)
        second = whole * piece[pl.ds(quarter, 16), :][0:1].astype(F32)
        right[pl.ds(0, quarter), lanes] = (whole - second).astype(BF16)
        right[pl.ds(quarter, quarter), lanes] = second.astype(BF16)
    for copy in copies:
        copy.wait()
    for m in range(left.shape[0] // TILE):
        part = dot(left[pl.ds(m * TILE, TILE), :], right[...], NT).astype(BF16)
        for i in range(4):
            chunk = m * 4 + i
            whole = part[i * 64 : i * 64 + 64]

            @pl.when(sel[2, 1] % 2 == chunk // 8)
            def _(chunk=chunk, whole=whole):
                mine[chunk // 2 % 4, chunk % 2] = whole

            @pl.when(sel[2, 1] % 2 != chunk // 8)
            def _(chunk=chunk, whole=whole):
                sent[chunk // 2 % 4, chunk % 2] = whole


def gradient(sel, firsts, firsts_peer, seconds, pieces):
    rows = firsts.shape[2]
    cols = 2 * (pieces[0].shape[1] - 16)
    return pl.pallas_call(
        gradient_kernel,
        out_shape=(jax.ShapeDtypeStruct((4, 2, 64, cols), BF16),) * 2,
        in_specs=[SM] + [VM] * 4 + [HB] * 6,
        out_specs=(VM, VM),
        scratch_shapes=[
            pltpu.VMEM((rows, 2048), BF16),
            pltpu.VMEM((cols, 2048), BF16),
            pltpu.SemaphoreType.DMA((16,)),
        ],
        compiler_params=pltpu.CompilerParams(vmem_limit_bytes=20 << 20),
        cost_estimate=cost(9e+09, 2e+07),
        name="gradient",
    )(sel, *pieces, *[in_hbm(a) for a in (firsts, firsts_peer, *seconds)])


def adapter_kernel(nl, gg, nl_peer, gg_peer, out):
    width = nl.shape[-1] - 128
    for k in range(2):
        n = jnp.concatenate([nl[0, k], nl_peer[k]], axis=0)
        g = jnp.concatenate([gg[0, k], gg_peer[k]], axis=0)
        for i, (lhs, rhs) in enumerate(((n, g[:, width:]), (g, n[:, width:]))):
            term = dot(lhs[:, :width], rhs, TN).astype(BF16)
            rows = pl.ds((2 * i + k) * 16, 16)
            for r in range(16):
                for t in range(7):
                    out[r % 2, r // 8, (r // 2) % 4, rows, pl.ds(t * 128, 128)] = (
                        term[r * 112 + t * 16 : r * 112 + t * 16 + 16]
                    )


def adapter_terms(nl, gg, nl_peer, gg_peer):
    return pl.pallas_call(
        adapter_kernel,
        out_shape=jax.ShapeDtypeStruct((2, 2, 4, 64, 896), BF16),
        in_specs=[VM] * 4,
        out_specs=VM,
        compiler_params=pltpu.CompilerParams(vmem_limit_bytes=16 << 20),
        cost_estimate=cost(2e9, 4e6),
        name="adapter_terms",
    )(pinned(nl), pinned(gg), nl_peer, gg_peer)


def at(array, index):
    return lax.dynamic_index_in_dim(array, index, 0, keepdims=False)


def move(array, dy=0, dz=0, flip=0):
    pairs = []
    for x in range(4):
        for y in range(4):
            for z in range(4):
                for core in range(2):
                    to_y, to_z = (y + dy) % 4, (z + dz) % 4
                    src = (x * 2 + y // 2) * 16 + y % 2 * 8 + z * 2 + core
                    dst = (x * 2 + to_y // 2) * 16 + to_y % 2 * 8 + to_z * 2 + (core ^ flip)
                    pairs.append((src, dst))
    return lax.ppermute(array, ("pipe", "dp"), pairs)


def over_y(part):
    return lax.ppermute(part, "dp", [(i, i ^ 8) for i in range(16)]).astype(F32)


def over_z(part, zs):
    total = at(part, zs[0]).astype(F32)
    for d in range(1, 4):
        pairs = [(i, i // 8 * 8 + (i + 2 * d) % 8) for i in range(16)]
        total = total + lax.ppermute(at(part, zs[d]), "dp", pairs).astype(F32)
    return total


def over_cores(mine, sent):
    got = lax.ppermute(sent, "dp", [(i, i ^ 1) for i in range(16)])
    return (mine.astype(F32) + got.astype(F32)).astype(BF16)


def shards(stored, common, down, up, selection, final_c):
    n_pipe, n_dp = lax.axis_size("pipe"), lax.axis_size("dp")
    together = lax.optimization_barrier
    p = lax.axis_index("pipe")
    r = lax.axis_index("dp")
    x_at, h, core = p // 2, p % 2, r % 2
    swap = [(i, i ^ 1) for i in range(n_pipe)]
    turns = [[(i, (i + 2 * d) % n_pipe) for i in range(n_pipe)] for d in range(4)]
    own = stored[0]
    rows, width = own.shape
    half = rows // 2
    a_own, u_own = down[0], up[0]
    rank = a_own.shape[-1]

    def swapped(array):
        return lax.ppermute(array, "pipe", swap)

    def onward(array):
        return lax.ppermute(array, "pipe", turns[1])

    def flip(array):
        return move(array, flip=1)

    def after(value, other):
        return together((value, other))[0]

    mixed = common.transpose(1, 0, 2)
    up_z, down_z = move(mixed, dz=1), move(mixed, dz=-1)
    y_a, y_b = move(mixed[0], dy=1), move(mixed[1], dy=-1)
    x_mine = lax.dynamic_slice_in_dim(own, h * half, half, 0)
    x_other = lax.dynamic_slice_in_dim(own, (1 - h) * half, half, 0)
    c = lax.dynamic_slice_in_dim(final_c, h * half, half, 0)
    marks = jnp.broadcast_to(jnp.pad(selection[0], (0, width - 2)).astype(BF16), (16, width))
    x_peer = swapped(jnp.concatenate([x_other, marks]))
    sel_peer = x_peer[half:, :2][:1].astype(F32).astype(jnp.int32)
    sel = jnp.concatenate([selection, sel_peer, jnp.stack([h, r, x_at, x_at]).astype(jnp.int32).reshape(2, 2)])
    entered = jnp.stack([x_mine, x_peer[:half]])
    near = move(jnp.where(core == 0, a_own, u_own), dy=2)
    first = first_rows(sel, entered)
    firsts = lax.all_gather(first, "pipe", axis_index_groups=[[0, 2, 4, 6], [1, 3, 5, 7]])
    up_z, down_z, y_a, y_b, sel, c, entered = together((up_z, down_z, y_a, y_b, sel, c, entered))
    yz_a, yz_b = move(up_z, dy=1), move(down_z, dy=-1)
    z_a, z_b = move(up_z[0], dz=1), move(down_z[1], dz=-1)
    flips = [flip(after(a, (z_a, z_b))) for a in (mixed, up_z, down_z)]
    flips += [flip(after(a, (yz_a, yz_b))) for a in (y_a, y_b)]
    yz_a, yz_b, z_a, z_b, flips, firsts = together((yz_a, yz_b, z_a, z_b, flips, firsts))
    firsts_peer = swapped(firsts[:, 1])
    yf_a, yf_b = move(yz_a[0], dz=1), move(yz_b[1], dz=-1)
    late = [flip(a) for a in (z_a, z_b, yz_a, yz_b, near)]
    yf_a, yf_b, late = together((yf_a, yf_b, late))
    flips += [*late[:4], flip(yf_a), flip(yf_b), late[4]]
    direct = (mixed, up_z, down_z, y_a, y_b, z_a, z_b, yz_a, yz_b, yf_a, yf_b)
    pieces = [q for pair in zip(direct, flips) for q in pair]
    z, y = (r // 2) % 4, r // 8
    places = ([core, 1 - core], [(z + d) % 4 for d in range(4)], [y, 1 - y])
    places += ([(x_at + d) % 4 for d in range(4)], [(x_at - s) % 4 for s in range(4)])
    places = [[index.astype(jnp.uint32) for index in group] for group in places]
    entered, firsts, places = together((entered, firsts, places))
    cores, zs, ys, xs, sources = places
    *kept, gg, second = forward(sel, entered, (a_own, u_own, near, flips[-1], *pieces))
    nl = kept[0]

    def hop(send, place):
        return lax.ppermute(send, "pipe", [(2 * place + i, 2 * place - 2 + i) for i in range(2)])

    def quarters_of(places, gg):
        parts = transposed(places, sel, gg)
        got = []
        for d in range(1, 4):
            pairs = [(2 * place + i, 2 * ((place + d) % 4) + i) for place in places for i in range(2)]
            got.append(lax.ppermute(parts[d], "pipe", pairs))
        return parts, got

    second_peer = swapped(second[1])
    gg, send = backward(3, sel, c, kept, gg)
    c = hop(send, 3)
    second_peer, gg, firsts_peer = together((second_peer, gg, firsts_peer))
    ring = [jnp.stack([second[0], second_peer])]
    ring.append(onward(ring[0]))
    gg, send = backward(2, sel, c, kept, gg)
    c = hop(send, 2)
    nl_peer = swapped(after(nl, gg)[1])
    gg, c = together((gg, c))
    parts, got = quarters_of((2, 3), gg)
    gg, send = backward(1, sel, c, kept, gg)
    c = hop(send, 1)
    got = [after(a, gg) for a in got]
    ring[1] = after(ring[1], gg)
    nl_peer = after(nl_peer, gg)
    ring.append(onward(ring[1]))
    high = choose((2, 3), sel, parts, got)
    high_peer = swapped(high)
    c, high = together((c, high))
    gg, _ = backward(0, sel, c, kept, gg)
    ring.append(onward(after(ring[2], gg)))
    high_peer, gg = together((high_peer, gg))
    parts, got = quarters_of((0, 1), gg)
    gg_peer = swapped(gg[1, :2])
    got, gg_peer = together((got, gg_peer))
    low = choose((0, 1), sel, parts, got)
    low_peer = swapped(low)
    pieces = (low, low_peer, high, high_peer)
    tile = gradient(sel, firsts, firsts_peer, ring, pieces)
    ct = gg[:, 2, :, :width]
    terms = adapter_terms(nl, gg, nl_peer, gg_peer)
    terms = over_cores(at(terms, cores[0]), at(terms, cores[1]))
    terms = (at(terms, ys[0]).astype(F32) + over_y(at(terms, ys[1]))).astype(BF16)
    terms = over_z(terms, zs)
    tile = over_z(over_cores(*tile), zs).astype(BF16)
    tile = at(tile, ys[0]).astype(F32) + over_y(at(tile, ys[1]))
    tile = tile.astype(BF16).reshape(4, 16, -1)
    placed = jnp.stack(
        [at(tile, xs[0])] + [lax.ppermute(at(tile, xs[d]), "pipe", turns[d]) for d in range(1, 4)]
    )
    placed = jnp.stack([at(placed, source) for source in sources], axis=1)
    each = width // (n_pipe * n_dp)
    shared = placed[:each].reshape(each, 4, 2, width // 4).transpose(0, 2, 1, 3)
    shared = shared.reshape(each, 2, width).astype(F32)

    ours, theirs = ct[0], swapped(ct[1])
    result = jnp.where(
        h == 0, jnp.concatenate([ours, theirs]), jnp.concatenate([theirs, ours])
    )
    both = terms.reshape(4, 16, 7, rank).transpose(0, 2, 1, 3).reshape(4, 112, rank)
    return result[None], shared, both[None, :2], both[None, 2:]


def solution(mesh):
    return jax.shard_map(
        shards,
        mesh=mesh,
        in_specs=(
            P("pipe", "dp", None),
            P("dp", None, None),
            P("pipe", None, None, None),
            P("pipe", None, None, None),
            P("pipe", None),
            P("dp", None),
        ),
        out_specs=(
            P("pipe", "dp", None),
            P(("pipe", "dp"), None, None),
            P("pipe", None, "dp", None),
            P("pipe", None, "dp", None),
        ),
        check_vma=False,
    )
```

```python
import functools

import jax
import jax.numpy as jnp
from jax import lax
from jax.experimental import pallas as pl
from jax.experimental.pallas import tpu as pltpu
from jax.sharding import PartitionSpec as P

EPS = 1e-06
TILE = 256
F32 = jnp.float32
BF16 = jnp.bfloat16
NT = (((1,), (1,)), ((), ()))
TN = (((0,), (0,)), ((), ()))
HB = pl.BlockSpec(memory_space=pltpu.HBM)
VM = pl.BlockSpec(memory_space=pltpu.VMEM)
SM = pl.BlockSpec(memory_space=pltpu.SMEM)


def dot(a, b, dims=(((1,), (0,)), ((), ()))):
    return lax.dot_general(a, b, dims, preferred_element_type=F32)


def cost(flops, bytes_accessed):
    return pl.CostEstimate(flops=int(flops), bytes_accessed=int(bytes_accessed), transcendentals=0)


def pinned(array):
    return pltpu.with_memory_space_constraint(array, pltpu.VMEM)


def in_hbm(array):
    return pltpu.with_memory_space_constraint(array, pltpu.HBM)


PIECES = ((0, 0, None), (0, 3, None), (0, 1, None), (1, 0, 0), (1, 0, 1), (0, 2, 0), (0, 2, 1)) + (
    (1, 3, None), (1, 1, None), (1, 2, 0), (1, 2, 1)
)


def row_blocks(src, tile, dst, h, lanes):
    width = src.shape[1]
    for t in range(width // TILE):
        tile[pl.ds(t * TILE, TILE), :] = src[:, t * TILE : (t + 1) * TILE].astype(F32).T
    tile[pl.ds(width, 8), :] = jnp.zeros((8, tile.shape[1]), F32)
    for p in range(8):
        x, half = p // 2, p % 2
        slot = jnp.bitwise_xor(h, half)
        for r in range(16):
            core, z, y = r % 2, (r // 2) % 4, r // 8
            at_row = (((core * 4 + z) * 2 + y) * 4 + x) * 16
            dst[slot, pl.ds(at_row, 16), lanes] = tile[pl.ds((p * 16 + r) * 14, 16), :].astype(BF16)


def first_kernel(sel, x, out, tile):
    rows = jnp.concatenate([x[0], x[1]], axis=0).astype(F32)
    sc = lax.rsqrt(jnp.mean(rows * rows, axis=-1, keepdims=True) + EPS)
    row_blocks((rows * sc).astype(BF16), tile, out, sel[2, 0], pl.ds(0, 128))


def first_rows(sel, x):
    width = x.shape[-1]
    return pl.pallas_call(
        first_kernel,
        out_shape=jax.ShapeDtypeStruct((2, 1024, 128), BF16),
        in_specs=[SM, VM],
        out_specs=VM,
        scratch_shapes=[pltpu.VMEM((width + 8, 128), F32)],
        compiler_params=pltpu.CompilerParams(vmem_limit_bytes=16 << 20),
        cost_estimate=cost(1e+09, 1e+06),
        name="first_rows",
    )(sel, x)


def forward_kernel(sel, x, *refs):
    a_own, u_own, near, far = refs[:4]
    pieces = refs[4 : 4 + 2 * len(PIECES)]
    nl, slope, scale, wt, auv, gg, out, wv, xs, tile, sems = refs[4 + 2 * len(PIECES) :]
    av, uv = auv.at[0], auv.at[1]
    width = x.shape[-1]
    per = pieces[0].shape[-2]
    h, r = sel[2, 0], sel[2, 1]
    core, z, y = r % 2, (r // 2) % 4, r // 8
    small = []
    for i, (src, dst) in enumerate(
        ((a_own, av.at[0]), (u_own, uv.at[0]), (near, auv.at[core, 1]), (far, auv.at[1 - core, 1]))
    ):
        small.append(pltpu.make_async_copy(src, dst, sems.at[32 + i]))
    for copy in small:
        copy.start()
    for block in range(2):
        for i, ref in enumerate(pieces):
            dy, dz, held = PIECES[i // 2]
            if held is not None and held != block:
                continue
            place = jnp.bitwise_xor(y, dy) * 8 + (z + dz) % 4 * 2 + jnp.bitwise_xor(core, i % 2)
            dst = wv.at[block, pl.ds(pl.multiple_of(place * per, 16), per), :]
            src = ref.at[block] if held is None else ref
            pltpu.make_async_copy(src, dst, sems.at[block * 16 + place]).start()
    big = []
    for block in range(2):
        for place in range(16):
            dst = wv.at[block, pl.ds(place * per, per), :]
            big.append(pltpu.make_async_copy(dst, dst, sems.at[block * 16 + place]))
    gg[...] = jnp.zeros_like(gg)
    for o in range(2):
        xs[o] = x[o]
    here = 0
    for block in range(2):
        for t in range(width // TILE):
            while here < 16 * block + min(16, -(-(t + 1) * TILE // per)):
                big[here].wait()
                here += 1
            wt[block, :, pl.ds(t * TILE, TILE)] = wv[block, pl.ds(t * TILE, TILE), :].T
    for copy in small:
        copy.wait()
    for k in range(2):
        rows = jnp.concatenate([xs[0], xs[1]], axis=0).astype(F32)
        sc = lax.rsqrt(jnp.mean(rows * rows, axis=-1, keepdims=True) + EPS)
        nm = (rows * sc).astype(BF16)
        if k == 1:
            row_blocks(nm, tile, out, h, pl.ds(0, 128))
        for o in range(2):
            part = slice(o * 64, (o + 1) * 64)
            scale[o, k] = jnp.broadcast_to(sc[part], scale.shape[2:])
            mine = nm[part]
            nl[o, k, :, pl.ds(0, width)] = mine
            low = dot(mine, av[o, k]).astype(BF16)
            nl[o, k, :, pl.ds(width, 128)] = low
            block = sel[o, k]
            for t in range(width // TILE):
                cols = pl.ds(t * TILE, TILE)
                pre = dot(mine, wv[block, :, cols]) + dot(low, uv[o, k, cols, :], NT)
                sigma = 1.0 / (1.0 + jnp.exp(-pre))
                slope[o, k, :, cols] = sigma * (1.0 + pre * (1.0 - sigma))
                if k == 0:
                    xs[o, :, cols] = (xs[o, :, cols].astype(F32) + pre * sigma).astype(BF16)


def forward(sel, x, weights):
    rows, width = x.shape[1:]
    rank = weights[0].shape[-1]
    return pl.pallas_call(
        forward_kernel,
        out_shape=(
            pltpu.VMEM((2, 2, rows, width + rank), BF16),
            pltpu.VMEM((2, 2, rows, width), F32),
            pltpu.VMEM((2, 2, rows, 128), F32),
            pltpu.VMEM((2, width, width), BF16),
            pltpu.VMEM((2, 2, 2, width, rank), BF16),
            pltpu.VMEM((2, 3, rows, width + rank), BF16),
            jax.ShapeDtypeStruct((2, 1024, 128), BF16),
        ),
        in_specs=[SM, VM] + [HB] * len(weights),
        out_specs=(VM,) * 7,
        scratch_shapes=[
            pltpu.VMEM((2, width, width), BF16),
            pltpu.VMEM((2, rows, width), BF16),
            pltpu.VMEM((width + 8, 128), F32),
            pltpu.SemaphoreType.DMA((36,)),
        ],
        compiler_params=pltpu.CompilerParams(vmem_limit_bytes=22 << 20),
        cost_estimate=cost(1.5e+10, 2e+07),
        name="forward",
    )(sel, x, *[in_hbm(w) for w in weights])


def backward_kernel(at_place, sel, c, nl, slope, scale, wt, auv, old_gg, gg, send, gn):
    width = c.shape[-1]
    av, uv = auv.at[0], auv.at[1]

    @pl.when(sel[3, 0] == at_place)
    def _():
        h = sel[2, 0]
        cur = c[...]
        for j in (1, 0):
            o = jnp.bitwise_xor(h, j)
            for k in (1, 0):
                c32 = cur.astype(F32)
                g = (c32 * slope[o, k]).astype(BF16)
                gg[o, k, :, pl.ds(0, width)] = g
                low = dot(g, uv[o, k]).astype(BF16)
                gg[o, k, :, pl.ds(width, 128)] = low
                block = sel[o, k]
                total = jnp.zeros((g.shape[0], 128), F32)
                for t in range(width // TILE):
                    cols = pl.ds(t * TILE, TILE)
                    part = dot(g, wt[block, :, cols]) + dot(low, av[o, k, cols, :], NT)
                    gn[:, cols] = part
                    product = part * nl[o, k, :, cols].astype(F32)
                    total = total + (product[:, :128] + product[:, 128:])
                mean = jnp.sum(total, axis=-1, keepdims=True) / width
                z = nl[o, k, :, pl.ds(0, width)].astype(F32)
                sc = scale[o, k, :, 0:1]
                cur = (c32 + sc * (gn[...] - z * mean)).astype(BF16)
            gg[o, 2, :, pl.ds(0, width)] = cur
        send[...] = cur


def backward(at_place, sel, c, kept, gg):
    rows, width = c.shape
    kept = [pinned(a) for a in kept]
    return pl.pallas_call(
        functools.partial(backward_kernel, at_place),
        out_shape=(jax.ShapeDtypeStruct(gg.shape, BF16), jax.ShapeDtypeStruct((rows, width), BF16)),
        in_specs=[SM, VM] + [VM] * 6,
        out_specs=(VM, VM),
        scratch_shapes=[pltpu.VMEM((rows, width), F32)],
        input_output_aliases={7: 0},
        compiler_params=pltpu.CompilerParams(vmem_limit_bytes=6 << 20),
        cost_estimate=cost(9e+09, 2e+07),
        name="backward",
    )(sel, c, *kept, pinned(gg))


def transpose_kernel(places, sel, gp, out):
    quarter = (gp.shape[-1] - 128) // 4

    @pl.when((sel[3, 0] >= places[0]) & (sel[3, 0] <= places[-1]))
    def _():
        for k in range(2):
            lanes = pl.ds(k * 128, 128)
            both = jnp.concatenate([gp[0, k], gp[1, k]], axis=0)[:, : 4 * quarter]
            for q in range(4):
                d = (q + 4 - sel[3, 0]) % 4
                for t in range(0, quarter, 64):
                    out[d, pl.ds(t, 64), lanes] = both[:, q * quarter + t : q * quarter + t + 64].T
            side = lax.broadcasted_iota(jnp.int32, (16, 128), 1) // 64
            mark = jnp.where(side == 0, sel[0, k], sel[1, k])
            for q in range(4):
                out[q, pl.ds(quarter, 16), lanes] = mark.astype(F32).astype(BF16)


def transposed(places, sel, gp):
    quarter = (gp.shape[-1] - 128) // 4
    return pl.pallas_call(
        functools.partial(transpose_kernel, places),
        out_shape=jax.ShapeDtypeStruct((4, quarter + 16, 256), BF16),
        in_specs=[SM, VM],
        out_specs=VM,
        compiler_params=pltpu.CompilerParams(vmem_limit_bytes=6 << 20),
        cost_estimate=cost(1.8e+09, 4e+06),
        name="transposed",
    )(sel, pinned(gp))


def choose_kernel(places, sel, quarters, one, two, three, out):
    for i, place in enumerate(places):
        away = (sel[3, 0] + 4 - place) % 4

        @pl.when(away == 0)
        def _(i=i):
            out[i] = quarters[0]

        for d, got in ((1, one), (2, two), (3, three)):

            @pl.when(away == d)
            def _(i=i, got=got):
                out[i] = got[...]


def choose(places, sel, quarters, got):
    return pl.pallas_call(
        functools.partial(choose_kernel, places),
        out_shape=jax.ShapeDtypeStruct((len(places),) + quarters.shape[1:], BF16),
        in_specs=[SM] + [VM] * 4,
        out_specs=VM,
        compiler_params=pltpu.CompilerParams(vmem_limit_bytes=8 << 20),
        cost_estimate=cost(1e+09, 1e+06),
        name="choose",
    )(sel, quarters, *got)


def gradient_kernel(*refs):
    sel, low, low_peer, high, high_peer, firsts, firsts_peer = refs[:7]
    seconds = refs[7:11]
    out, left, right, sems = refs[11:]
    pieces = [ref.at[i] for mine, peer in ((low, low_peer), (high, high_peer)) for i in range(2) for ref in (mine, peer)]
    copies = []
    for d in range(4):
        source = (sel[3, 0] + 4 - d) % 4
        for side in range(2):
            first = firsts_peer.at[source] if side else firsts.at[source, 0]
            for k, rows in enumerate((first, seconds[d].at[side])):
                lanes = pl.ds(pl.multiple_of(source * 512, 128) + (side * 2 + k) * 128, 128)
                copies.append(pltpu.make_async_copy(rows, left.at[:, lanes], sems.at[len(copies)]))
    for copy in copies:
        copy.start()
    quarter = low.shape[1] - 16
    for i, piece in enumerate(pieces):
        lanes = pl.ds(i * 256, 256)
        whole = piece[pl.ds(0, quarter), :].astype(F32)
        second = whole * piece[pl.ds(quarter, 16), :][0:1].astype(F32)
        right[pl.ds(0, quarter), lanes] = (whole - second).astype(BF16)
        right[pl.ds(quarter, quarter), lanes] = second.astype(BF16)
    for copy in copies:
        copy.wait()
    for m in range(left.shape[0] // TILE):
        part = dot(left[pl.ds(m * TILE, TILE), :], right[...], NT).astype(BF16)
        for i in range(4):
            at_chunk = m * 4 + i
            out[at_chunk // 8, at_chunk // 2 % 4, at_chunk % 2, pl.ds(0, 64), :] = part[i * 64 : i * 64 + 64]


def gradient(sel, firsts, firsts_peer, seconds, pieces):
    rows = firsts.shape[2]
    cols = 2 * (pieces[0].shape[1] - 16)
    return pl.pallas_call(
        gradient_kernel,
        out_shape=jax.ShapeDtypeStruct((2, 4, 2, 64, cols), BF16),
        in_specs=[SM] + [VM] * 4 + [HB] * 6,
        out_specs=VM,
        scratch_shapes=[
            pltpu.VMEM((rows, 2048), BF16),
            pltpu.VMEM((cols, 2048), BF16),
            pltpu.SemaphoreType.DMA((16,)),
        ],
        compiler_params=pltpu.CompilerParams(vmem_limit_bytes=20 << 20),
        cost_estimate=cost(9e+09, 2e+07),
        name="gradient",
    )(sel, *pieces, *[in_hbm(a) for a in (firsts, firsts_peer, *seconds)])


def adapter_kernel(nl, gg, nl_peer, gg_peer, out):
    width = nl.shape[-1] - 128
    for k in range(2):
        n = jnp.concatenate([nl[0, k], nl_peer[k]], axis=0)
        g = jnp.concatenate([gg[0, k], gg_peer[k]], axis=0)
        for i, (lhs, rhs) in enumerate(((n, g[:, width:]), (g, n[:, width:]))):
            term = dot(lhs[:, :width], rhs, TN).astype(BF16)
            rows = pl.ds((2 * i + k) * 16, 16)
            for r in range(16):
                for t in range(7):
                    out[r % 2, r // 8, (r // 2) % 4, rows, pl.ds(t * 128, 128)] = (
                        term[r * 112 + t * 16 : r * 112 + t * 16 + 16]
                    )


def adapter_terms(nl, gg, nl_peer, gg_peer):
    return pl.pallas_call(
        adapter_kernel,
        out_shape=jax.ShapeDtypeStruct((2, 2, 4, 64, 896), BF16),
        in_specs=[VM] * 4,
        out_specs=VM,
        compiler_params=pltpu.CompilerParams(vmem_limit_bytes=16 << 20),
        cost_estimate=cost(2e9, 4e6),
        name="adapter_terms",
    )(pinned(nl), pinned(gg), nl_peer, gg_peer)


def at(array, index):
    return lax.dynamic_index_in_dim(array, index, 0, keepdims=False)


def move(array, dy=0, dz=0, flip=0):
    pairs = []
    for x in range(4):
        for y in range(4):
            for z in range(4):
                for core in range(2):
                    to_y, to_z = (y + dy) % 4, (z + dz) % 4
                    src = (x * 2 + y // 2) * 16 + y % 2 * 8 + z * 2 + core
                    dst = (x * 2 + to_y // 2) * 16 + to_y % 2 * 8 + to_z * 2 + (core ^ flip)
                    pairs.append((src, dst))
    return lax.ppermute(array, ("pipe", "dp"), pairs)


def over_y(part):
    return lax.ppermute(part, "dp", [(i, i ^ 8) for i in range(16)]).astype(F32)


def over_z(part, zs):
    total = at(part, zs[0]).astype(F32)
    for d in range(1, 4):
        pairs = [(i, i // 8 * 8 + (i + 2 * d) % 8) for i in range(16)]
        total = total + lax.ppermute(at(part, zs[d]), "dp", pairs).astype(F32)
    return total


def over_cores(part, cores):
    got = lax.ppermute(at(part, cores[1]), "dp", [(i, i ^ 1) for i in range(16)])
    return (at(part, cores[0]).astype(F32) + got.astype(F32)).astype(BF16)


def shards(stored, common, down, up, selection, final_c):
    n_pipe, n_dp = lax.axis_size("pipe"), lax.axis_size("dp")
    together = lax.optimization_barrier
    p = lax.axis_index("pipe")
    r = lax.axis_index("dp")
    x_at, h, core = p // 2, p % 2, r % 2
    swap = [(i, i ^ 1) for i in range(n_pipe)]
    turns = [[(i, (i + 2 * d) % n_pipe) for i in range(n_pipe)] for d in range(4)]
    own = stored[0]
    rows, width = own.shape
    half = rows // 2
    a_own, u_own = down[0], up[0]
    rank = a_own.shape[-1]

    def swapped(array):
        return lax.ppermute(array, "pipe", swap)

    def onward(array):
        return lax.ppermute(array, "pipe", turns[1])

    def flip(array):
        return move(array, flip=1)

    def after(value, other):
        return together((value, other))[0]

    mixed = common.transpose(1, 0, 2)
    up_z, down_z = move(mixed, dz=1), move(mixed, dz=-1)
    y_a, y_b = move(mixed[0], dy=1), move(mixed[1], dy=-1)
    x_mine = lax.dynamic_slice_in_dim(own, h * half, half, 0)
    x_other = lax.dynamic_slice_in_dim(own, (1 - h) * half, half, 0)
    c = lax.dynamic_slice_in_dim(final_c, h * half, half, 0)
    marks = jnp.broadcast_to(jnp.pad(selection[0], (0, width - 2)).astype(BF16), (16, width))
    x_peer = swapped(jnp.concatenate([x_other, marks]))
    sel_peer = x_peer[half:, :2][:1].astype(F32).astype(jnp.int32)
    sel = jnp.concatenate([selection, sel_peer, jnp.stack([h, r, x_at, x_at]).astype(jnp.int32).reshape(2, 2)])
    entered = jnp.stack([x_mine, x_peer[:half]])
    near = move(jnp.where(core == 0, a_own, u_own), dy=2)
    first = first_rows(sel, entered)
    firsts = lax.all_gather(first, "pipe", axis_index_groups=[[0, 2, 4, 6], [1, 3, 5, 7]])
    up_z, down_z, y_a, y_b, sel, c, entered = together((up_z, down_z, y_a, y_b, sel, c, entered))
    yz_a, yz_b = move(up_z, dy=1), move(down_z, dy=-1)
    z_a, z_b = move(up_z[0], dz=1), move(down_z[1], dz=-1)
    flips = [flip(after(a, (z_a, z_b))) for a in (mixed, up_z, down_z)]
    flips += [flip(after(a, (yz_a, yz_b))) for a in (y_a, y_b)]
    yz_a, yz_b, z_a, z_b, flips, firsts = together((yz_a, yz_b, z_a, z_b, flips, firsts))
    firsts_peer = swapped(firsts[:, 1])
    yf_a, yf_b = move(yz_a[0], dz=1), move(yz_b[1], dz=-1)
    late = [flip(a) for a in (z_a, z_b, yz_a, yz_b, near)]
    yf_a, yf_b, late = together((yf_a, yf_b, late))
    flips += [*late[:4], flip(yf_a), flip(yf_b), late[4]]
    direct = (mixed, up_z, down_z, y_a, y_b, z_a, z_b, yz_a, yz_b, yf_a, yf_b)
    pieces = [q for pair in zip(direct, flips) for q in pair]
    z, y = (r // 2) % 4, r // 8
    places = ([core, 1 - core], [(z + d) % 4 for d in range(4)], [y, 1 - y])
    places += ([(x_at + d) % 4 for d in range(4)], [(x_at - s) % 4 for s in range(4)])
    places = [[index.astype(jnp.uint32) for index in group] for group in places]
    entered, firsts, places = together((entered, firsts, places))
    cores, zs, ys, xs, sources = places
    *kept, gg, second = forward(sel, entered, (a_own, u_own, near, flips[-1], *pieces))
    nl = kept[0]

    def hop(send, place):
        return lax.ppermute(send, "pipe", [(2 * place + i, 2 * place - 2 + i) for i in range(2)])

    def quarters_of(places, gg):
        parts = transposed(places, sel, gg)
        got = []
        for d in range(1, 4):
            pairs = [(2 * place + i, 2 * ((place + d) % 4) + i) for place in places for i in range(2)]
            got.append(lax.ppermute(parts[d], "pipe", pairs))
        return parts, got

    second_peer = swapped(second[1])
    gg, send = backward(3, sel, c, kept, gg)
    c = hop(send, 3)
    second_peer, gg, firsts_peer = together((second_peer, gg, firsts_peer))
    ring = [jnp.stack([second[0], second_peer])]
    ring.append(onward(ring[0]))
    gg, send = backward(2, sel, c, kept, gg)
    c = hop(send, 2)
    nl_peer = swapped(after(nl, gg)[1])
    gg, c = together((gg, c))
    parts, got = quarters_of((2, 3), gg)
    gg, send = backward(1, sel, c, kept, gg)
    c = hop(send, 1)
    got = [after(a, gg) for a in got]
    ring[1] = after(ring[1], gg)
    nl_peer = after(nl_peer, gg)
    ring.append(onward(ring[1]))
    high = choose((2, 3), sel, parts, got)
    high_peer = swapped(high)
    c, high = together((c, high))
    gg, _ = backward(0, sel, c, kept, gg)
    ring.append(onward(after(ring[2], gg)))
    high_peer, gg = together((high_peer, gg))
    parts, got = quarters_of((0, 1), gg)
    low = choose((0, 1), sel, parts, got)
    low_peer = swapped(low)
    gg_peer = swapped(gg[1, :2])
    pieces = (low, low_peer, high, high_peer)
    tile = gradient(sel, firsts, firsts_peer, ring, pieces)
    terms = over_cores(adapter_terms(nl, gg, nl_peer, gg_peer), cores)
    terms = (at(terms, ys[0]).astype(F32) + over_y(at(terms, ys[1]))).astype(BF16)
    terms = over_z(terms, zs)
    tile = over_z(over_cores(tile, cores), zs).astype(BF16)
    tile = at(tile, ys[0]).astype(F32) + over_y(at(tile, ys[1]))
    tile = tile.astype(BF16).reshape(4, 16, -1)
    ct = gg[:, 2, :, :width]
    placed = jnp.stack(
        [at(tile, xs[0])] + [lax.ppermute(at(tile, xs[d]), "pipe", turns[d]) for d in range(1, 4)]
    )
    placed = jnp.stack([at(placed, source) for source in sources], axis=1)
    each = width // (n_pipe * n_dp)
    shared = placed[:each].reshape(each, 4, 2, width // 4).transpose(0, 2, 1, 3)
    shared = shared.reshape(each, 2, width).astype(F32)

    ours, theirs = ct[0], swapped(ct[1])
    result = jnp.where(
        h == 0, jnp.concatenate([ours, theirs]), jnp.concatenate([theirs, ours])
    )
    both = terms.reshape(4, 16, 7, rank).transpose(0, 2, 1, 3).reshape(4, 112, rank)
    return result[None], shared, both[None, :2], both[None, 2:]


def solution(mesh):
    return jax.shard_map(
        shards,
        mesh=mesh,
        in_specs=(
            P("pipe", "dp", None),
            P("dp", None, None),
            P("pipe", None, None, None),
            P("pipe", None, None, None),
            P("pipe", None),
            P("dp", None),
        ),
        out_specs=(
            P("pipe", "dp", None),
            P(("pipe", "dp"), None, None),
            P("pipe", None, "dp", None),
            P("pipe", None, "dp", None),
        ),
        check_vma=False,
    )
```
